256 devices in a mesh: dp: 32 (over z_hi, y, core), shard: 8 (over x, z_lo).
Axes of the slice: x: 4, y: 4, z: 8 (z_hi: 4, z_lo: 2; z = z_hi * 2 + z_lo), core: 2. Of those that a mesh axis runs over, the one named last changes fastest.
Arguments:
- packed: bfloat16 [8192, 4096], P('dp'), may hold values from -1.5 to 1.5
- counts: int32 [32, 8], P('dp'), may hold values from 8 to 32, as said below
- dest_plan: int32 [32, 8], P('dp'), may hold values from 0 to 7, as said below
- source_plan: int32 [32, 8], P('dp'), may hold values from 0 to 7, as said below
- slot_counts: int32 [32, 8], P('dp'), may hold values from 8 to 32, as said below
- cotangent: bfloat16 [256, 32, 4096], P('dp'), may hold values from -6 to 6
- qkv_weight: bfloat16 [4096, 24, 384], P('dp', 'shard'), may hold values from -0.09375 to 0.09375
- out_weight: bfloat16 [4096, 24, 128], P('dp', 'shard'), may hold values from -0.5 to 0.5
- ln_gain: float32 [4096], replicated, may hold values from 0.4 to 2.5
- qk_gains: float32 [2, 128], replicated, may hold values from 0.5 to 5
Outputs:
- block_out: bfloat16 [256, 32, 4096], P('dp', None, 'shard')
- grad_qkv: float32 [4096, 24, 384], P('dp', 'shard')
- grad_out: float32 [4096, 24, 128], P('dp', 'shard')
- grad_ln_gain: float32 [4096], replicated
- grad_qk_gains: float32 [2, 128], replicated
The draws below stay inside these ranges and needn't reach their ends.
Inputs may be any that keep to these rules, and one draw needn't show every extreme that they name: `counts`: at every dp index some image has exactly 32 patches. Each row is an ordering of 0 to 7; image i of dp index a goes to dp index (a + gap(dest_plan)) mod 32. Each row is an ordering of 0 to 7; block k of dp index a holds the image that dp index (a - gap(source_plan)) mod 32 sends to a. `slot_counts`: the patch count of the image that fills each block.
All inputs are finite; a program needn't handle non-finite values.
Results may differ from the reference program's by a relative error of at most 0.025.
The reference program's roundings to bfloat16 on the way count: a program that leaves them out, or rounds other values in their place, can miss the bound.
Values may be sent and summed in bfloat16 or wider, within the bound.
No kernel may reach another device: no remote copies, remote signals or barrier semaphores. Data moves between devices by JAX's collectives and lax.ppermute only.
A program may use at most 128 MiB of HBM per device.

```python
import math
import jax
import jax.numpy as jnp
from jax import lax

D = 4096
HEAD = 128
HEADS_DEV = 3
BLOCK = 32
IMAGES = 8
HEADS = 24
TOK_DEV = 256
HALF_GAP = 12
DATA_GROUP = 32
N_DP = 32
N_SHARD = 8


def image_tables(key):
    count_key = jax.random.fold_in(key, 101)
    base_counts = jax.random.randint(count_key, (DATA_GROUP, IMAGES), max(1, BLOCK // 4), BLOCK + 1)
    largest = jax.random.randint(jax.random.fold_in(key, 102), (DATA_GROUP, 1), 0, IMAGES)
    image_ids = jnp.arange(IMAGES, dtype=jnp.int32)
    counts = jnp.where(image_ids[None, :] == largest, BLOCK, base_counts).astype(jnp.int32)

    def ordering(row_key):
        return jax.random.permutation(row_key, IMAGES).astype(jnp.int32)
    dest_plan = jax.vmap(ordering)(jax.random.split(jax.random.fold_in(key, 103), DATA_GROUP)).astype(jnp.int32)
    source_plan = jax.vmap(ordering)(jax.random.split(jax.random.fold_in(key, 104), DATA_GROUP)).astype(jnp.int32)
    group_ids = jnp.arange(DATA_GROUP, dtype=jnp.int32)
    gaps = source_plan + jnp.where(source_plan >= IMAGES // 2, HALF_GAP, 0)
    source_groups = ((group_ids[:, None] - gaps) % DATA_GROUP).astype(jnp.int32)
    matches = dest_plan[source_groups] == source_plan[:, :, None]
    slot_counts = jnp.sum(jnp.where(matches, counts[source_groups], 0), axis=-1).astype(jnp.int32)
    return (counts, dest_plan, source_plan, slot_counts)


def draw_counts(key, part):
    return image_tables(key)[0]


def draw_dest_plan(key, part):
    return image_tables(key)[1]


def draw_source_plan(key, part):
    return image_tables(key)[2]


def draw_slot_counts(key, part):
    return image_tables(key)[3]


def draw_packed(key, part):
    key = jax.random.fold_in(key, 21)
    total_rows = DATA_GROUP * TOK_DEV
    values = 0.25 * jax.random.normal(key, (total_rows, D), jnp.float32)
    return jnp.clip(values, -1.5, 1.5).astype(jnp.bfloat16)


def draw_qkv_weight(key, part):
    key = jax.random.fold_in(key, 22)
    query_key, key_key, value_key = jax.random.split(key, 3)
    factor = D ** (-0.5)
    query_cols = jnp.clip(jax.random.normal(query_key, (D, HEADS, HEAD), jnp.float32), -6.0, 6.0) * factor
    key_cols = jnp.clip(jax.random.normal(key_key, (D, HEADS, HEAD), jnp.float32), -6.0, 6.0) * factor
    value_cols = jnp.clip(jax.random.normal(value_key, (D, HEADS, HEAD), jnp.float32), -6.0, 6.0) * factor
    return jnp.concatenate([query_cols, key_cols, value_cols], axis=2).astype(jnp.bfloat16)


def draw_qk_gains(key, part):
    key = jax.random.fold_in(key, 11)
    return jax.random.uniform(key, (2, HEAD), jnp.float32, 0.5, 2.0)


def levels(key, shape, shards, low, high):
    def one(axis_at, parts):
        heights = jax.random.uniform(jax.random.fold_in(jax.random.fold_in(key, 6), axis_at), (parts,), jnp.float32, low / len(shards), high / len(shards))
        return jnp.repeat(jnp.exp(heights), shape[axis_at] // parts).reshape((-1,) + (1,) * (len(shape) - axis_at - 1))

    level = one(*shards[0])
    for cut in shards[1:]:
        level = level * one(*cut)
    return level


def noise(rng, extent, scale, most, cuts=(), held_as=jnp.bfloat16):
    values = jax.random.normal(rng, extent, jnp.float32) * scale
    if len(cuts) > 0:
        values = levels(rng, extent, cuts, -0.22, 0.18) * values
    return jnp.clip(values, min=-most, max=most).astype(held_as)


def setup_inputs(seed: int = 0) -> dict:
    key_list = jax.random.split(jax.random.key(seed), 11)
    return {
        "packed": draw_packed(jax.random.fold_in(key_list[10], 71), 0),
        "counts": draw_counts(jax.random.fold_in(key_list[10], 71), 0),
        "dest_plan": draw_dest_plan(jax.random.fold_in(key_list[10], 71), 0),
        "source_plan": draw_source_plan(jax.random.fold_in(key_list[10], 71), 0),
        "slot_counts": draw_slot_counts(jax.random.fold_in(key_list[10], 71), 0),
        "cotangent": noise(key_list[5], (DATA_GROUP * IMAGES, BLOCK, D), 1.0, 6.0, ((0, 32),)),
        "qkv_weight": draw_qkv_weight(jax.random.fold_in(key_list[10], 71), 0),
        "out_weight": noise(key_list[7], (D, HEADS, HEAD), HEAD ** -0.5, 0.5, ((0, 32), (1, 8))),
        "ln_gain": jnp.clip(jnp.exp(jax.random.uniform(key_list[8], (D,), jnp.float32, math.log(0.4), math.log(2.5))), 0.4, 2.5),
        "qk_gains": draw_qk_gains(jax.random.fold_in(key_list[10], 71), 0),
    }


EPSILON = 1e-06

def layer_norm(values, scales):
    centred = values - lax.optimization_barrier(jnp.mean(values, axis=-1, keepdims=True))
    spread = lax.optimization_barrier(jnp.mean(centred * centred, axis=-1, keepdims=True))
    return centred * lax.rsqrt(spread + EPSILON) * scales

def head_attend(blocks, qkv_group, ln_gain, qk_gains, valid_rows):
    slots, length, width = blocks.shape
    heads = qkv_group.shape[1]
    head_size = qkv_group.shape[2] // 3
    normed = layer_norm(blocks.astype(jnp.float32), ln_gain).astype(jnp.bfloat16)
    projected = jnp.dot(normed.reshape(slots * length, width), qkv_group.reshape(width, heads * 3 * head_size), preferred_element_type=jnp.float32)
    projected = projected.reshape(slots, length, heads, 3 * head_size)
    queries = layer_norm(projected[..., :head_size], qk_gains[0]).astype(jnp.bfloat16)
    key_rows = layer_norm(projected[..., head_size:2 * head_size], qk_gains[1]).astype(jnp.bfloat16)
    value_rows = projected[..., 2 * head_size:].astype(jnp.bfloat16)
    scores = jnp.einsum('sqnh,sknh->snqk', queries.astype(jnp.float32), key_rows.astype(jnp.float32)) / math.sqrt(head_size)
    scores = jnp.where(valid_rows[:, None, None, :], scores, -1e+30)
    row_max = lax.optimization_barrier(jnp.max(scores, axis=-1, keepdims=True))
    expo = jnp.exp(scores - row_max)
    attend = (expo / lax.optimization_barrier(jnp.sum(expo, axis=-1, keepdims=True))).astype(jnp.bfloat16)
    attended = jnp.einsum('snqk,sknh->sqnh', attend.astype(jnp.float32), value_rows.astype(jnp.float32)).astype(jnp.bfloat16)
    return attended.reshape(slots, length, heads * head_size)

def head_project(attended, out_group, valid_rows):
    slots, length, inner = attended.shape
    width = out_group.shape[0]
    branch = jnp.dot(attended.reshape(slots * length, inner), out_group.reshape(width, inner).T, preferred_element_type=jnp.float32)
    return jnp.where(valid_rows[..., None], branch.reshape(slots, length, width), 0.0)

def reference(packed, counts, dest_plan, source_plan, slot_counts, cotangent, qkv_weight, out_weight, ln_gain, qk_gains):
    packed_dev = packed.reshape(N_DP, TOK_DEV, D)
    counts_dev = counts.astype(jnp.int32)
    offsets_dev = (jnp.cumsum(counts_dev, axis=-1) - counts_dev).astype(jnp.int32)
    dest_dev = dest_plan.astype(jnp.int32)
    source_dev = source_plan.astype(jnp.int32)
    slot_dev = slot_counts.astype(jnp.int32)
    cot_dev = cotangent.reshape(N_DP, IMAGES, BLOCK, D)
    positions = jnp.arange(BLOCK, dtype=jnp.int32)
    group_ids = jnp.arange(N_SHARD, dtype=jnp.int32)

    def assemble(group_index):
        offset_ids = source_dev[group_index]
        gaps = (offset_ids + jnp.where(offset_ids >= IMAGES // 2, HALF_GAP, 0)).astype(jnp.int32)
        sources = ((group_index - gaps) % N_DP).astype(jnp.int32)
        chosen = dest_dev[sources] == offset_ids[:, None]
        starts = lax.optimization_barrier(jnp.sum(jnp.where(chosen, offsets_dev[sources], 0), axis=-1)).astype(jnp.int32)
        lengths = lax.optimization_barrier(jnp.sum(jnp.where(chosen, counts_dev[sources], 0), axis=-1)).astype(jnp.int32)
        row_index = jnp.clip(starts[:, None] + positions[None, :], 0, TOK_DEV - 1).astype(jnp.int32)
        gathered = packed_dev[sources[:, None], row_index]
        keep_rows = (positions[None, :] < lengths[:, None])[..., None]
        return jnp.where(keep_rows, gathered, jnp.zeros((), packed.dtype))

    def group_step(totals, group_index):
        blocks = assemble(group_index)
        valid_rows = positions[None, :] < slot_dev[group_index][:, None]
        cot_here = cot_dev[group_index].astype(jnp.float32)

        def one_group(head_group):
            qkv_group = lax.dynamic_slice_in_dim(qkv_weight, head_group * HEADS_DEV, HEADS_DEV, 1)
            out_group = lax.dynamic_slice_in_dim(out_weight, head_group * HEADS_DEV, HEADS_DEV, 1)

            def attend_part(qkv_part, gain_vec, gain_pair):
                return head_attend(blocks, qkv_part, gain_vec, gain_pair, valid_rows)

            def project_part(attended, out_part):
                return head_project(attended, out_part, valid_rows)
            attended, pull_attend = jax.vjp(attend_part, qkv_group, ln_gain, qk_gains)
            branch, pull_project = jax.vjp(project_part, attended, out_group)
            grad_attended, grad_o = pull_project(cot_here)
            grad_q, grad_l, grad_g = pull_attend(grad_attended)
            return (branch, grad_q, grad_o, grad_l, grad_g)
        branches, grad_q, grad_o, grad_l, grad_g = jax.vmap(one_group)(group_ids)
        summed = blocks.astype(jnp.float32) + lax.optimization_barrier(jnp.sum(branches, axis=0))
        result = jnp.where(valid_rows[..., None], summed, 0.0).astype(jnp.bfloat16)
        full_q = jnp.transpose(grad_q, (1, 0, 2, 3)).reshape(D, HEADS, 3 * HEAD).astype(jnp.float32)
        full_o = jnp.transpose(grad_o, (1, 0, 2, 3)).reshape(D, HEADS, HEAD).astype(jnp.float32)
        total_q, total_o, total_l, total_g = totals
        totals = (total_q + full_q, total_o + full_o, total_l + lax.optimization_barrier(jnp.sum(grad_l, axis=0)), total_g + lax.optimization_barrier(jnp.sum(grad_g, axis=0)))
        return (totals, result)
    initial = (jnp.zeros((D, HEADS, 3 * HEAD), jnp.float32), jnp.zeros((D, HEADS, HEAD), jnp.float32), jnp.zeros((D,), jnp.float32), jnp.zeros((2, HEAD), jnp.float32))
    totals, stacked = lax.scan(group_step, initial, jnp.arange(N_DP, dtype=jnp.int32))
    block_out = stacked.reshape(N_DP * IMAGES, BLOCK, D)
    return (block_out, totals[0], totals[1], totals[2], totals[3])
```

```python
import math

import jax
import jax.numpy as jnp
import numpy as np
from jax import lax
from jax.experimental import pallas as pl
from jax.experimental.pallas import tpu as pltpu
from jax.sharding import PartitionSpec as P

EPSILON = 1e-06
BF = jnp.bfloat16
F32 = jnp.float32

NZ, NY, NC = 4, 4, 2
NX, NL = 4, 2
N_DP = NZ * NY * NC
N_SHARD = NX * NL
ROWS = 128

QKV_GROUPS = {"own": (0,), "near": (1, 3), "far": (2,)}
Y_ORDER = (0, 1, 3, 2)
Z_ORDER = (0, 1, 3, 2)
QKV_ORDER = [
    (c, y, z) for c in range(NC) for zs in QKV_GROUPS.values() for y in Y_ORDER for z in zs
]
OUT_ORDER = [(c, y, z) for c in range(NC) for y in Y_ORDER for z in Z_ORDER]


def dp_shift(value, dz=0, dy=0, dc=0):
    pairs = []
    for z in range(NZ):
        for y in range(NY):
            for c in range(NC):
                target = ((z + dz) % NZ) * NY * NC + ((y + dy) % NY) * NC + (c + dc) % NC
                pairs.append((z * NY * NC + y * NC + c, target))
    return lax.ppermute(value, "dp", pairs)


def dp_rotate(value, steps):
    return lax.ppermute(value, "dp", [(s, (s + steps) % N_DP) for s in range(N_DP)])


def shard_shift(value, dx=0, dl=0):
    pairs = []
    for x in range(NX):
        for low in range(NL):
            pairs.append((x * NL + low, ((x + dx) % NX) * NL + (low + dl) % NL))
    return lax.ppermute(value, "shard", pairs)


def absolute_blocks(order):
    me = lax.axis_index("dp")
    z, y, c = me // (NY * NC), (me // NC) % NY, me % NC
    table = np.asarray(order, dtype=np.int32)
    return (
        ((z + table[:, 2]) % NZ) * (NY * NC) + ((y + table[:, 1]) % NY) * NC + (c + table[:, 0]) % NC
    ).astype(jnp.int32)


def ring_gather(piece, shift):
    half = piece.shape[0] // 2
    ahead, behind = shift(piece, -1), shift(piece, 1)
    across = jnp.concatenate([shift(ahead[:half], -1), shift(behind[half:], 1)], axis=0)
    return [piece, ahead, behind, across]


def ring_scatter(own, ahead, behind, across, shift):
    half = across.shape[0] // 2
    first, second = shift(across[:half], 1), shift(across[half:], -1)
    ahead = jnp.concatenate(
        [(ahead[:half].astype(F32) + first.astype(F32)).astype(BF), ahead[half:]], axis=0
    )
    behind = jnp.concatenate(
        [behind[:half], (behind[half:].astype(F32) + second.astype(F32)).astype(BF)], axis=0
    )
    return own.astype(F32) + shift(ahead, 1).astype(F32) + shift(behind, -1).astype(F32)


def y_step(value, steps):
    return dp_shift(value, dy=steps)


def z_step(value, steps):
    return dp_shift(value, dz=steps)


def gather_qkv(weight):
    z_own, z_ahead, z_behind, z_across = ring_gather(weight, z_step)
    parts = {}
    for name, piece in (
        ("own", z_own),
        ("near", jnp.concatenate([z_ahead, z_behind], axis=0)),
        ("far", z_across),
    ):
        half = jnp.concatenate(ring_gather(piece, y_step), axis=0)
        parts[name] = half
    mine = [parts["own"], parts["near"], parts["far"]]
    other = [dp_shift(part, dc=1) for part in mine]
    return mine + other


def gather_out(weight):
    z_all = jnp.concatenate(
        [weight, z_step(weight, -1), z_step(weight, 1), z_step(weight, 2)], axis=0
    )
    mine = jnp.concatenate(ring_gather(z_all, y_step), axis=0)
    return mine, dp_shift(mine, dc=1)


def core_sum(mine, other):
    return (mine + dp_shift(other, dc=1).astype(F32)).astype(BF)


def quarter(value, index):
    size = value.shape[0] // 4
    return value[index * size : (index + 1) * size]


def scatter_y(total):
    return ring_scatter(*[quarter(total, i) for i in range(4)], y_step)


def scatter_out(total):
    sums = scatter_y(total).astype(BF)
    own, ahead, behind, across = [quarter(sums, i) for i in range(4)]
    return (own.astype(F32) + z_step(ahead, 1).astype(F32) + z_step(behind, -1).astype(F32)) + (
        z_step(across, 2).astype(F32)
    )


def sum_everywhere(value):
    value = value + dp_shift(value, dc=1)
    for shift in (y_step, z_step, lambda v, n: shard_shift(v, dx=n)):
        value = (value + shift(value, 2)) + (shift(value, 1) + shift(value, 3))
    return value + shard_shift(value, dl=1)


def norm_kernel(table, tokens, gain, out):
    width = tokens.shape[0] * tokens.shape[2]
    per = tokens.shape[2] // ROWS
    rows = tokens.shape[1]
    total = jnp.zeros((rows, ROWS), F32)
    for j in range(width // ROWS):
        total += tokens[j // per, :, (j % per) * ROWS : (j % per + 1) * ROWS].astype(F32)
    mean = jnp.sum(total, axis=-1, keepdims=True) / width
    square = jnp.zeros((rows, ROWS), F32)
    for j in range(width // ROWS):
        part = tokens[j // per, :, (j % per) * ROWS : (j % per + 1) * ROWS].astype(F32) - mean
        square += part * part
    scale = lax.rsqrt(jnp.sum(square, axis=-1, keepdims=True) / width + EPSILON)
    for j in range(width // ROWS):
        block = table[j]
        at = pl.multiple_of((block % per) * ROWS, ROWS)
        part = tokens[block // per, :, pl.ds(at, ROWS)].astype(F32) - mean
        full_at = pl.multiple_of(block * ROWS, ROWS)
        out[:, j * ROWS : (j + 1) * ROWS] = (part * scale * gain[:, pl.ds(full_at, ROWS)]).astype(BF)


def reorder_kernel(table, values, keep, out):
    for j in range(values.shape[1] // ROWS):
        at = pl.multiple_of(table[j] * ROWS, ROWS)
        part = values[:, pl.ds(at, ROWS)].astype(F32)
        out[:, j * ROWS : (j + 1) * ROWS] = jnp.where(keep[...] > 0, part, 0.0).astype(BF)


def dot_nt(left, right):
    return lax.dot_general(left, right, (((1,), (1,)), ((), ())), preferred_element_type=F32)


def dot_tn(left, right):
    return lax.dot_general(left, right, (((0,), (0,)), ((), ())), preferred_element_type=F32)


def head_norm(values):
    centred = values - jnp.mean(values, axis=-1, keepdims=True)
    scale = lax.rsqrt(jnp.mean(centred * centred, axis=-1, keepdims=True) + EPSILON)
    return centred * scale, scale


def block_mask(valid_keys, block_len):
    rows = valid_keys.shape[1]
    row_block = lax.broadcasted_iota(jnp.int32, (rows, rows), 0) // block_len
    col_block = lax.broadcasted_iota(jnp.int32, (rows, rows), 1) // block_len
    return (row_block == col_block) & (valid_keys > 0)


def softmax(queries, keys, mask, size):
    scores = dot_nt(queries, keys) / math.sqrt(size)
    scores = jnp.where(mask, scores, -1e30)
    expo = jnp.exp(scores - jnp.max(scores, axis=-1, keepdims=True))
    return expo / jnp.sum(expo, axis=-1, keepdims=True)


def make_attend_kernel(block_len, size):
    def kernel(projected, gains, valid_keys, attended):
        mask = block_mask(valid_keys[...], block_len)
        for head in range(projected.shape[1] // (3 * size)):
            at = head * 3 * size
            q_hat, _ = head_norm(projected[:, at : at + size])
            k_hat, _ = head_norm(projected[:, at + size : at + 2 * size])
            queries = (q_hat * gains[0:1, :]).astype(BF)
            keys = (k_hat * gains[1:2, :]).astype(BF)
            values = projected[:, at + 2 * size : at + 3 * size].astype(BF)
            attend = softmax(queries, keys, mask, size).astype(BF)
            attended[:, head * size : (head + 1) * size] = jnp.dot(
                attend, values, preferred_element_type=F32
            ).astype(BF)

    return kernel


def make_attend_back_kernel(block_len, size):
    def norm_back(grad, hat, scale, gain):
        inner = grad * gain
        middle = jnp.mean(inner, axis=-1, keepdims=True)
        slope = jnp.mean(inner * hat, axis=-1, keepdims=True)
        return scale * (inner - middle - hat * slope)

    def kernel(projected, gains, valid_keys, grad_attended, grad_projected, grad_gains):
        mask = block_mask(valid_keys[...], block_len)
        gain_q, gain_k = gains[0:1, :], gains[1:2, :]
        sum_q = jnp.zeros((1, size), F32)
        sum_k = jnp.zeros((1, size), F32)
        for head in range(projected.shape[1] // (3 * size)):
            at = head * 3 * size
            q_hat, q_scale = head_norm(projected[:, at : at + size])
            k_hat, k_scale = head_norm(projected[:, at + size : at + 2 * size])
            queries = (q_hat * gain_q).astype(BF)
            keys = (k_hat * gain_k).astype(BF)
            values = projected[:, at + 2 * size : at + 3 * size].astype(BF)
            soft = softmax(queries, keys, mask, size)
            grad_out = grad_attended[:, head * size : (head + 1) * size]
            grad_values = dot_tn(soft.astype(BF), grad_out).astype(BF)
            grad_attend = dot_nt(grad_out, values).astype(BF).astype(F32)
            inner = jnp.sum(grad_attend * soft, axis=-1, keepdims=True)
            grad_scores = soft * (grad_attend - inner) / math.sqrt(size)
            grad_scores = jnp.where(mask, grad_scores, 0.0).astype(BF)
            grad_q = jnp.dot(grad_scores, keys, preferred_element_type=F32).astype(BF).astype(F32)
            grad_k = dot_tn(grad_scores, queries).astype(BF).astype(F32)
            sum_q += jnp.sum(grad_q * q_hat, axis=0, keepdims=True)
            sum_k += jnp.sum(grad_k * k_hat, axis=0, keepdims=True)
            grad_projected[:, at : at + size] = norm_back(grad_q, q_hat, q_scale, gain_q).astype(BF)
            grad_projected[:, at + size : at + 2 * size] = norm_back(
                grad_k, k_hat, k_scale, gain_k
            ).astype(BF)
            grad_projected[:, at + 2 * size : at + 3 * size] = grad_values
        grad_gains[0:1, :] = sum_q
        grad_gains[1:2, :] = sum_k

    return kernel


def branch_kernel(table, attended, weight_mine, weight_other, branch):
    per = branch.shape[2] // ROWS
    half = weight_mine.shape[0] // ROWS
    for j in range(2 * half):
        weight = weight_mine if j < half else weight_other
        rows = weight[(j % half) * ROWS : (j % half + 1) * ROWS, :]
        block = table[j]
        at = pl.multiple_of((block % per) * ROWS, ROWS)
        branch[block // per, :, pl.ds(at, ROWS)] = dot_nt(attended[...], rows).astype(BF)


def gain_kernel(table, grad_projected, normed, *refs):
    weights, out = refs[:-1], refs[-1]
    step = 4
    j = 0
    for weight in weights:
        for at in range(0, weight.shape[0], step * ROWS):
            rows = weight[at : at + step * ROWS, :]
            grad = dot_nt(grad_projected[...], rows).astype(BF).astype(F32)
            here = normed[:, j * ROWS : (j + step) * ROWS].astype(F32)
            sums = jnp.sum(grad * here, axis=0, keepdims=True)
            for k in range(step):
                out[pl.ds(table[j + k], 1), :] = sums[:, k * ROWS : (k + 1) * ROWS]
            j += step


def call(kernel, shapes, tables, *arrays, flops=0):
    smem = pl.BlockSpec(memory_space=pltpu.SMEM)
    vmem = pl.BlockSpec(memory_space=pltpu.VMEM)
    several = isinstance(shapes, tuple)
    moved = sum(a.size * a.dtype.itemsize for a in arrays)
    return pl.pallas_call(
        kernel,
        out_shape=shapes,
        in_specs=[smem] * len(tables) + [vmem] * len(arrays),
        out_specs=(vmem,) * len(shapes) if several else vmem,
        compiler_params=pltpu.CompilerParams(vmem_limit_bytes=40 * 1024 * 1024),
        cost_estimate=pl.CostEstimate(flops=flops, bytes_accessed=moved, transcendentals=0),
    )(*tables, *arrays)


def shape(dims, dtype):
    return jax.ShapeDtypeStruct(dims, dtype)


def per_device(
    packed,
    counts,
    dest_plan,
    source_plan,
    slot_counts,
    cotangent,
    qkv_weight,
    out_weight,
    ln_gain,
    qk_gains,
):
    image_total = counts.shape[1]
    half_images = image_total // 2
    far_gap = N_DP // 2 - half_images
    block_len, width = cotangent.shape[1], cotangent.shape[2]
    rows = image_total * block_len
    heads, size = out_weight.shape[1], out_weight.shape[2]
    share = width // N_SHARD
    me = lax.axis_index("shard")

    qkv_table = absolute_blocks(QKV_ORDER)
    out_table = absolute_blocks(OUT_ORDER)
    qkv_parts = gather_qkv(qkv_weight.reshape(ROWS, heads * 3 * size))
    out_mine, out_other = gather_out(out_weight.reshape(ROWS, heads * size))

    packed_share = lax.dynamic_slice_in_dim(packed, me * share, share, 1)
    image_counts = counts[0]
    offsets = jnp.cumsum(image_counts) - image_counts
    positions = jnp.arange(block_len, dtype=jnp.int32)
    offset_ids = jnp.arange(image_total, dtype=jnp.int32)
    chosen = dest_plan[0][None, :] == offset_ids[:, None]
    starts = jnp.sum(jnp.where(chosen, offsets[None, :], 0), axis=1)
    lengths = jnp.sum(jnp.where(chosen, image_counts[None, :], 0), axis=1)
    row_index = jnp.clip(starts[:, None] + positions[None, :], 0, packed.shape[0] - 1)
    keep_rows = (positions[None, :] < lengths[:, None])[..., None]
    outgoing = jnp.where(
        keep_rows, jnp.take(packed_share, row_index, axis=0), jnp.zeros((), BF)
    )
    received = [outgoing[0]]
    for number in range(1, image_total):
        distance = number + (far_gap if number >= half_images else 0)
        received.append(dp_rotate(outgoing[number], distance))
    arrived = jnp.stack(received)
    block_share = jnp.take(arrived, source_plan[0], axis=0)
    tokens = lax.all_gather(block_share.reshape(rows, share), "shard", axis=0, tiled=False)

    valid_rows = positions[None, :] < slot_counts[0][:, None]
    valid_keys = valid_rows.astype(F32).reshape(1, rows)
    valid_column = valid_rows.astype(F32).reshape(rows, 1)

    normed = call(
        norm_kernel, shape((rows, width), BF), (qkv_table,), tokens, ln_gain.reshape(1, width)
    )
    cot = call(
        reorder_kernel,
        shape((rows, width), BF),
        (out_table,),
        cotangent.reshape(rows, width),
        valid_column,
    )

    bounds = np.cumsum([0] + [part.shape[0] for part in qkv_parts])
    columns = [normed[:, a:b] for a, b in zip(bounds[:-1], bounds[1:])]
    projected = sum(
        jnp.dot(column, part, preferred_element_type=F32)
        for column, part in zip(columns, qkv_parts)
    )
    attended = call(
        make_attend_kernel(block_len, size),
        shape((rows, heads * size), BF),
        (),
        projected,
        qk_gains,
        valid_keys,
    )

    half = width // 2
    out_other_grad = dot_tn(cot[:, half:], attended).astype(BF)
    out_mine_grad = dot_tn(cot[:, :half], attended)
    final_o = scatter_out(core_sum(out_mine_grad, out_other_grad))

    branch = call(
        branch_kernel,
        shape((N_SHARD, rows, share), BF),
        (out_table,),
        attended,
        out_mine,
        out_other,
        flops=2 * rows * width * heads * size,
    )
    summed = lax.psum_scatter(branch, "shard", scatter_dimension=0, tiled=False)
    summed = summed.reshape(image_total, block_len, share).astype(F32)
    block_out = jnp.where(valid_rows[..., None], block_share.astype(F32) + summed, 0.0).astype(BF)

    grad_attended = (
        jnp.dot(cot[:, :half], out_mine, preferred_element_type=F32)
        + jnp.dot(cot[:, half:], out_other, preferred_element_type=F32)
    ).astype(BF)
    grad_projected, grad_gains = call(
        make_attend_back_kernel(block_len, size),
        (shape((rows, heads * 3 * size), BF), shape((2, size), F32)),
        (),
        projected,
        qk_gains,
        valid_keys,
        grad_attended,
    )
    grad_gain = call(
        gain_kernel,
        shape((N_DP, ROWS), F32),
        (qkv_table,),
        grad_projected,
        normed,
        *qkv_parts,
        flops=2 * rows * width * heads * 3 * size,
    )
    grad_gain = grad_gain / ln_gain.reshape(N_DP, ROWS)

    count = len(QKV_GROUPS)
    sums = []
    for index in reversed(range(count)):
        other = dot_tn(columns[count + index], grad_projected).astype(BF)
        mine = dot_tn(columns[index], grad_projected)
        sums.append(scatter_y(core_sum(mine, other)).astype(BF))
    far, near, own = sums
    final_q = ring_scatter(own, near[:ROWS], near[ROWS:], far, z_step)

    totals = sum_everywhere(jnp.concatenate([grad_gain, grad_gains], axis=0))
    return (
        block_out,
        final_q.reshape(ROWS, heads, 3 * size),
        final_o.reshape(ROWS, heads, size),
        totals[:N_DP].reshape(width),
        totals[N_DP:],
    )


def solution(mesh):
    return jax.shard_map(
        per_device,
        mesh=mesh,
        in_specs=(
            P("dp", None),
            P("dp", None),
            P("dp", None),
            P("dp", None),
            P("dp", None),
            P("dp", None, None),
            P("dp", "shard", None),
            P("dp", "shard", None),
            P(),
            P(),
        ),
        out_specs=(
            P("dp", None, "shard"),
            P("dp", "shard", None),
            P("dp", "shard", None),
            P(),
            P(),
        ),
        check_vma=False,
    )
```

```python
import math

import jax
import jax.numpy as jnp
import numpy as np
from jax import lax
from jax.experimental import pallas as pl
from jax.experimental.pallas import tpu as pltpu
from jax.sharding import PartitionSpec as P

EPSILON = 1e-06
BF = jnp.bfloat16
F32 = jnp.float32

NZ, NY, NC = 4, 4, 2
NX, NL = 4, 2
N_DP = NZ * NY * NC
N_SHARD = NX * NL
ROWS = 128

QKV_PARTS = (
    ((0, 0), (0, 1), (0, 3), (1, 0), (3, 0)),
    ((1, 1), (1, 3), (2, 0), (3, 1), (3, 3), (0, 2)),
    ((1, 2), (2, 1)),
    ((3, 2), (2, 3)),
    ((2, 2),),
)
QKV_ORDER = [(c, y, z) for c in range(NC) for part in QKV_PARTS for y, z in part]
EARLY = 10 * ROWS
OUT_ORDER = [(c, y, z) for c in range(NC) for y in (0, 1, 3, 2) for z in (0, 1, 3, 2)]


def dp_shift(value, dz=0, dy=0, dc=0):
    pairs = []
    for z in range(NZ):
        for y in range(NY):
            for c in range(NC):
                target = ((z + dz) % NZ) * NY * NC + ((y + dy) % NY) * NC + (c + dc) % NC
                pairs.append((z * NY * NC + y * NC + c, target))
    return lax.ppermute(value, "dp", pairs)


def dp_rotate(value, steps):
    return lax.ppermute(value, "dp", [(s, (s + steps) % N_DP) for s in range(N_DP)])


def shard_shift(value, dx=0, dl=0):
    pairs = []
    for x in range(NX):
        for low in range(NL):
            pairs.append((x * NL + low, ((x + dx) % NX) * NL + (low + dl) % NL))
    return lax.ppermute(value, "shard", pairs)


def absolute_blocks(order):
    me = lax.axis_index("dp")
    z, y, c = me // (NY * NC), (me // NC) % NY, me % NC
    table = np.asarray(order, dtype=np.int32)
    return (
        ((z + table[:, 2]) % NZ) * (NY * NC) + ((y + table[:, 1]) % NY) * NC + (c + table[:, 0]) % NC
    ).astype(jnp.int32)


def y_step(value, steps):
    return dp_shift(value, dy=steps)


def z_step(value, steps):
    return dp_shift(value, dz=steps)


def swap(value):
    return dp_shift(value, dc=1)


def combine(plans, *arrays, after=(), dtype=BF):
    count = len(arrays)
    width = arrays[0].shape[1]

    def kernel(*refs):
        for plan, out in zip(plans, refs[count + len(after) :]):
            at = 0
            for terms in plan:
                rows = terms[0][2] - terms[0][1]
                parts = [refs[i][a:b, :] for i, a, b in terms]
                if len(parts) > 1:
                    parts = [part.astype(F32) for part in parts]
                total = parts[0]
                for part in parts[1:]:
                    total = total + part
                out[at : at + rows, :] = total.astype(dtype)
                at += rows

    sizes = [sum(terms[0][2] - terms[0][1] for terms in plan) for plan in plans]
    return call(kernel, tuple(shape((size, width), dtype) for size in sizes), (), *arrays, after=after)


def gather_qkv(weight):
    one = ROWS
    z_ahead, z_behind = z_step(weight, -1), z_step(weight, 1)
    y_ahead, y_behind = y_step(weight, -1), y_step(weight, 1)
    z_across = z_step(z_ahead, -1)
    first, up, near = combine(
        (
            (((0, 0, one),), ((1, 0, one),), ((2, 0, one),), ((3, 0, one),), ((4, 0, one),)),
            (((1, 0, one),), ((2, 0, one),), ((3, 0, one),)),
            (((1, 0, one),), ((2, 0, one),)),
        ),
        weight,
        z_ahead,
        z_behind,
        y_ahead,
        y_behind,
    )
    other_first = swap(first)
    from_ahead, from_behind = y_step(up, -1), y_step(near, 1)
    second, up, down = combine(
        (
            (((0, 0, 3 * one),), ((1, 0, 2 * one),), ((2, 0, one),)),
            (((2, 0, one),), ((0, 0, one),)),
            (((2, 0, one),), ((1, one, 2 * one),)),
        ),
        from_ahead,
        from_behind,
        z_across,
        after=(other_first,),
    )
    third, fourth = y_step(up, -1), y_step(down, 1)
    fifth = y_step(fourth[:one], 1)
    mine = [first, second, third, fourth, fifth]
    return mine, [other_first] + [swap(part) for part in mine[1:]]


def gather_out(weight, after_z, after_y):
    one = ROWS
    (weight,) = combine(((((0, 0, one),),),), weight, after=after_z)
    z_ahead, z_behind = z_step(weight, -1), z_step(weight, 1)
    z_across = z_step(z_ahead, -1)
    (column,) = combine(
        ((((0, 0, one),), ((1, 0, one),), ((2, 0, one),), ((3, 0, one),)),),
        weight,
        z_ahead,
        z_behind,
        z_across,
        after=after_y,
    )
    y_ahead, y_behind = y_step(column, -1), y_step(column, 1)
    first, up, down = combine(
        (
            (((0, 0, 4 * one),), ((1, 0, 4 * one),), ((2, 0, 4 * one),)),
            (((1, 0, 2 * one),),),
            (((2, 2 * one, 4 * one),),),
        ),
        column,
        y_ahead,
        y_behind,
    )
    (second,) = combine(
        ((((0, 0, 2 * one),), ((1, 0, 2 * one),)),), y_step(up, -1), y_step(down, 1)
    )
    return (first, second), (swap(first), swap(second))


def core_sums(left, right, base, received, bounds, after=()):
    def kernel(left_ref, right_ref, received_ref, *refs):
        outs = refs[len(after) :]
        for (a, b), out in zip(bounds, outs):
            product = dot_tn(left_ref[:, base + a : base + b], right_ref[...])
            out[...] = (product + received_ref[a:b, :].astype(F32)).astype(BF)

    shapes = tuple(shape((b - a, right.shape[1]), BF) for a, b in bounds)
    return call(kernel, shapes, (), left, right, received, after=after)


def part_product(left, right, base, rows, after=()):
    def kernel(*refs):
        left_ref, right_ref, out = refs[0], refs[1], refs[-1]
        step = 2 * ROWS
        for a in range(0, rows, step):
            out[a : a + step, :] = dot_tn(
                left_ref[:, base + a : base + a + step], right_ref[...]
            ).astype(BF)

    return call(kernel, shape((rows, right.shape[1]), BF), (), left, right, after=after)


def scatter_qkv(normed, grad, after, after_late):
    one = ROWS
    half = normed.shape[1] // 2
    late = half - EARLY
    product = part_product(normed, grad, half + EARLY, late, after)
    late_other = swap(product)
    early_other = swap(part_product(normed, grad, half, EARLY, (product,)))
    rows = lambda *at: [(a * one, b * one) for a, b in at]
    s02, s12_21, s32_23, s22 = core_sums(
        normed, grad, EARLY, late_other, rows((0, 1), (1, 3), (3, 5), (5, 6)), after_late
    )
    hop = y_step(s22, 1)
    s00, s01_03, s10, s30, s11_13, s20, s31_33 = core_sums(
        normed,
        grad,
        0,
        early_other,
        rows((0, 1), (1, 3), (3, 4), (4, 5), (5, 7), (7, 8), (8, 10)),
    )
    (plus,) = combine(
        ((((0, 0, one), (1, 0, one)), ((0, one, 2 * one),)),), s12_21, hop
    )
    below, above = y_step(plus, 1), y_step(s32_23, -1)
    plus, minus, z_across = combine(
        (
            (((0, 0, one), (3, one, 2 * one)), ((0, one, 2 * one),)),
            (
                ((1, 0, one),),
                ((1, one, 2 * one), (4, one, 2 * one)),
                ((2, 0, one),),
            ),
            (((5, 0, one), (3, 0, one), (4, 0, one)),),
        ),
        s11_13,
        s31_33,
        s20,
        below,
        above,
        s02,
    )
    z_hop = z_step(z_across, 1)
    below, above = y_step(plus, 1), y_step(minus, -1)
    last_below = y_step(s10, 1)
    midway = z_across
    minus, z_ahead, z_behind = combine(
        (
            (((0, 0, one), (1, 2 * one, 3 * one)),),
            (((2, 0, one), (3, 0, one), (1, 0, one), (4, 0, one)),),
            (((2, one, 2 * one), (3, one, 2 * one), (1, one, 2 * one)),),
        ),
        s30,
        above,
        s01_03,
        below,
        z_hop,
        after=(last_below,),
    )
    last_above = y_step(minus, -1)
    from_below, from_above = z_step(z_ahead, 1), z_step(z_behind, -1)
    (total,) = combine(
        ((tuple((i, 0, one) for i in range(5)),),),
        s00,
        last_below,
        last_above,
        from_below,
        from_above,
        dtype=F32,
    )
    return total, midway


def scatter_out(cot, attended):
    one = ROWS
    half = cot.shape[1] // 2
    product = part_product(cot, attended, half, half)
    other = swap(product)
    own, ahead, behind, across_up, across_down = core_sums(
        cot,
        attended,
        0,
        other,
        [(a * one, b * one) for a, b in ((0, 4), (4, 8), (8, 12), (12, 14), (14, 16))],
    )
    up, down = y_step(across_up, 1), y_step(across_down, -1)
    plus, minus = combine(
        (
            (((0, 0, 2 * one), (2, 0, 2 * one)), ((0, 2 * one, 4 * one),)),
            (((1, 0, 2 * one),), ((1, 2 * one, 4 * one), (3, 0, 2 * one))),
        ),
        ahead,
        behind,
        up,
        down,
    )
    below, above = y_step(plus, 1), y_step(minus, -1)
    parts = combine(
        tuple(
            (tuple((i, k * one, (k + 1) * one) for i in range(3)),) for k in range(4)
        ),
        own,
        below,
        above,
    )
    (total,) = combine(
        ((tuple((i, 0, one) for i in range(4)),),),
        parts[0],
        z_step(parts[1], 1),
        z_step(parts[2], -1),
        z_step(parts[3], 2),
        dtype=F32,
    )
    return total, (own,), (up, down), (below, above)


def sum_everywhere(value):
    value = value + swap(value)
    for shift in (y_step, z_step, lambda v, n: shard_shift(v, dx=n)):
        value = (value + shift(value, 2)) + (shift(value, 1) + shift(value, 3))
    return value + shard_shift(value, dl=1)


def norm_kernel(table, tokens, gain, out):
    width = tokens.shape[0] * tokens.shape[2]
    per = tokens.shape[2] // ROWS
    rows = tokens.shape[1]
    total = jnp.zeros((rows, ROWS), F32)
    for j in range(width // ROWS):
        total += tokens[j // per, :, (j % per) * ROWS : (j % per + 1) * ROWS].astype(F32)
    mean = jnp.sum(total, axis=-1, keepdims=True) / width
    square = jnp.zeros((rows, ROWS), F32)
    for j in range(width // ROWS):
        part = tokens[j // per, :, (j % per) * ROWS : (j % per + 1) * ROWS].astype(F32) - mean
        square += part * part
    scale = lax.rsqrt(jnp.sum(square, axis=-1, keepdims=True) / width + EPSILON)
    for j in range(width // ROWS):
        block = table[j]
        at = pl.multiple_of((block % per) * ROWS, ROWS)
        part = tokens[block // per, :, pl.ds(at, ROWS)].astype(F32) - mean
        full_at = pl.multiple_of(block * ROWS, ROWS)
        out[:, j * ROWS : (j + 1) * ROWS] = (part * scale * gain[:, pl.ds(full_at, ROWS)]).astype(BF)


def reorder_kernel(table, values, keep, out):
    for j in range(values.shape[1] // ROWS):
        at = pl.multiple_of(table[j] * ROWS, ROWS)
        part = values[:, pl.ds(at, ROWS)].astype(F32)
        out[:, j * ROWS : (j + 1) * ROWS] = jnp.where(keep[...] > 0, part, 0.0).astype(BF)


def dot_nt(left, right):
    return lax.dot_general(left, right, (((1,), (1,)), ((), ())), preferred_element_type=F32)


def dot_tn(left, right):
    return lax.dot_general(left, right, (((0,), (0,)), ((), ())), preferred_element_type=F32)


def head_norm(values):
    centred = values - jnp.mean(values, axis=-1, keepdims=True)
    scale = lax.rsqrt(jnp.mean(centred * centred, axis=-1, keepdims=True) + EPSILON)
    return centred * scale, scale


def block_mask(valid_keys, block_len):
    rows = valid_keys.shape[1]
    row_block = lax.broadcasted_iota(jnp.int32, (rows, rows), 0) // block_len
    col_block = lax.broadcasted_iota(jnp.int32, (rows, rows), 1) // block_len
    return (row_block == col_block) & (valid_keys > 0)


def softmax(queries, keys, mask, size):
    scores = dot_nt(queries, keys) / math.sqrt(size)
    scores = jnp.where(mask, scores, -1e30)
    expo = jnp.exp(scores - jnp.max(scores, axis=-1, keepdims=True))
    return expo / jnp.sum(expo, axis=-1, keepdims=True)


def project_kernel_over(bounds, carry):
    def kernel(*refs):
        sums = refs[0] if carry else None
        normed, weights, out = refs[carry], refs[carry + 1 : -1], refs[-1]
        step = 3 * ROWS
        for at in range(0, out.shape[1], step):
            total = sums[:, at : at + step] if carry else jnp.zeros((out.shape[0], step), F32)
            for (a, b), weight in zip(bounds, weights):
                total += jnp.dot(
                    normed[:, a:b], weight[:, at : at + step], preferred_element_type=F32
                )
            out[:, at : at + step] = total

    return kernel


def make_attend_kernel(block_len, size):
    def kernel(projected, gains, valid_keys, attended):
        mask = block_mask(valid_keys[...], block_len)
        for head in range(projected.shape[1] // (3 * size)):
            at = head * 3 * size
            q_hat, _ = head_norm(projected[:, at : at + size])
            k_hat, _ = head_norm(projected[:, at + size : at + 2 * size])
            queries = (q_hat * gains[0:1, :]).astype(BF)
            keys = (k_hat * gains[1:2, :]).astype(BF)
            values = projected[:, at + 2 * size : at + 3 * size].astype(BF)
            attend = softmax(queries, keys, mask, size).astype(BF)
            attended[:, head * size : (head + 1) * size] = jnp.dot(
                attend, values, preferred_element_type=F32
            ).astype(BF)

    return kernel


def make_attend_back_kernel(block_len, size):
    def norm_back(grad, hat, scale, gain):
        inner = grad * gain
        middle = jnp.mean(inner, axis=-1, keepdims=True)
        slope = jnp.mean(inner * hat, axis=-1, keepdims=True)
        return scale * (inner - middle - hat * slope)

    def kernel(projected, gains, valid_keys, grad_attended, after, grad_projected, grad_gains):
        mask = block_mask(valid_keys[...], block_len)
        gain_q, gain_k = gains[0:1, :], gains[1:2, :]
        sum_q = jnp.zeros((1, size), F32)
        sum_k = jnp.zeros((1, size), F32)
        for head in range(projected.shape[1] // (3 * size)):
            at = head * 3 * size
            q_hat, q_scale = head_norm(projected[:, at : at + size])
            k_hat, k_scale = head_norm(projected[:, at + size : at + 2 * size])
            queries = (q_hat * gain_q).astype(BF)
            keys = (k_hat * gain_k).astype(BF)
            values = projected[:, at + 2 * size : at + 3 * size].astype(BF)
            soft = softmax(queries, keys, mask, size)
            grad_out = grad_attended[:, head * size : (head + 1) * size]
            grad_values = dot_tn(soft.astype(BF), grad_out).astype(BF)
            grad_attend = dot_nt(grad_out, values).astype(BF).astype(F32)
            inner = jnp.sum(grad_attend * soft, axis=-1, keepdims=True)
            grad_scores = soft * (grad_attend - inner) / math.sqrt(size)
            grad_scores = jnp.where(mask, grad_scores, 0.0).astype(BF)
            grad_q = jnp.dot(grad_scores, keys, preferred_element_type=F32).astype(BF).astype(F32)
            grad_k = dot_tn(grad_scores, queries).astype(BF).astype(F32)
            sum_q += jnp.sum(grad_q * q_hat, axis=0, keepdims=True)
            sum_k += jnp.sum(grad_k * k_hat, axis=0, keepdims=True)
            grad_projected[:, at : at + size] = norm_back(grad_q, q_hat, q_scale, gain_q).astype(BF)
            grad_projected[:, at + size : at + 2 * size] = norm_back(
                grad_k, k_hat, k_scale, gain_k
            ).astype(BF)
            grad_projected[:, at + 2 * size : at + 3 * size] = grad_values
        grad_gains[0:1, :] = sum_q
        grad_gains[1:2, :] = sum_k

    return kernel


def branch_kernel(table, attended, *refs):
    weights, branch = refs[:-1], refs[-1]
    per = branch.shape[2] // ROWS
    j = 0
    for weight in weights:
        step = 2 * ROWS
        for a in range(0, weight.shape[0], step):
            product = dot_nt(attended[...], weight[a : a + step, :]).astype(BF)
            for k in range(2):
                block = table[j + k]
                at = pl.multiple_of((block % per) * ROWS, ROWS)
                branch[block // per, :, pl.ds(at, ROWS)] = product[:, k * ROWS : (k + 1) * ROWS]
            j += 2


def out_back_kernel(cot, *refs):
    weights, out = refs[:-1], refs[-1]
    total = jnp.zeros(out.shape, F32)
    at = 0
    for weight in weights:
        rows = weight.shape[0]
        total += jnp.dot(cot[:, at : at + rows], weight[...], preferred_element_type=F32)
        at += rows
    out[...] = total.astype(BF)


def gain_kernel(table, grad_projected, normed, *refs):
    weights, out = refs[:-2], refs[-1]
    j = 0
    for weight in weights:
        blocks = weight.shape[0] // ROWS
        grad = dot_nt(grad_projected[...], weight[...]).astype(BF).astype(F32)
        here = normed[:, j * ROWS : (j + blocks) * ROWS].astype(F32)
        sums = jnp.sum(grad * here, axis=0, keepdims=True)
        for k in range(blocks):
            out[pl.ds(table[j + k], 1), :] = sums[:, k * ROWS : (k + 1) * ROWS]
        j += blocks


def call(kernel, shapes, tables, *arrays, flops=0, after=()):
    smem = pl.BlockSpec(memory_space=pltpu.SMEM)
    vmem = pl.BlockSpec(memory_space=pltpu.VMEM)
    several = isinstance(shapes, tuple)
    moved = sum(a.size * a.dtype.itemsize for a in arrays)
    return pl.pallas_call(
        kernel,
        out_shape=shapes,
        in_specs=[smem] * len(tables)
        + [vmem] * len(arrays)
        + [pl.BlockSpec(memory_space=pl.ANY)] * len(after),
        out_specs=(vmem,) * len(shapes) if several else vmem,
        compiler_params=pltpu.CompilerParams(vmem_limit_bytes=28 * 1024 * 1024),
        cost_estimate=pl.CostEstimate(flops=flops, bytes_accessed=moved, transcendentals=0),
    )(*tables, *arrays, *after)


def shape(dims, dtype):
    return jax.ShapeDtypeStruct(dims, dtype)


def per_device(
    packed,
    counts,
    dest_plan,
    source_plan,
    slot_counts,
    cotangent,
    qkv_weight,
    out_weight,
    ln_gain,
    qk_gains,
):
    image_total = counts.shape[1]
    half_images = image_total // 2
    far_gap = N_DP // 2 - half_images
    block_len, width = cotangent.shape[1], cotangent.shape[2]
    rows = image_total * block_len
    heads, size = out_weight.shape[1], out_weight.shape[2]
    share = width // N_SHARD
    me = lax.axis_index("shard")

    qkv_table = absolute_blocks(QKV_ORDER)
    out_table = absolute_blocks(OUT_ORDER)
    mine, other = gather_qkv(qkv_weight.reshape(ROWS, heads * 3 * size))
    out_mine, out_other = gather_out(
        out_weight.reshape(ROWS, heads * size), (mine[1],), (mine[2], mine[3], other[1])
    )

    packed_share = lax.dynamic_slice_in_dim(packed, me * share, share, 1)
    image_counts = counts[0]
    offsets = jnp.cumsum(image_counts) - image_counts
    positions = jnp.arange(block_len, dtype=jnp.int32)
    offset_ids = jnp.arange(image_total, dtype=jnp.int32)
    chosen = dest_plan[0][None, :] == offset_ids[:, None]
    starts = jnp.sum(jnp.where(chosen, offsets[None, :], 0), axis=1)
    lengths = jnp.sum(jnp.where(chosen, image_counts[None, :], 0), axis=1)
    row_index = jnp.clip(starts[:, None] + positions[None, :], 0, packed.shape[0] - 1)
    keep_rows = (positions[None, :] < lengths[:, None])[..., None]
    outgoing = jnp.where(
        keep_rows, jnp.take(packed_share, row_index, axis=0), jnp.zeros((), BF)
    )
    arrived = jnp.concatenate(
        [outgoing[:half_images], dp_rotate(outgoing[half_images:], half_images + far_gap)], axis=0
    ).reshape(2, 2, 2, block_len, share)
    moved = dp_rotate(arrived[:, 1], 2)
    arrived = jnp.stack([arrived[:, 0], moved], axis=1)
    moved = dp_rotate(arrived[:, :, 1], 1)
    arrived = jnp.stack([arrived[:, :, 0], moved], axis=2).reshape(image_total, block_len, share)
    block_share = jnp.take(arrived, source_plan[0], axis=0)
    own_share = block_share.reshape(rows, share)
    next_share = shard_shift(own_share, dl=1)
    low = me % NL == 0
    pair = jnp.stack(
        [jnp.where(low, own_share, next_share), jnp.where(low, next_share, own_share)]
    )
    groups = [[x * NL + low_part for x in range(NX)] for low_part in range(NL)]
    tokens = lax.all_gather(pair, "shard", axis=0, tiled=True, axis_index_groups=groups)

    valid_rows = positions[None, :] < slot_counts[0][:, None]
    valid_keys = valid_rows.astype(F32).reshape(1, rows)
    valid_column = valid_rows.astype(F32).reshape(rows, 1)

    normed = call(
        norm_kernel, shape((rows, width), BF), (qkv_table,), tokens, ln_gain.reshape(1, width)
    )
    cot = call(
        reorder_kernel,
        shape((rows, width), BF),
        (out_table,),
        cotangent.reshape(rows, width),
        valid_column,
    )

    parts = mine + other
    bounds = np.cumsum([0] + [part.shape[0] for part in parts])
    bounds = list(zip(bounds[:-1].tolist(), bounds[1:].tolist()))
    early, late = (0, 1, 5, 6), (2, 3, 4, 7, 8, 9)
    projected_shape = shape((rows, heads * 3 * size), F32)
    projected = call(
        project_kernel_over([bounds[i] for i in early], 0),
        projected_shape,
        (),
        normed,
        *[parts[i] for i in early],
        flops=2 * rows * width * heads * 2 * size,
    )
    projected = call(
        project_kernel_over([bounds[i] for i in late], 1),
        projected_shape,
        (),
        projected,
        normed,
        *[parts[i] for i in late],
        flops=2 * rows * width * heads * size,
    )
    attended = call(
        make_attend_kernel(block_len, size),
        shape((rows, heads * size), BF),
        (),
        projected,
        qk_gains,
        valid_keys,
    )

    final_o, out_sums, out_hops, out_moved = scatter_out(cot, attended)

    out_parts = (*out_mine, *out_other)
    branch = call(
        branch_kernel,
        shape((N_SHARD, rows, share), BF),
        (out_table,),
        attended,
        *out_parts,
        flops=2 * rows * width * heads * size,
    )
    summed = lax.psum_scatter(branch, "shard", scatter_dimension=0, tiled=False)
    summed = summed.reshape(image_total, block_len, share).astype(F32)
    block_out = jnp.where(valid_rows[..., None], block_share.astype(F32) + summed, 0.0).astype(BF)

    grad_attended = call(
        out_back_kernel,
        shape((rows, heads * size), BF),
        (),
        cot,
        *out_parts,
        flops=2 * rows * width * heads * size,
    )
    grad_projected, grad_gains = call(
        make_attend_back_kernel(block_len, size),
        (shape((rows, heads * 3 * size), BF), shape((2, size), F32)),
        (),
        projected,
        qk_gains,
        valid_keys,
        grad_attended,
        after=out_sums,
    )
    final_q, midway = scatter_qkv(
        normed, grad_projected, (*out_hops, branch), out_moved
    )
    grad_gain = call(
        gain_kernel,
        shape((N_DP, ROWS), F32),
        (qkv_table,),
        grad_projected,
        normed,
        *parts,
        after=(midway,),
        flops=2 * rows * width * heads * 3 * size,
    )
    grad_gain = grad_gain / ln_gain.reshape(N_DP, ROWS)
    totals = sum_everywhere(jnp.concatenate([grad_gain, grad_gains], axis=0))
    return (
        block_out,
        final_q.reshape(ROWS, heads, 3 * size),
        final_o.reshape(ROWS, heads, size),
        totals[:N_DP].reshape(width),
        totals[N_DP:],
    )


def solution(mesh):
    return jax.shard_map(
        per_device,
        mesh=mesh,
        in_specs=(
            P("dp", None),
            P("dp", None),
            P("dp", None),
            P("dp", None),
            P("dp", None),
            P("dp", None, None),
            P("dp", "shard", None),
            P("dp", "shard", None),
            P(),
            P(),
        ),
        out_specs=(
            P("dp", None, "shard"),
            P("dp", "shard", None),
            P("dp", "shard", None),
            P(),
            P(),
        ),
        check_vma=False,
    )
```

```python
import math

import jax
import jax.numpy as jnp
import numpy as np
from jax import lax
from jax.experimental import pallas as pl
from jax.experimental.pallas import tpu as pltpu
from jax.sharding import PartitionSpec as P

EPSILON = 1e-06
BF = jnp.bfloat16
F32 = jnp.float32

NZ, NY, NC = 4, 4, 2
NX, NL = 4, 2
N_DP = NZ * NY * NC
N_SHARD = NX * NL
ROWS = 128

QKV_PARTS = (
    ((0, 0), (0, 1), (0, 3), (1, 0), (3, 0)),
    ((1, 1), (1, 3), (2, 0), (3, 1), (3, 3), (0, 2)),
    ((1, 2), (2, 1)),
    ((3, 2), (2, 3)),
    ((2, 2),),
)
QKV_ORDER = [(c, y, z) for c in range(NC) for part in QKV_PARTS for y, z in part]
EARLY = 10 * ROWS
OUT_ORDER = [(c, y, z) for c in range(NC) for y in (0, 1, 3, 2) for z in (0, 1, 3, 2)]


def dp_shift(value, dz=0, dy=0, dc=0):
    pairs = []
    for z in range(NZ):
        for y in range(NY):
            for c in range(NC):
                target = ((z + dz) % NZ) * NY * NC + ((y + dy) % NY) * NC + (c + dc) % NC
                pairs.append((z * NY * NC + y * NC + c, target))
    return lax.ppermute(value, "dp", pairs)


def dp_rotate(value, steps):
    return lax.ppermute(value, "dp", [(s, (s + steps) % N_DP) for s in range(N_DP)])


def shard_shift(value, dx=0, dl=0):
    pairs = []
    for x in range(NX):
        for low in range(NL):
            pairs.append((x * NL + low, ((x + dx) % NX) * NL + (low + dl) % NL))
    return lax.ppermute(value, "shard", pairs)


def absolute_blocks(order):
    me = lax.axis_index("dp")
    z, y, c = me // (NY * NC), (me // NC) % NY, me % NC
    table = np.asarray(order, dtype=np.int32)
    return (
        ((z + table[:, 2]) % NZ) * (NY * NC) + ((y + table[:, 1]) % NY) * NC + (c + table[:, 0]) % NC
    ).astype(jnp.int32)


def y_step(value, steps):
    return dp_shift(value, dy=steps)


def z_step(value, steps):
    return dp_shift(value, dz=steps)


def swap(value):
    return dp_shift(value, dc=1)


def combine(plans, *arrays, after=(), dtype=BF):
    count = len(arrays)
    width = arrays[0].shape[1]

    def kernel(*refs):
        for plan, out in zip(plans, refs[count + len(after) :]):
            at = 0
            for terms in plan:
                rows = terms[0][2] - terms[0][1]
                parts = [refs[i][a:b, :] for i, a, b in terms]
                if len(parts) > 1:
                    parts = [part.astype(F32) for part in parts]
                total = parts[0]
                for part in parts[1:]:
                    total = total + part
                out[at : at + rows, :] = total.astype(dtype)
                at += rows

    sizes = [sum(terms[0][2] - terms[0][1] for terms in plan) for plan in plans]
    return call(kernel, tuple(shape((size, width), dtype) for size in sizes), (), *arrays, after=after)


def copied(value, after):
    (value,) = combine(((((0, 0, value.shape[0]),),),), value, after=after, dtype=value.dtype)
    return value


def gather_first(weight, z_ahead, z_behind, y_ahead, y_behind):
    one = ROWS
    return combine(
        (
            tuple(((i, 0, one),) for i in range(5)),
            (((1, 0, one),), ((2, 0, one),), ((3, 0, one),)),
            (((1, 0, one),), ((2, 0, one),)),
        ),
        weight,
        z_ahead,
        z_behind,
        y_ahead,
        y_behind,
    )


def gather_second(from_ahead, from_behind, z_across, after):
    one = ROWS
    return combine(
        (
            (((0, 0, 3 * one),), ((1, 0, 2 * one),), ((2, 0, one),)),
            (((2, 0, one),), ((0, 0, one),)),
            (((2, 0, one),), ((1, one, 2 * one),)),
        ),
        from_ahead,
        from_behind,
        z_across,
        after=after,
    )


def gather_out(weight, z_ahead, z_behind, z_across, after):
    one = ROWS
    (column,) = combine(
        (tuple(((i, 0, one),) for i in range(4)),),
        weight,
        z_ahead,
        z_behind,
        z_across,
        after=after,
    )
    y_ahead, y_behind = y_step(column, -1), y_step(column, 1)
    first, up, down = combine(
        (
            (((0, 0, 4 * one),), ((1, 0, 4 * one),), ((2, 0, 4 * one),)),
            (((1, 0, 2 * one),),),
            (((2, 2 * one, 4 * one),),),
        ),
        column,
        y_ahead,
        y_behind,
    )
    (second,) = combine(
        ((((0, 0, 2 * one),), ((1, 0, 2 * one),)),), y_step(up, -1), y_step(down, 1)
    )
    return (first, second), (swap(first), swap(second)), column, (y_ahead, y_behind)


def core_sums(left, right, base, received, bounds, after=()):
    def kernel(left_ref, right_ref, received_ref, *refs):
        outs = refs[len(after) :]
        for (a, b), out in zip(bounds, outs):
            product = dot_tn(left_ref[:, base + a : base + b], right_ref[...])
            out[...] = (product + received_ref[a:b, :].astype(F32)).astype(BF)

    shapes = tuple(shape((b - a, right.shape[1]), BF) for a, b in bounds)
    return call(kernel, shapes, (), left, right, received, after=after)


def part_product(left, right, base, rows, after=()):
    def kernel(*refs):
        left_ref, right_ref, out = refs[0], refs[1], refs[-1]
        step = 2 * ROWS
        for a in range(0, rows, step):
            out[a : a + step, :] = dot_tn(
                left_ref[:, base + a : base + a + step], right_ref[...]
            ).astype(BF)

    return call(kernel, shape((rows, right.shape[1]), BF), (), left, right, after=after)


def scatter_qkv(normed, grad, after, after_late, after_near, meanwhile):
    one = ROWS
    half = normed.shape[1] // 2
    late = half - EARLY
    product = part_product(normed, grad, half + EARLY, late, after)
    late_other = swap(product)
    early_other = swap(part_product(normed, grad, half, EARLY, (product,)))
    rows = lambda *at: [(a * one, b * one) for a, b in at]
    s02, s12_21, s32_23, s22 = core_sums(
        normed, grad, EARLY, late_other, rows((0, 1), (1, 3), (3, 5), (5, 6)), after_late
    )
    hop = y_step(s22, 1)
    s00, s01_03, s10, s30, s11_13, s20, s31_33 = core_sums(
        normed,
        grad,
        0,
        early_other,
        rows((0, 1), (1, 3), (3, 4), (4, 5), (5, 7), (7, 8), (8, 10)),
    )
    (plus,) = combine(
        ((((0, 0, one), (1, 0, one)), ((0, one, 2 * one),)),), s12_21, hop
    )
    below, above = y_step(plus, 1), y_step(s32_23, -1)
    plus, minus, z_across = combine(
        (
            (((0, 0, one), (3, one, 2 * one)), ((0, one, 2 * one),)),
            (
                ((1, 0, one),),
                ((1, one, 2 * one), (4, one, 2 * one)),
                ((2, 0, one),),
            ),
            (((5, 0, one), (3, 0, one), (4, 0, one)),),
        ),
        s11_13,
        s31_33,
        s20,
        below,
        above,
        s02,
        after=after_near,
    )
    gains = meanwhile(z_across)
    z_hop = z_step(z_across, 1)
    below, above = y_step(plus, 1), y_step(minus, -1)
    last_below = y_step(s10, 1)
    minus, z_ahead, z_behind = combine(
        (
            (((0, 0, one), (1, 2 * one, 3 * one)),),
            (((2, 0, one), (3, 0, one), (1, 0, one), (4, 0, one)),),
            (((2, one, 2 * one), (3, one, 2 * one), (1, one, 2 * one)),),
        ),
        s30,
        above,
        s01_03,
        below,
        z_hop,
        after=(last_below, gains),
    )
    last_above = y_step(minus, -1)
    from_below, from_above = z_step(z_ahead, 1), z_step(z_behind, -1)
    (total,) = combine(
        ((tuple((i, 0, one) for i in range(5)),),),
        s00,
        last_below,
        last_above,
        from_below,
        from_above,
        dtype=F32,
    )
    return total, gains


def scatter_out(cot, attended, after):
    one = ROWS
    half = cot.shape[1] // 2
    product = part_product(cot, attended, half, half, after)
    other = swap(product)
    own, ahead, behind, across_up, across_down = core_sums(
        cot,
        attended,
        0,
        other,
        [(a * one, b * one) for a, b in ((0, 4), (4, 8), (8, 12), (12, 14), (14, 16))],
    )
    up, down = y_step(across_up, 1), y_step(across_down, -1)
    plus, minus = combine(
        (
            (((0, 0, 2 * one), (2, 0, 2 * one)), ((0, 2 * one, 4 * one),)),
            (((1, 0, 2 * one),), ((1, 2 * one, 4 * one), (3, 0, 2 * one))),
        ),
        ahead,
        behind,
        up,
        down,
    )
    below, above = y_step(plus, 1), y_step(minus, -1)
    parts = combine(
        tuple(
            (tuple((i, k * one, (k + 1) * one) for i in range(3)),) for k in range(4)
        ),
        own,
        below,
        above,
    )
    hops = (z_step(parts[1], 1), z_step(parts[2], -1), z_step(parts[3], 2))
    (total,) = combine(
        ((tuple((i, 0, one) for i in range(4)),),), parts[0], *hops, dtype=F32
    )
    return total, (own,), (up, down), (below, above), hops


def ring_sum(value, shift):
    return (value + shift(value, 2)) + (shift(value, 1) + shift(value, 3))


def sum_everywhere(value):
    value = value + swap(value)
    value = ring_sum(value, lambda v, n: shard_shift(v, dx=n))
    value = value + shard_shift(value, dl=1)
    return ring_sum(ring_sum(value, z_step), y_step)


def norm_kernel(places, table, tokens, gain, after, out):
    width = tokens.shape[0] * tokens.shape[2]
    per = tokens.shape[2] // ROWS
    rows = tokens.shape[1]
    total = jnp.zeros((rows, ROWS), F32)
    for j in range(width // ROWS):
        total += tokens[j // per, :, (j % per) * ROWS : (j % per + 1) * ROWS].astype(F32)
    mean = jnp.sum(total, axis=-1, keepdims=True) / width
    square = jnp.zeros((rows, ROWS), F32)
    for j in range(width // ROWS):
        part = tokens[j // per, :, (j % per) * ROWS : (j % per + 1) * ROWS].astype(F32) - mean
        square += part * part
    scale = lax.rsqrt(jnp.sum(square, axis=-1, keepdims=True) / width + EPSILON)
    for j in range(width // ROWS):
        place = places[j]
        at = pl.multiple_of((place % per) * ROWS, ROWS)
        part = tokens[place // per, :, pl.ds(at, ROWS)].astype(F32) - mean
        full_at = pl.multiple_of(table[j] * ROWS, ROWS)
        out[:, j * ROWS : (j + 1) * ROWS] = (part * scale * gain[:, pl.ds(full_at, ROWS)]).astype(BF)


def pick_kernel(plan, kept, moved, out):
    rows = kept.shape[0] // 4
    for k in range(8):
        number = plan[k]
        at = pl.multiple_of((number // 2 % 2 * 2 + number // 4) * rows, rows)
        even = kept[pl.ds(at, rows), :].astype(F32)
        odd = moved[pl.ds(at, rows), :].astype(F32)
        out[k * rows : (k + 1) * rows, :] = jnp.where(number % 2 == 0, even, odd).astype(BF)


def reorder_kernel(table, values, keep, out):
    for j in range(values.shape[1] // ROWS):
        at = pl.multiple_of(table[j] * ROWS, ROWS)
        part = values[:, pl.ds(at, ROWS)].astype(F32)
        out[:, j * ROWS : (j + 1) * ROWS] = jnp.where(keep[...] > 0, part, 0.0).astype(BF)


def dot_nt(left, right):
    return lax.dot_general(left, right, (((1,), (1,)), ((), ())), preferred_element_type=F32)


def dot_tn(left, right):
    return lax.dot_general(left, right, (((0,), (0,)), ((), ())), preferred_element_type=F32)


def head_norm(values):
    centred = values - jnp.mean(values, axis=-1, keepdims=True)
    scale = lax.rsqrt(jnp.mean(centred * centred, axis=-1, keepdims=True) + EPSILON)
    return centred * scale, scale


def block_mask(valid_keys, block_len):
    rows = valid_keys.shape[1]
    row_block = lax.broadcasted_iota(jnp.int32, (rows, rows), 0) // block_len
    col_block = lax.broadcasted_iota(jnp.int32, (rows, rows), 1) // block_len
    return (row_block == col_block) & (valid_keys > 0)


def softmax(queries, keys, mask, size):
    scores = dot_nt(queries, keys) / math.sqrt(size)
    scores = jnp.where(mask, scores, -1e30)
    expo = jnp.exp(scores - jnp.max(scores, axis=-1, keepdims=True))
    return expo / jnp.sum(expo, axis=-1, keepdims=True)


def project_kernel_over(bounds, carry):
    def kernel(*refs):
        sums = refs[0] if carry else None
        normed, weights, out = refs[carry], refs[carry + 1 : -1], refs[-1]
        step = 3 * ROWS
        for at in range(0, out.shape[1], step):
            total = sums[:, at : at + step] if carry else jnp.zeros((out.shape[0], step), F32)
            for (a, b), weight in zip(bounds, weights):
                total += jnp.dot(
                    normed[:, a:b], weight[:, at : at + step], preferred_element_type=F32
                )
            out[:, at : at + step] = total

    return kernel


def make_attend_kernel(block_len, size):
    def kernel(projected, gains, valid_keys, attended):
        mask = block_mask(valid_keys[...], block_len)
        for head in range(projected.shape[1] // (3 * size)):
            at = head * 3 * size
            q_hat, _ = head_norm(projected[:, at : at + size])
            k_hat, _ = head_norm(projected[:, at + size : at + 2 * size])
            queries = (q_hat * gains[0:1, :]).astype(BF)
            keys = (k_hat * gains[1:2, :]).astype(BF)
            values = projected[:, at + 2 * size : at + 3 * size].astype(BF)
            attend = softmax(queries, keys, mask, size).astype(BF)
            attended[:, head * size : (head + 1) * size] = jnp.dot(
                attend, values, preferred_element_type=F32
            ).astype(BF)

    return kernel


def make_attend_back_kernel(block_len, size):
    def norm_back(grad, hat, scale, gain):
        inner = grad * gain
        middle = jnp.mean(inner, axis=-1, keepdims=True)
        slope = jnp.mean(inner * hat, axis=-1, keepdims=True)
        return scale * (inner - middle - hat * slope)

    def kernel(projected, gains, valid_keys, grad_attended, after, grad_projected, grad_gains):
        mask = block_mask(valid_keys[...], block_len)
        gain_q, gain_k = gains[0:1, :], gains[1:2, :]
        sum_q = jnp.zeros((1, size), F32)
        sum_k = jnp.zeros((1, size), F32)
        for head in range(projected.shape[1] // (3 * size)):
            at = head * 3 * size
            q_hat, q_scale = head_norm(projected[:, at : at + size])
            k_hat, k_scale = head_norm(projected[:, at + size : at + 2 * size])
            queries = (q_hat * gain_q).astype(BF)
            keys = (k_hat * gain_k).astype(BF)
            values = projected[:, at + 2 * size : at + 3 * size].astype(BF)
            soft = softmax(queries, keys, mask, size)
            grad_out = grad_attended[:, head * size : (head + 1) * size]
            grad_values = dot_tn(soft.astype(BF), grad_out).astype(BF)
            grad_attend = dot_nt(grad_out, values).astype(BF).astype(F32)
            inner = jnp.sum(grad_attend * soft, axis=-1, keepdims=True)
            grad_scores = soft * (grad_attend - inner) / math.sqrt(size)
            grad_scores = jnp.where(mask, grad_scores, 0.0).astype(BF)
            grad_q = jnp.dot(grad_scores, keys, preferred_element_type=F32).astype(BF).astype(F32)
            grad_k = dot_tn(grad_scores, queries).astype(BF).astype(F32)
            sum_q += jnp.sum(grad_q * q_hat, axis=0, keepdims=True)
            sum_k += jnp.sum(grad_k * k_hat, axis=0, keepdims=True)
            grad_projected[:, at : at + size] = norm_back(grad_q, q_hat, q_scale, gain_q).astype(BF)
            grad_projected[:, at + size : at + 2 * size] = norm_back(
                grad_k, k_hat, k_scale, gain_k
            ).astype(BF)
            grad_projected[:, at + 2 * size : at + 3 * size] = grad_values
        grad_gains[0:1, :] = sum_q
        grad_gains[1:2, :] = sum_k

    return kernel


def branch_kernel(table, attended, *refs):
    weights, branch = refs[:-1], refs[-1]
    per = branch.shape[2] // ROWS
    j = 0
    for weight in weights:
        step = 2 * ROWS
        for a in range(0, weight.shape[0], step):
            product = dot_nt(attended[...], weight[a : a + step, :]).astype(BF)
            for k in range(2):
                block = table[j + k]
                at = pl.multiple_of((block % per) * ROWS, ROWS)
                branch[block // per, :, pl.ds(at, ROWS)] = product[:, k * ROWS : (k + 1) * ROWS]
            j += 2


def out_back_kernel(cot, *refs):
    weights, out = refs[:-1], refs[-1]
    total = jnp.zeros(out.shape, F32)
    at = 0
    for weight in weights:
        rows = weight.shape[0]
        total += jnp.dot(cot[:, at : at + rows], weight[...], preferred_element_type=F32)
        at += rows
    out[...] = total.astype(BF)


def gain_kernel(table, grad_projected, normed, *refs):
    weights, out = refs[:-2], refs[-1]
    j = 0
    for weight in weights:
        blocks = weight.shape[0] // ROWS
        grad = dot_nt(grad_projected[...], weight[...]).astype(BF).astype(F32)
        here = normed[:, j * ROWS : (j + blocks) * ROWS].astype(F32)
        sums = jnp.sum(grad * here, axis=0, keepdims=True)
        for k in range(blocks):
            out[pl.ds(table[j + k], 1), :] = sums[:, k * ROWS : (k + 1) * ROWS]
        j += blocks


def call(kernel, shapes, tables, *arrays, flops=0, after=()):
    smem = pl.BlockSpec(memory_space=pltpu.SMEM)
    vmem = pl.BlockSpec(memory_space=pltpu.VMEM)
    several = isinstance(shapes, tuple)
    moved = sum(a.size * a.dtype.itemsize for a in arrays)
    return pl.pallas_call(
        kernel,
        out_shape=shapes,
        in_specs=[smem] * len(tables)
        + [vmem] * len(arrays)
        + [pl.BlockSpec(memory_space=pl.ANY)] * len(after),
        out_specs=(vmem,) * len(shapes) if several else vmem,
        compiler_params=pltpu.CompilerParams(vmem_limit_bytes=28 * 1024 * 1024),
        cost_estimate=pl.CostEstimate(flops=flops, bytes_accessed=moved, transcendentals=0),
    )(*tables, *arrays, *after)


def shape(dims, dtype):
    return jax.ShapeDtypeStruct(dims, dtype)


def per_device(
    packed,
    counts,
    dest_plan,
    source_plan,
    slot_counts,
    cotangent,
    qkv_weight,
    out_weight,
    ln_gain,
    qk_gains,
):
    image_total = counts.shape[1]
    half_images = image_total // 2
    far_gap = N_DP // 2 - half_images
    block_len, width = cotangent.shape[1], cotangent.shape[2]
    rows = image_total * block_len
    heads, size = out_weight.shape[1], out_weight.shape[2]
    share = width // N_SHARD
    me = lax.axis_index("shard")

    qkv_table = absolute_blocks(QKV_ORDER)
    out_table = absolute_blocks(OUT_ORDER)
    packed_share = lax.dynamic_slice_in_dim(packed, me * share, share, 1)
    image_counts = counts[0]
    offsets = jnp.cumsum(image_counts) - image_counts
    positions = jnp.arange(block_len, dtype=jnp.int32)
    offset_ids = jnp.arange(image_total, dtype=jnp.int32)
    chosen = dest_plan[0][None, :] == offset_ids[:, None]
    starts = jnp.sum(jnp.where(chosen, offsets[None, :], 0), axis=1)
    lengths = jnp.sum(jnp.where(chosen, image_counts[None, :], 0), axis=1)
    row_index = jnp.clip(starts[:, None] + positions[None, :], 0, packed.shape[0] - 1)
    keep_rows = (positions[None, :] < lengths[:, None])[..., None]
    outgoing = jnp.where(
        keep_rows, jnp.take(packed_share, row_index, axis=0), jnp.zeros((), BF)
    )
    outgoing = outgoing.reshape(rows, share)
    quarter, eighth = rows // 4, rows // 8
    weight = qkv_weight.reshape(ROWS, heads * 3 * size)
    far_images = dp_rotate(outgoing[rows // 2 :], half_images + far_gap)
    z_ahead, z_behind = z_step(weight, -1), z_step(weight, 1)
    send, keep = combine(
        (
            (((0, quarter, 2 * quarter),), ((1, quarter, 2 * quarter),)),
            (((0, 0, quarter),), ((1, 0, quarter),)),
        ),
        outgoing,
        far_images,
    )
    moved = dp_rotate(send, 2)
    y_weight = copied(weight, (moved,))
    y_ahead, y_behind = y_step(y_weight, -1), y_step(y_weight, 1)
    send, keep = combine(
        tuple(
            tuple(((i, a + low, a + low + eighth),) for i in (0, 1) for a in (0, quarter))
            for low in (eighth, 0)
        ),
        keep,
        moved,
        after=(z_ahead, z_behind),
    )
    moved = dp_rotate(send, 1)
    own_share = call(
        pick_kernel, shape((rows, share), BF), (source_plan[0],), keep, moved
    )
    block_share = own_share.reshape(image_total, block_len, share)
    next_share = shard_shift(own_share, dl=1)

    first, up, near = gather_first(weight, z_ahead, z_behind, y_ahead, y_behind)
    from_ahead, from_behind = y_step(up, -1), y_step(near, 1)
    other_first = swap(first)
    z_across = z_step(z_ahead, -1)

    (pair,) = combine(((((0, 0, rows),), ((1, 0, rows),)),), own_share, next_share, after=(near,))
    groups = [[x * NL + low for x in range(NX)] for low in range(NL)]
    tokens = lax.all_gather(pair, "shard", axis=0, tiled=True, axis_index_groups=groups)
    tokens = tokens.reshape(N_SHARD, rows, share)
    out_start = copied(out_weight.reshape(ROWS, heads * size), (pair,))
    out_ahead, out_behind = z_step(out_start, -1), z_step(out_start, 1)
    out_across = z_step(out_ahead, -1)

    valid_rows = positions[None, :] < slot_counts[0][:, None]
    valid_keys = valid_rows.astype(F32).reshape(1, rows)
    valid_column = valid_rows.astype(F32).reshape(rows, 1)

    cot = call(
        reorder_kernel,
        shape((rows, width), BF),
        (out_table,),
        cotangent.reshape(rows, width),
        valid_column,
    )

    second, up, down = gather_second(
        from_ahead, from_behind, z_across, (other_first, out_across, out_behind, cot)
    )
    third, fourth = y_step(up, -1), y_step(down, 1)
    other_second = swap(second)
    fifth = y_step(fourth[:ROWS], 1)
    out_mine, out_other, out_column, out_near = gather_out(
        out_start, out_ahead, out_behind, out_across, (third, fourth, other_second)
    )

    per = share // ROWS
    places = ((qkv_table // per) ^ (me % NL)) * per + qkv_table % per
    normed = call(
        norm_kernel,
        shape((rows, width), BF),
        (places, qkv_table),
        tokens,
        ln_gain.reshape(1, width),
        after=(out_column,),
    )
    sizes = [len(part) * ROWS for part in QKV_PARTS] * 2
    bounds = np.cumsum([0] + sizes)
    bounds = list(zip(bounds[:-1].tolist(), bounds[1:].tolist()))
    early, late = (0, 1, 5, 6), (2, 3, 4, 7, 8, 9)
    projected_shape = shape((rows, heads * 3 * size), F32)
    projected = call(
        project_kernel_over([bounds[i] for i in early], 0),
        projected_shape,
        (),
        normed,
        first,
        second,
        other_first,
        other_second,
        flops=2 * rows * width * heads * 2 * size,
    )
    other_third, other_fourth = swap(third), swap(fourth)
    other_fifth = swap(copied(fifth, (projected,)))
    parts = [first, second, third, fourth, fifth]
    parts += [other_first, other_second, other_third, other_fourth, other_fifth]
    projected = call(
        project_kernel_over([bounds[i] for i in late], 1),
        projected_shape,
        (),
        projected,
        normed,
        *[parts[i] for i in late],
        flops=2 * rows * width * heads * size,
    )
    attended = call(
        make_attend_kernel(block_len, size),
        shape((rows, heads * size), BF),
        (),
        projected,
        qk_gains,
        valid_keys,
    )

    final_o, out_sums, out_hops, out_moved, out_last = scatter_out(cot, attended, out_near)

    out_parts = (*out_mine, *out_other)
    branch = call(
        branch_kernel,
        shape((N_SHARD, rows, share), BF),
        (out_table,),
        attended,
        *out_parts,
        flops=2 * rows * width * heads * size,
    )
    summed = lax.psum_scatter(branch, "shard", scatter_dimension=0, tiled=False)
    summed = summed.reshape(image_total, block_len, share).astype(F32)
    block_out = jnp.where(valid_rows[..., None], block_share.astype(F32) + summed, 0.0).astype(BF)

    grad_attended = call(
        out_back_kernel,
        shape((rows, heads * size), BF),
        (),
        cot,
        *out_parts,
        flops=2 * rows * width * heads * size,
    )
    grad_projected, grad_gains = call(
        make_attend_back_kernel(block_len, size),
        (shape((rows, heads * 3 * size), BF), shape((2, size), F32)),
        (),
        projected,
        qk_gains,
        valid_keys,
        grad_attended,
        after=out_sums,
    )

    def gain_sums(midway):
        grad_gain = call(
            gain_kernel,
            shape((N_DP, ROWS), F32),
            (qkv_table,),
            grad_projected,
            normed,
            *parts,
            after=(midway,),
            flops=2 * rows * width * heads * 3 * size,
        )
        grad_gain = grad_gain / ln_gain.reshape(N_DP, ROWS)
        return sum_everywhere(jnp.concatenate([grad_gain, grad_gains], axis=0))

    final_q, totals = scatter_qkv(
        normed, grad_projected, (*out_hops, branch), out_moved, out_last, gain_sums
    )
    return (
        block_out,
        final_q.reshape(ROWS, heads, 3 * size),
        final_o.reshape(ROWS, heads, size),
        totals[:N_DP].reshape(width),
        totals[N_DP:],
    )


def solution(mesh):
    return jax.shard_map(
        per_device,
        mesh=mesh,
        in_specs=(
            P("dp", None),
            P("dp", None),
            P("dp", None),
            P("dp", None),
            P("dp", None),
            P("dp", None, None),
            P("dp", "shard", None),
            P("dp", "shard", None),
            P(),
            P(),
        ),
        out_specs=(
            P("dp", None, "shard"),
            P("dp", "shard", None),
            P("dp", "shard", None),
            P(),
            P(),
        ),
        check_vma=False,
    )
```

```python
import math

import jax
import jax.numpy as jnp
import numpy as np
from jax import lax
from jax.experimental import pallas as pl
from jax.experimental.pallas import tpu as pltpu
from jax.sharding import PartitionSpec as P

EPSILON = 1e-06
BF = jnp.bfloat16
F32 = jnp.float32

NZ, NY, NC = 4, 4, 2
NX, NL = 4, 2
N_DP = NZ * NY * NC
N_SHARD = NX * NL
ROWS = 128

QKV_PARTS = (
    ((0, 0), (0, 1), (0, 3), (1, 0), (3, 0)),
    ((1, 1), (1, 3), (2, 0), (3, 1), (3, 3), (0, 2)),
    ((1, 2), (2, 1)),
    ((3, 2), (2, 3)),
    ((2, 2),),
)
QKV_ORDER = [(c, y, z) for c in range(NC) for part in QKV_PARTS for y, z in part]
EARLY = 10 * ROWS
OUT_ORDER = [(c, y, z) for c in range(NC) for z in (0, 1, 3, 2) for y in (0, 1, 3, 2)]


def dp_shift(value, dz=0, dy=0, dc=0):
    pairs = []
    for z in range(NZ):
        for y in range(NY):
            for c in range(NC):
                target = ((z + dz) % NZ) * NY * NC + ((y + dy) % NY) * NC + (c + dc) % NC
                pairs.append((z * NY * NC + y * NC + c, target))
    return lax.ppermute(value, "dp", pairs)


def dp_rotate(value, steps):
    return lax.ppermute(value, "dp", [(s, (s + steps) % N_DP) for s in range(N_DP)])


def shard_shift(value, dx=0, dl=0):
    pairs = []
    for x in range(NX):
        for low in range(NL):
            pairs.append((x * NL + low, ((x + dx) % NX) * NL + (low + dl) % NL))
    return lax.ppermute(value, "shard", pairs)


def absolute_blocks(order):
    me = lax.axis_index("dp")
    z, y, c = me // (NY * NC), (me // NC) % NY, me % NC
    table = np.asarray(order, dtype=np.int32)
    return (
        ((z + table[:, 2]) % NZ) * (NY * NC) + ((y + table[:, 1]) % NY) * NC + (c + table[:, 0]) % NC
    ).astype(jnp.int32)


def y_step(value, steps):
    return dp_shift(value, dy=steps)


def z_step(value, steps):
    return dp_shift(value, dz=steps)


def swap(value):
    return dp_shift(value, dc=1)


def combine(plans, *arrays, after=(), dtype=BF):
    count = len(arrays)
    width = arrays[0].shape[1]

    def kernel(*refs):
        for plan, out in zip(plans, refs[count + len(after) :]):
            at = 0
            for terms in plan:
                rows = terms[0][2] - terms[0][1]
                parts = [refs[i][a:b, :] for i, a, b in terms]
                if len(parts) > 1:
                    parts = [part.astype(F32) for part in parts]
                total = parts[0]
                for part in parts[1:]:
                    total = total + part
                out[at : at + rows, :] = total.astype(dtype)
                at += rows

    sizes = [sum(terms[0][2] - terms[0][1] for terms in plan) for plan in plans]
    return call(kernel, tuple(shape((size, width), dtype) for size in sizes), (), *arrays, after=after)


def copied(value, after):
    (value,) = combine(((((0, 0, value.shape[0]),),),), value, after=after, dtype=value.dtype)
    return value


def gather_first(weight, z_ahead, z_behind, y_ahead, y_behind, after):
    one = ROWS
    return combine(
        (
            tuple(((i, 0, one),) for i in range(5)),
            (((1, 0, one),), ((2, 0, one),), ((3, 0, one),)),
            (((1, 0, one),), ((2, 0, one),)),
        ),
        weight,
        z_ahead,
        z_behind,
        y_ahead,
        y_behind,
        after=after,
    )


def gather_second(from_ahead, from_behind, z_across, after):
    one = ROWS
    return combine(
        (
            (((0, 0, 3 * one),), ((1, 0, 2 * one),), ((2, 0, one),)),
            (((2, 0, one),), ((0, 0, one),)),
            (((2, 0, one),), ((1, one, 2 * one),)),
        ),
        from_ahead,
        from_behind,
        z_across,
        after=after,
    )


def gather_out(weight, y_ahead, y_behind, y_across, after):
    one = ROWS
    (column,) = combine(
        (tuple(((i, 0, one),) for i in range(4)),),
        weight,
        y_ahead,
        y_behind,
        y_across,
        after=after,
    )
    z_ahead, z_behind = z_step(column, -1), z_step(column, 1)
    first, up, down = combine(
        (
            (((0, 0, 4 * one),), ((1, 0, 4 * one),), ((2, 0, 4 * one),)),
            (((1, 0, 2 * one),),),
            (((2, 2 * one, 4 * one),),),
        ),
        column,
        z_ahead,
        z_behind,
    )
    (second,) = combine(
        ((((0, 0, 2 * one),), ((1, 0, 2 * one),)),), z_step(up, -1), z_step(down, 1)
    )
    return (first, second), (swap(first), swap(second)), (first,)


def core_sums(left, right, base, received, bounds, after=()):
    def kernel(left_ref, right_ref, received_ref, *refs):
        outs = refs[len(after) :]
        for (a, b), out in zip(bounds, outs):
            product = dot_tn(left_ref[:, base + a : base + b], right_ref[...])
            out[...] = (product + received_ref[a:b, :].astype(F32)).astype(BF)

    shapes = tuple(shape((b - a, right.shape[1]), BF) for a, b in bounds)
    return call(kernel, shapes, (), left, right, received, after=after)


def part_product(left, right, base, rows, after=()):
    def kernel(*refs):
        left_ref, right_ref, out = refs[0], refs[1], refs[-1]
        step = 2 * ROWS
        for a in range(0, rows, step):
            out[a : a + step, :] = dot_tn(
                left_ref[:, base + a : base + a + step], right_ref[...]
            ).astype(BF)

    return call(kernel, shape((rows, right.shape[1]), BF), (), left, right, after=after)


def scatter_qkv(normed, grad, after_first, after_early, after_sums, after_last, meanwhile):
    one = ROWS
    half = normed.shape[1] // 2
    late = half - EARLY
    product = part_product(normed, grad, half + EARLY, late, after_first)
    late_other = swap(product)
    product = part_product(normed, grad, half, EARLY, (product, *after_early))
    early_other = swap(product)
    own_gains, gains = meanwhile(product)
    rows = lambda *at: [(a * one, b * one) for a, b in at]
    s02, s12_21, s32_23, s22 = core_sums(
        normed, grad, EARLY, late_other, rows((0, 1), (1, 3), (3, 5), (5, 6)), (own_gains, after_sums[0])
    )
    hop = y_step(s22, 1)
    s00, s01_03, s10, s30, s11_13, s20, s31_33 = core_sums(
        normed,
        grad,
        0,
        early_other,
        rows((0, 1), (1, 3), (3, 4), (4, 5), (5, 7), (7, 8), (8, 10)),
        after_sums[1:],
    )
    (plus,) = combine(
        ((((0, 0, one), (1, 0, one)), ((0, one, 2 * one),)),), s12_21, hop
    )
    below, above = y_step(plus, 1), y_step(s32_23, -1)
    plus, minus, z_across = combine(
        (
            (((0, 0, one), (3, one, 2 * one)), ((0, one, 2 * one),)),
            (
                ((1, 0, one),),
                ((1, one, 2 * one), (4, one, 2 * one)),
                ((2, 0, one),),
            ),
            (((5, 0, one), (3, 0, one), (4, 0, one)),),
        ),
        s11_13,
        s31_33,
        s20,
        below,
        above,
        s02,
        after=(gains,),
    )
    gains = sum_last(gains, (plus,))
    z_hop = z_step(z_across, 1)
    below, above = y_step(plus, 1), y_step(minus, -1)
    last_below = y_step(s10, 1)
    minus, z_ahead, z_behind = combine(
        (
            (((0, 0, one), (1, 2 * one, 3 * one)),),
            (((2, 0, one), (3, 0, one), (1, 0, one), (4, 0, one)),),
            (((2, one, 2 * one), (3, one, 2 * one), (1, one, 2 * one)),),
        ),
        s30,
        above,
        s01_03,
        below,
        z_hop,
        after=(gains, *after_last),
    )
    last_above = y_step(minus, -1)
    from_below, from_above = z_step(z_ahead, 1), z_step(z_behind, -1)
    total = sum(
        part.astype(F32) for part in (s00, last_below, last_above, from_below, from_above)
    )
    return total, gains


def scatter_out(cot, attended, after):
    one = ROWS
    half = cot.shape[1] // 2
    product = part_product(cot, attended, half, half, after)
    other = swap(product)
    own, ahead, behind, across_up, across_down = core_sums(
        cot,
        attended,
        0,
        other,
        [(a * one, b * one) for a, b in ((0, 4), (4, 8), (8, 12), (12, 14), (14, 16))],
    )
    up, down = z_step(across_up, 1), z_step(across_down, -1)
    plus, minus = combine(
        (
            (((0, 0, 2 * one), (2, 0, 2 * one)), ((0, 2 * one, 4 * one),)),
            (((1, 0, 2 * one),), ((1, 2 * one, 4 * one), (3, 0, 2 * one))),
        ),
        ahead,
        behind,
        up,
        down,
    )
    below, above = z_step(plus, 1), z_step(minus, -1)
    parts = combine(
        tuple(
            (tuple((i, k * one, (k + 1) * one) for i in range(3)),) for k in range(4)
        ),
        own,
        below,
        above,
    )
    hops = (y_step(parts[1], 1), y_step(parts[2], -1), y_step(parts[3], 2))
    total = sum(hop.astype(F32) for hop in (parts[0], *hops))
    return total, own, (up, down), (plus, below, above), hops


def dp_exchange(value, bit):
    return lax.ppermute(value, "dp", [(s, s ^ bit) for s in range(N_DP)])


def shard_exchange(value, bit):
    return lax.ppermute(value, "shard", [(s, s ^ bit) for s in range(N_SHARD)])


def sum_first(value):
    value = value + dp_exchange(value, 1)
    for bit in (2, 4, 1):
        value = value + shard_exchange(value, bit)
    return value


def sum_last(value, after):
    value = copied(value, after)
    for bit in (8, 16, 2, 4):
        value = value + dp_exchange(value, bit)
    return value


def norm_kernel(places, table, tokens, gain, after, out):
    width = tokens.shape[0] * tokens.shape[2]
    per = tokens.shape[2] // ROWS
    rows = tokens.shape[1]
    total = jnp.zeros((rows, ROWS), F32)
    for j in range(width // ROWS):
        total += tokens[j // per, :, (j % per) * ROWS : (j % per + 1) * ROWS].astype(F32)
    mean = jnp.sum(total, axis=-1, keepdims=True) / width
    square = jnp.zeros((rows, ROWS), F32)
    for j in range(width // ROWS):
        part = tokens[j // per, :, (j % per) * ROWS : (j % per + 1) * ROWS].astype(F32) - mean
        square += part * part
    scale = lax.rsqrt(jnp.sum(square, axis=-1, keepdims=True) / width + EPSILON)
    for j in range(width // ROWS):
        place = places[j]
        at = pl.multiple_of((place % per) * ROWS, ROWS)
        part = tokens[place // per, :, pl.ds(at, ROWS)].astype(F32) - mean
        full_at = pl.multiple_of(table[j] * ROWS, ROWS)
        out[:, j * ROWS : (j + 1) * ROWS] = (part * scale * gain[:, pl.ds(full_at, ROWS)]).astype(BF)


def pick_kernel(plan, kept, moved, out):
    rows = kept.shape[0] // 4
    for k in range(8):
        number = plan[k]
        at = pl.multiple_of(number % 4 * rows, rows)
        near = kept[pl.ds(at, rows), :].astype(F32)
        far = moved[pl.ds(at, rows), :].astype(F32)
        out[k * rows : (k + 1) * rows, :] = jnp.where(number < 4, near, far).astype(BF)


def reorder_kernel(table, values, keep, out):
    for j in range(values.shape[1] // ROWS):
        at = pl.multiple_of(table[j] * ROWS, ROWS)
        part = values[:, pl.ds(at, ROWS)].astype(F32)
        out[:, j * ROWS : (j + 1) * ROWS] = jnp.where(keep[...] > 0, part, 0.0).astype(BF)


def dot_nt(left, right):
    return lax.dot_general(left, right, (((1,), (1,)), ((), ())), preferred_element_type=F32)


def dot_tn(left, right):
    return lax.dot_general(left, right, (((0,), (0,)), ((), ())), preferred_element_type=F32)


def head_norm(values):
    centred = values - jnp.mean(values, axis=-1, keepdims=True)
    scale = lax.rsqrt(jnp.mean(centred * centred, axis=-1, keepdims=True) + EPSILON)
    return centred * scale, scale


def block_mask(valid_keys, block_len):
    rows = valid_keys.shape[1]
    row_block = lax.broadcasted_iota(jnp.int32, (rows, rows), 0) // block_len
    col_block = lax.broadcasted_iota(jnp.int32, (rows, rows), 1) // block_len
    return (row_block == col_block) & (valid_keys > 0)


def softmax(queries, keys, mask, size):
    scores = dot_nt(queries, keys) / math.sqrt(size)
    scores = jnp.where(mask, scores, -1e30)
    expo = jnp.exp(scores - jnp.max(scores, axis=-1, keepdims=True))
    return expo / jnp.sum(expo, axis=-1, keepdims=True)


def project_kernel_over(bounds, carry):
    def kernel(*refs):
        sums = refs[0] if carry else None
        normed, weights, out = refs[carry], refs[carry + 1 : -1], refs[-1]
        step = 3 * ROWS
        for at in range(0, out.shape[1], step):
            total = sums[:, at : at + step] if carry else jnp.zeros((out.shape[0], step), F32)
            for (a, b), weight in zip(bounds, weights):
                total += jnp.dot(
                    normed[:, a:b], weight[:, at : at + step], preferred_element_type=F32
                )
            out[:, at : at + step] = total

    return kernel


def make_attend_kernel(block_len, size):
    def kernel(projected, gains, valid_keys, attended):
        mask = block_mask(valid_keys[...], block_len)
        for head in range(projected.shape[1] // (3 * size)):
            at = head * 3 * size
            q_hat, _ = head_norm(projected[:, at : at + size])
            k_hat, _ = head_norm(projected[:, at + size : at + 2 * size])
            queries = (q_hat * gains[0:1, :]).astype(BF)
            keys = (k_hat * gains[1:2, :]).astype(BF)
            values = projected[:, at + 2 * size : at + 3 * size].astype(BF)
            attend = softmax(queries, keys, mask, size).astype(BF)
            attended[:, head * size : (head + 1) * size] = jnp.dot(
                attend, values, preferred_element_type=F32
            ).astype(BF)

    return kernel


def make_attend_back_kernel(block_len, size):
    def norm_back(grad, hat, scale, gain):
        inner = grad * gain
        middle = jnp.mean(inner, axis=-1, keepdims=True)
        slope = jnp.mean(inner * hat, axis=-1, keepdims=True)
        return scale * (inner - middle - hat * slope)

    def kernel(projected, gains, valid_keys, grad_attended, after, grad_projected, grad_gains):
        mask = block_mask(valid_keys[...], block_len)
        gain_q, gain_k = gains[0:1, :], gains[1:2, :]
        sum_q = jnp.zeros((1, size), F32)
        sum_k = jnp.zeros((1, size), F32)
        for head in range(projected.shape[1] // (3 * size)):
            at = head * 3 * size
            q_hat, q_scale = head_norm(projected[:, at : at + size])
            k_hat, k_scale = head_norm(projected[:, at + size : at + 2 * size])
            queries = (q_hat * gain_q).astype(BF)
            keys = (k_hat * gain_k).astype(BF)
            values = projected[:, at + 2 * size : at + 3 * size].astype(BF)
            soft = softmax(queries, keys, mask, size)
            grad_out = grad_attended[:, head * size : (head + 1) * size]
            grad_values = dot_tn(soft.astype(BF), grad_out).astype(BF)
            grad_attend = dot_nt(grad_out, values).astype(BF).astype(F32)
            inner = jnp.sum(grad_attend * soft, axis=-1, keepdims=True)
            grad_scores = soft * (grad_attend - inner) / math.sqrt(size)
            grad_scores = jnp.where(mask, grad_scores, 0.0).astype(BF)
            grad_q = jnp.dot(grad_scores, keys, preferred_element_type=F32).astype(BF).astype(F32)
            grad_k = dot_tn(grad_scores, queries).astype(BF).astype(F32)
            sum_q += jnp.sum(grad_q * q_hat, axis=0, keepdims=True)
            sum_k += jnp.sum(grad_k * k_hat, axis=0, keepdims=True)
            grad_projected[:, at : at + size] = norm_back(grad_q, q_hat, q_scale, gain_q).astype(BF)
            grad_projected[:, at + size : at + 2 * size] = norm_back(
                grad_k, k_hat, k_scale, gain_k
            ).astype(BF)
            grad_projected[:, at + 2 * size : at + 3 * size] = grad_values
        grad_gains[0:1, :] = sum_q
        grad_gains[1:2, :] = sum_k

    return kernel


def branch_kernel(table, attended, *refs):
    weights, branch = refs[:-2], refs[-1]
    per = branch.shape[2] // ROWS
    j = 0
    for weight in weights:
        step = 2 * ROWS
        for a in range(0, weight.shape[0], step):
            product = dot_nt(attended[...], weight[a : a + step, :]).astype(BF)
            for k in range(2):
                block = table[j + k]
                at = pl.multiple_of((block % per) * ROWS, ROWS)
                branch[block // per, :, pl.ds(at, ROWS)] = product[:, k * ROWS : (k + 1) * ROWS]
            j += 2


def out_back_kernel(cot, *refs):
    weights, out = refs[:-1], refs[-1]
    total = jnp.zeros(out.shape, F32)
    at = 0
    for weight in weights:
        rows = weight.shape[0]
        total += jnp.dot(cot[:, at : at + rows], weight[...], preferred_element_type=F32)
        at += rows
    out[...] = total.astype(BF)


def gain_kernel(table, grad_projected, normed, *refs):
    weights, out = refs[:-2], refs[-1]
    j = 0
    for weight in weights:
        blocks = weight.shape[0] // ROWS
        grad = dot_nt(grad_projected[...], weight[...]).astype(BF).astype(F32)
        here = normed[:, j * ROWS : (j + blocks) * ROWS].astype(F32)
        sums = jnp.sum(grad * here, axis=0, keepdims=True)
        for k in range(blocks):
            out[pl.ds(table[j + k], 1), :] = sums[:, k * ROWS : (k + 1) * ROWS]
        j += blocks


def call(kernel, shapes, tables, *arrays, flops=0, after=()):
    smem = pl.BlockSpec(memory_space=pltpu.SMEM)
    vmem = pl.BlockSpec(memory_space=pltpu.VMEM)
    several = isinstance(shapes, tuple)
    moved = sum(a.size * a.dtype.itemsize for a in arrays)
    return pl.pallas_call(
        kernel,
        out_shape=shapes,
        in_specs=[smem] * len(tables)
        + [vmem] * len(arrays)
        + [pl.BlockSpec(memory_space=pl.ANY)] * len(after),
        out_specs=(vmem,) * len(shapes) if several else vmem,
        compiler_params=pltpu.CompilerParams(vmem_limit_bytes=28 * 1024 * 1024),
        cost_estimate=pl.CostEstimate(flops=flops, bytes_accessed=moved, transcendentals=0),
    )(*tables, *arrays, *after)


def shape(dims, dtype):
    return jax.ShapeDtypeStruct(dims, dtype)


def per_device(
    packed,
    counts,
    dest_plan,
    source_plan,
    slot_counts,
    cotangent,
    qkv_weight,
    out_weight,
    ln_gain,
    qk_gains,
):
    image_total = counts.shape[1]
    half_images = image_total // 2
    far_gap = N_DP // 2 - half_images
    block_len, width = cotangent.shape[1], cotangent.shape[2]
    rows = image_total * block_len
    heads, size = out_weight.shape[1], out_weight.shape[2]
    share = width // N_SHARD
    me = lax.axis_index("shard")

    qkv_table = absolute_blocks(QKV_ORDER)
    out_table = absolute_blocks(OUT_ORDER)
    packed_share = lax.dynamic_slice_in_dim(packed, me * share, share, 1)
    image_counts = counts[0]
    offsets = jnp.cumsum(image_counts) - image_counts
    positions = jnp.arange(block_len, dtype=jnp.int32)
    offset_ids = jnp.arange(image_total, dtype=jnp.int32)
    chosen = dest_plan[0][None, :] == offset_ids[:, None]
    starts = jnp.sum(jnp.where(chosen, offsets[None, :], 0), axis=1)
    lengths = jnp.sum(jnp.where(chosen, image_counts[None, :], 0), axis=1)
    row_index = jnp.clip(starts[:, None] + positions[None, :], 0, packed.shape[0] - 1)
    keep_rows = (positions[None, :] < lengths[:, None])[..., None]
    outgoing = jnp.where(
        keep_rows, jnp.take(packed_share, row_index, axis=0), jnp.zeros((), BF)
    )
    outgoing = outgoing.reshape(rows, share)
    weight = qkv_weight.reshape(ROWS, heads * 3 * size)
    z_ahead, z_behind = z_step(weight, -1), z_step(weight, 1)
    y_ahead, y_behind = y_step(weight, -1), y_step(weight, 1)

    def pieces(chosen):
        return tuple(((i, k * block_len, (k + 1) * block_len),) for i, k in chosen)

    send, keep = combine(
        (pieces([(0, k) for k in (1, 3, 5, 7)]), pieces([(0, k) for k in (0, 2, 4, 6)])), outgoing
    )
    moved = dp_rotate(send, 1)
    odd, even = [(i, k) for i in (0, 1) for k in (1, 3)], [(i, k) for i in (0, 1) for k in (0, 2)]
    send, keep = combine(
        (pieces(odd), pieces(even)),
        keep,
        moved,
        after=(y_ahead, y_behind, z_ahead, z_behind),
    )
    moved = dp_rotate(send, 2)
    out_start = copied(out_weight.reshape(ROWS, heads * size), (y_ahead, y_behind))
    out_ahead, out_behind = y_step(out_start, -1), y_step(out_start, 1)
    out_across = y_step(out_start, 2)

    first, up, near = gather_first(
        weight, z_ahead, z_behind, y_ahead, y_behind, (out_ahead, out_behind, out_across)
    )
    from_ahead, from_behind = y_step(up, -1), y_step(near, 1)
    other_first = swap(first)
    z_across = z_step(z_ahead, -1)

    send, keep = combine((pieces(odd), pieces(even)), keep, moved)
    moved = dp_rotate(send, half_images + far_gap)
    own_share = call(
        pick_kernel, shape((rows, share), BF), (source_plan[0],), keep, moved
    )
    block_share = own_share.reshape(image_total, block_len, share)
    next_share = shard_shift(own_share, dl=1)
    (pair,) = combine(((((0, 0, rows),), ((1, 0, rows),)),), own_share, next_share)
    groups = [[x * NL + low for x in range(NX)] for low in range(NL)]
    tokens = lax.all_gather(pair, "shard", axis=0, tiled=True, axis_index_groups=groups)
    tokens = tokens.reshape(N_SHARD, rows, share)
    valid_rows = positions[None, :] < slot_counts[0][:, None]
    valid_keys = valid_rows.astype(F32).reshape(1, rows)
    valid_column = valid_rows.astype(F32).reshape(rows, 1)

    cot = call(
        reorder_kernel,
        shape((rows, width), BF),
        (out_table,),
        cotangent.reshape(rows, width),
        valid_column,
    )

    second, up, down = gather_second(
        from_ahead, from_behind, z_across, (other_first, cot)
    )
    third, fourth = y_step(up, -1), y_step(down, 1)
    other_second = swap(second)
    fifth = y_step(fourth[:ROWS], 1)
    out_mine, out_other, out_column = gather_out(
        out_start, out_ahead, out_behind, out_across, (first,)
    )

    per = share // ROWS
    places = ((qkv_table // per) ^ (me % NL)) * per + qkv_table % per
    normed = call(
        norm_kernel,
        shape((rows, width), BF),
        (places, qkv_table),
        tokens,
        ln_gain.reshape(1, width),
        after=out_column,
    )
    sizes = [len(part) * ROWS for part in QKV_PARTS] * 2
    bounds = np.cumsum([0] + sizes)
    bounds = list(zip(bounds[:-1].tolist(), bounds[1:].tolist()))
    early, late = (0, 1, 5, 6), (2, 3, 4, 7, 8, 9)
    projected_shape = shape((rows, heads * 3 * size), F32)
    projected = call(
        project_kernel_over([bounds[i] for i in early], 0),
        projected_shape,
        (),
        normed,
        first,
        second,
        other_first,
        other_second,
        flops=2 * rows * width * heads * 2 * size,
    )
    other_third, other_fourth = swap(third), swap(fourth)
    other_fifth = swap(copied(fifth, (projected,)))
    parts = [first, second, third, fourth, fifth]
    parts += [other_first, other_second, other_third, other_fourth, other_fifth]
    projected = call(
        project_kernel_over([bounds[i] for i in late], 1),
        projected_shape,
        (),
        projected,
        normed,
        *[parts[i] for i in late],
        flops=2 * rows * width * heads * size,
    )
    attended = call(
        make_attend_kernel(block_len, size),
        shape((rows, heads * size), BF),
        (),
        projected,
        qk_gains,
        valid_keys,
    )

    final_o, out_sums, out_hops, out_moved, out_last = scatter_out(cot, attended, ())

    out_parts = (*out_mine, *out_other)
    branch = call(
        branch_kernel,
        shape((N_SHARD, rows, share), BF),
        (out_table,),
        attended,
        *out_parts,
        after=(out_sums,),
        flops=2 * rows * width * heads * size,
    )
    summed = lax.psum_scatter(branch, "shard", scatter_dimension=0, tiled=False)
    summed = summed.reshape(image_total, block_len, share).astype(F32)
    block_out = jnp.where(valid_rows[..., None], block_share.astype(F32) + summed, 0.0).astype(BF)

    grad_attended = call(
        out_back_kernel,
        shape((rows, heads * size), BF),
        (),
        cot,
        *out_parts,
        flops=2 * rows * width * heads * size,
    )
    grad_projected, grad_gains = call(
        make_attend_back_kernel(block_len, size),
        (shape((rows, heads * 3 * size), BF), shape((2, size), F32)),
        (),
        projected,
        qk_gains,
        valid_keys,
        grad_attended,
        after=(out_sums,),
    )

    def gain_sums(midway):
        grad_gain = call(
            gain_kernel,
            shape((N_DP, ROWS), F32),
            (qkv_table,),
            grad_projected,
            normed,
            *parts,
            after=(midway,),
            flops=2 * rows * width * heads * 3 * size,
        )
        grad_gain = grad_gain / ln_gain.reshape(N_DP, ROWS)
        own_gains = jnp.concatenate([grad_gain, grad_gains], axis=0)
        return own_gains, sum_first(own_gains)

    final_q, totals = scatter_qkv(
        normed, grad_projected, (branch,), out_hops, out_moved, out_last, gain_sums
    )
    return (
        block_out,
        final_q.reshape(ROWS, heads, 3 * size),
        final_o.reshape(ROWS, heads, size),
        totals[:N_DP].reshape(width),
        totals[N_DP:],
    )


def solution(mesh):
    return jax.shard_map(
        per_device,
        mesh=mesh,
        in_specs=(
            P("dp", None),
            P("dp", None),
            P("dp", None),
            P("dp", None),
            P("dp", None),
            P("dp", None, None),
            P("dp", "shard", None),
            P("dp", "shard", None),
            P(),
            P(),
        ),
        out_specs=(
            P("dp", None, "shard"),
            P("dp", "shard", None),
            P("dp", "shard", None),
            P(),
            P(),
        ),
        check_vma=False,
    )
```

```python
import math

import jax
import jax.numpy as jnp
import numpy as np
from jax import lax
from jax.experimental import pallas as pl
from jax.experimental.pallas import tpu as pltpu
from jax.sharding import PartitionSpec as P

EPSILON = 1e-06
BF = jnp.bfloat16
F32 = jnp.float32

NZ, NY, NC = 4, 4, 2
NX, NL = 4, 2
N_DP = NZ * NY * NC
N_SHARD = NX * NL
ROWS = 128

QKV_PARTS = (
    ((0, 0), (0, 1), (0, 3), (1, 0), (3, 0)),
    ((1, 1), (1, 3), (2, 0), (3, 1), (3, 3), (0, 2)),
    ((1, 2), (2, 1)),
    ((3, 2), (2, 3)),
    ((2, 2),),
)
QKV_ORDER = [(c, y, z) for c in range(NC) for part in QKV_PARTS for y, z in part]
EARLY = 10 * ROWS
OUT_ORDER = [(c, y, z) for c in range(NC) for z in (0, 1, 3, 2) for y in (0, 1, 3, 2)]


def dp_shift(value, dz=0, dy=0, dc=0):
    pairs = []
    for z in range(NZ):
        for y in range(NY):
            for c in range(NC):
                target = ((z + dz) % NZ) * NY * NC + ((y + dy) % NY) * NC + (c + dc) % NC
                pairs.append((z * NY * NC + y * NC + c, target))
    return lax.ppermute(value, "dp", pairs)


def dp_rotate(value, steps):
    return lax.ppermute(value, "dp", [(s, (s + steps) % N_DP) for s in range(N_DP)])


def shard_shift(value, dx=0, dl=0):
    pairs = []
    for x in range(NX):
        for low in range(NL):
            pairs.append((x * NL + low, ((x + dx) % NX) * NL + (low + dl) % NL))
    return lax.ppermute(value, "shard", pairs)


def absolute_blocks(order):
    me = lax.axis_index("dp")
    z, y, c = me // (NY * NC), (me // NC) % NY, me % NC
    table = np.asarray(order, dtype=np.int32)
    return (
        ((z + table[:, 2]) % NZ) * (NY * NC) + ((y + table[:, 1]) % NY) * NC + (c + table[:, 0]) % NC
    ).astype(jnp.int32)


def y_step(value, steps):
    return dp_shift(value, dy=steps)


def z_step(value, steps):
    return dp_shift(value, dz=steps)


def swap(value):
    return dp_shift(value, dc=1)


def combine(plans, *arrays, after=(), dtype=BF):
    count = len(arrays)
    width = arrays[0].shape[1]

    def kernel(*refs):
        for plan, out in zip(plans, refs[count + len(after) :]):
            at = 0
            for terms in plan:
                rows = terms[0][2] - terms[0][1]
                parts = [refs[i][a:b, :] for i, a, b in terms]
                if len(parts) > 1:
                    parts = [part.astype(F32) for part in parts]
                total = parts[0]
                for part in parts[1:]:
                    total = total + part
                out[at : at + rows, :] = total.astype(dtype)
                at += rows

    sizes = [sum(terms[0][2] - terms[0][1] for terms in plan) for plan in plans]
    return call(kernel, tuple(shape((size, width), dtype) for size in sizes), (), *arrays, after=after)


def copied(value, after):
    (value,) = combine(((((0, 0, value.shape[0]),),),), value, after=after, dtype=value.dtype)
    return value


def gather_first(weight, z_ahead, z_behind, y_ahead, y_behind, after):
    one = ROWS
    return combine(
        (
            tuple(((i, 0, one),) for i in range(5)),
            (((1, 0, one),), ((2, 0, one),), ((3, 0, one),)),
            (((1, 0, one),), ((2, 0, one),)),
        ),
        weight,
        z_ahead,
        z_behind,
        y_ahead,
        y_behind,
        after=after,
    )


def gather_second(from_ahead, from_behind, z_across, after):
    one = ROWS
    return combine(
        (
            (((0, 0, 3 * one),), ((1, 0, 2 * one),), ((2, 0, one),)),
            (((2, 0, one),), ((0, 0, one),)),
            (((2, 0, one),), ((1, one, 2 * one),)),
        ),
        from_ahead,
        from_behind,
        z_across,
        after=after,
    )


def gather_out(weight, y_ahead, y_behind, y_across, after, after_z):
    one = ROWS
    (column,) = combine(
        (tuple(((i, 0, one),) for i in range(4)),),
        weight,
        y_ahead,
        y_behind,
        y_across,
        after=after,
    )
    z_ahead, z_behind = z_step(column, -1), z_step(column, 1)
    first, up, down = combine(
        (
            (((0, 0, 4 * one),), ((1, 0, 4 * one),), ((2, 0, 4 * one),)),
            (((1, 0, 2 * one),),),
            (((2, 2 * one, 4 * one),),),
        ),
        column,
        z_ahead,
        z_behind,
        after=after_z,
    )
    (second,) = combine(
        ((((0, 0, 2 * one),), ((1, 0, 2 * one),)),), z_step(up, -1), z_step(down, 1)
    )
    return (first, second), (swap(first), swap(second)), (first,), (second,)


def core_sums(left, right, base, received, bounds, after=()):
    def kernel(left_ref, right_ref, received_ref, *refs):
        outs = refs[len(after) :]
        for (a, b), out in zip(bounds, outs):
            product = dot_tn(left_ref[:, base + a : base + b], right_ref[...])
            out[...] = (product + received_ref[a:b, :].astype(F32)).astype(BF)

    shapes = tuple(shape((b - a, right.shape[1]), BF) for a, b in bounds)
    return call(kernel, shapes, (), left, right, received, after=after)


def part_product(left, right, base, rows, after=()):
    def kernel(*refs):
        left_ref, right_ref, out = refs[0], refs[1], refs[-1]
        step = 2 * ROWS
        for a in range(0, rows, step):
            out[a : a + step, :] = dot_tn(
                left_ref[:, base + a : base + a + step], right_ref[...]
            ).astype(BF)

    return call(kernel, shape((rows, right.shape[1]), BF), (), left, right, after=after)


def scatter_qkv(normed, grad, after_first, after_sums, meanwhile):
    one = ROWS
    half = normed.shape[1] // 2
    late = half - EARLY
    product = part_product(normed, grad, half + EARLY, late, after_first)
    late_other = swap(product)
    product = part_product(normed, grad, half, EARLY, (product,))
    early_other = swap(product)
    own_gains, gains = meanwhile(product)
    rows = lambda *at: [(a * one, b * one) for a, b in at]
    s02, s12_21, s32_23, s22 = core_sums(
        normed, grad, EARLY, late_other, rows((0, 1), (1, 3), (3, 5), (5, 6)), (own_gains,)
    )
    hop = y_step(s22, 1)
    s00, s01_03, s10, s30, s11_13, s20, s31_33 = core_sums(
        normed,
        grad,
        0,
        early_other,
        rows((0, 1), (1, 3), (3, 4), (4, 5), (5, 7), (7, 8), (8, 10)),
    )
    (plus,) = combine(
        ((((0, 0, one), (1, 0, one)), ((0, one, 2 * one),)),), s12_21, hop, after=(gains, *after_sums)
    )
    gains = sum_over(copied(gains, (plus,)), shard_exchange, (1,))
    gains = sum_over(gains, dp_exchange, (8, 16))
    below, above = y_step(plus, 1), y_step(s32_23, -1)
    plus, minus, z_across = combine(
        (
            (((0, 0, one), (3, one, 2 * one)), ((0, one, 2 * one),)),
            (
                ((1, 0, one),),
                ((1, one, 2 * one), (4, one, 2 * one)),
                ((2, 0, one),),
            ),
            (((5, 0, one), (3, 0, one), (4, 0, one)),),
        ),
        s11_13,
        s31_33,
        s20,
        below,
        above,
        s02,
        after=(gains,),
    )
    z_hop = z_step(z_across, 1)
    gains = sum_over(copied(gains, (z_hop,)), dp_exchange, (2, 4))
    below, above = y_step(plus, 1), y_step(minus, -1)
    last_below = y_step(s10, 1)
    minus, z_ahead, z_behind = combine(
        (
            (((0, 0, one), (1, 2 * one, 3 * one)),),
            (((2, 0, one), (3, 0, one), (1, 0, one), (4, 0, one)),),
            (((2, one, 2 * one), (3, one, 2 * one), (1, one, 2 * one)),),
        ),
        s30,
        above,
        s01_03,
        below,
        z_hop,
        after=(gains, last_below),
    )
    last_above = y_step(minus, -1)
    from_below, from_above = z_step(z_ahead, 1), z_step(z_behind, -1)
    total = sum(
        part.astype(F32) for part in (s00, last_below, last_above, from_below, from_above)
    )
    return total, gains, (minus,)


def scatter_out(cot, attended, after):
    one = ROWS
    half = cot.shape[1] // 2
    product = part_product(cot, attended, half, half, after)
    other = swap(product)
    own, ahead, behind, across_up, across_down = core_sums(
        cot,
        attended,
        0,
        other,
        [(a * one, b * one) for a, b in ((0, 4), (4, 8), (8, 12), (12, 14), (14, 16))],
    )
    up, down = z_step(across_up, 1), z_step(across_down, -1)
    plus, minus = combine(
        (
            (((0, 0, 2 * one), (2, 0, 2 * one)), ((0, 2 * one, 4 * one),)),
            (((1, 0, 2 * one),), ((1, 2 * one, 4 * one), (3, 0, 2 * one))),
        ),
        ahead,
        behind,
        up,
        down,
    )
    below, above = z_step(plus, 1), z_step(minus, -1)
    return own, plus, below, above


def scatter_out_last(own, below, above, after):
    one = ROWS
    parts = combine(
        tuple(
            (tuple((i, k * one, (k + 1) * one) for i in range(3)),) for k in range(4)
        ),
        own,
        below,
        above,
        after=after,
    )
    hops = (y_step(parts[1], 1), y_step(parts[2], -1), y_step(parts[3], 2))
    return sum(hop.astype(F32) for hop in (parts[0], *hops))


def dp_exchange(value, bit):
    return lax.ppermute(value, "dp", [(s, s ^ bit) for s in range(N_DP)])


def shard_exchange(value, bit):
    return lax.ppermute(value, "shard", [(s, s ^ bit) for s in range(N_SHARD)])


def sum_over(value, exchange, bits):
    for bit in bits:
        value = value + exchange(value, bit)
    return value


def norm_kernel(places, table, tokens, gain, after, out):
    width = tokens.shape[0] * tokens.shape[2]
    per = tokens.shape[2] // ROWS
    rows = tokens.shape[1]
    total = jnp.zeros((rows, ROWS), F32)
    for j in range(width // ROWS):
        total += tokens[j // per, :, (j % per) * ROWS : (j % per + 1) * ROWS].astype(F32)
    mean = jnp.sum(total, axis=-1, keepdims=True) / width
    square = jnp.zeros((rows, ROWS), F32)
    for j in range(width // ROWS):
        part = tokens[j // per, :, (j % per) * ROWS : (j % per + 1) * ROWS].astype(F32) - mean
        square += part * part
    scale = lax.rsqrt(jnp.sum(square, axis=-1, keepdims=True) / width + EPSILON)
    for j in range(width // ROWS):
        place = places[j]
        at = pl.multiple_of((place % per) * ROWS, ROWS)
        part = tokens[place // per, :, pl.ds(at, ROWS)].astype(F32) - mean
        full_at = pl.multiple_of(table[j] * ROWS, ROWS)
        out[:, j * ROWS : (j + 1) * ROWS] = (part * scale * gain[:, pl.ds(full_at, ROWS)]).astype(BF)


def pick_kernel(plan, kept, moved, after, after_also, out):
    rows = kept.shape[0] // 4
    for k in range(8):
        number = plan[k]
        at = pl.multiple_of((number // 2 % 2 * 2 + number // 4) * rows, rows)
        even = kept[pl.ds(at, rows), :].astype(F32)
        odd = moved[pl.ds(at, rows), :].astype(F32)
        out[k * rows : (k + 1) * rows, :] = jnp.where(number % 2 == 0, even, odd).astype(BF)


def reorder_kernel(table, values, keep, out):
    for j in range(values.shape[1] // ROWS):
        at = pl.multiple_of(table[j] * ROWS, ROWS)
        part = values[:, pl.ds(at, ROWS)].astype(F32)
        out[:, j * ROWS : (j + 1) * ROWS] = jnp.where(keep[...] > 0, part, 0.0).astype(BF)


def dot_nt(left, right):
    return lax.dot_general(left, right, (((1,), (1,)), ((), ())), preferred_element_type=F32)


def dot_tn(left, right):
    return lax.dot_general(left, right, (((0,), (0,)), ((), ())), preferred_element_type=F32)


def head_norm(values):
    centred = values - jnp.mean(values, axis=-1, keepdims=True)
    scale = lax.rsqrt(jnp.mean(centred * centred, axis=-1, keepdims=True) + EPSILON)
    return centred * scale, scale


def block_mask(valid_keys, block_len):
    rows = valid_keys.shape[1]
    row_block = lax.broadcasted_iota(jnp.int32, (rows, rows), 0) // block_len
    col_block = lax.broadcasted_iota(jnp.int32, (rows, rows), 1) // block_len
    return (row_block == col_block) & (valid_keys > 0)


def softmax(queries, keys, mask, size):
    scores = dot_nt(queries, keys) / math.sqrt(size)
    scores = jnp.where(mask, scores, -1e30)
    expo = jnp.exp(scores - jnp.max(scores, axis=-1, keepdims=True))
    return expo / jnp.sum(expo, axis=-1, keepdims=True)


def project_kernel_over(bounds, carry):
    def kernel(*refs):
        sums = refs[0] if carry else None
        normed, weights, out = refs[carry], refs[carry + 1 : carry + 1 + len(bounds)], refs[-1]
        step = 3 * ROWS
        for at in range(0, out.shape[1], step):
            total = sums[:, at : at + step] if carry else jnp.zeros((out.shape[0], step), F32)
            for (a, b), weight in zip(bounds, weights):
                total += jnp.dot(
                    normed[:, a:b], weight[:, at : at + step], preferred_element_type=F32
                )
            out[:, at : at + step] = total

    return kernel


def make_attend_kernel(block_len, size):
    def kernel(projected, gains, valid_keys, attended):
        mask = block_mask(valid_keys[...], block_len)
        for head in range(projected.shape[1] // (3 * size)):
            at = head * 3 * size
            q_hat, _ = head_norm(projected[:, at : at + size])
            k_hat, _ = head_norm(projected[:, at + size : at + 2 * size])
            queries = (q_hat * gains[0:1, :]).astype(BF)
            keys = (k_hat * gains[1:2, :]).astype(BF)
            values = projected[:, at + 2 * size : at + 3 * size].astype(BF)
            attend = softmax(queries, keys, mask, size).astype(BF)
            attended[:, head * size : (head + 1) * size] = jnp.dot(
                attend, values, preferred_element_type=F32
            ).astype(BF)

    return kernel


def make_attend_back_kernel(block_len, size):
    def norm_back(grad, hat, scale, gain):
        inner = grad * gain
        middle = jnp.mean(inner, axis=-1, keepdims=True)
        slope = jnp.mean(inner * hat, axis=-1, keepdims=True)
        return scale * (inner - middle - hat * slope)

    def kernel(projected, gains, valid_keys, grad_attended, after, grad_projected, grad_gains):
        mask = block_mask(valid_keys[...], block_len)
        gain_q, gain_k = gains[0:1, :], gains[1:2, :]
        sum_q = jnp.zeros((1, size), F32)
        sum_k = jnp.zeros((1, size), F32)
        for head in range(projected.shape[1] // (3 * size)):
            at = head * 3 * size
            q_hat, q_scale = head_norm(projected[:, at : at + size])
            k_hat, k_scale = head_norm(projected[:, at + size : at + 2 * size])
            queries = (q_hat * gain_q).astype(BF)
            keys = (k_hat * gain_k).astype(BF)
            values = projected[:, at + 2 * size : at + 3 * size].astype(BF)
            soft = softmax(queries, keys, mask, size)
            grad_out = grad_attended[:, head * size : (head + 1) * size]
            grad_values = dot_tn(soft.astype(BF), grad_out).astype(BF)
            grad_attend = dot_nt(grad_out, values).astype(BF).astype(F32)
            inner = jnp.sum(grad_attend * soft, axis=-1, keepdims=True)
            grad_scores = soft * (grad_attend - inner) / math.sqrt(size)
            grad_scores = jnp.where(mask, grad_scores, 0.0).astype(BF)
            grad_q = jnp.dot(grad_scores, keys, preferred_element_type=F32).astype(BF).astype(F32)
            grad_k = dot_tn(grad_scores, queries).astype(BF).astype(F32)
            sum_q += jnp.sum(grad_q * q_hat, axis=0, keepdims=True)
            sum_k += jnp.sum(grad_k * k_hat, axis=0, keepdims=True)
            grad_projected[:, at : at + size] = norm_back(grad_q, q_hat, q_scale, gain_q).astype(BF)
            grad_projected[:, at + size : at + 2 * size] = norm_back(
                grad_k, k_hat, k_scale, gain_k
            ).astype(BF)
            grad_projected[:, at + 2 * size : at + 3 * size] = grad_values
        grad_gains[0:1, :] = sum_q
        grad_gains[1:2, :] = sum_k

    return kernel


def branch_kernel(table, attended, *refs):
    weights, branch = refs[:-2], refs[-1]
    per = branch.shape[2] // ROWS
    j = 0
    for weight in weights:
        step = 2 * ROWS
        for a in range(0, weight.shape[0], step):
            product = dot_nt(attended[...], weight[a : a + step, :]).astype(BF)
            for k in range(2):
                block = table[j + k]
                at = pl.multiple_of((block % per) * ROWS, ROWS)
                branch[block // per, :, pl.ds(at, ROWS)] = product[:, k * ROWS : (k + 1) * ROWS]
            j += 2


def out_back_kernel(cot, *refs):
    weights, out = refs[:-1], refs[-1]
    total = jnp.zeros(out.shape, F32)
    at = 0
    for weight in weights:
        rows = weight.shape[0]
        total += jnp.dot(cot[:, at : at + rows], weight[...], preferred_element_type=F32)
        at += rows
    out[...] = total.astype(BF)


def gain_kernel(table, grad_projected, normed, *refs):
    weights, out = refs[:-2], refs[-1]
    j = 0
    for weight in weights:
        blocks = weight.shape[0] // ROWS
        grad = dot_nt(grad_projected[...], weight[...]).astype(BF).astype(F32)
        here = normed[:, j * ROWS : (j + blocks) * ROWS].astype(F32)
        sums = jnp.sum(grad * here, axis=0, keepdims=True)
        for k in range(blocks):
            out[pl.ds(table[j + k], 1), :] = sums[:, k * ROWS : (k + 1) * ROWS]
        j += blocks


def call(kernel, shapes, tables, *arrays, flops=0, after=()):
    smem = pl.BlockSpec(memory_space=pltpu.SMEM)
    vmem = pl.BlockSpec(memory_space=pltpu.VMEM)
    several = isinstance(shapes, tuple)
    moved = sum(a.size * a.dtype.itemsize for a in arrays)
    return pl.pallas_call(
        kernel,
        out_shape=shapes,
        in_specs=[smem] * len(tables)
        + [vmem] * len(arrays)
        + [pl.BlockSpec(memory_space=pl.ANY)] * len(after),
        out_specs=(vmem,) * len(shapes) if several else vmem,
        compiler_params=pltpu.CompilerParams(vmem_limit_bytes=28 * 1024 * 1024),
        cost_estimate=pl.CostEstimate(flops=flops, bytes_accessed=moved, transcendentals=0),
    )(*tables, *arrays, *after)


def shape(dims, dtype):
    return jax.ShapeDtypeStruct(dims, dtype)


def per_device(
    packed,
    counts,
    dest_plan,
    source_plan,
    slot_counts,
    cotangent,
    qkv_weight,
    out_weight,
    ln_gain,
    qk_gains,
):
    image_total = counts.shape[1]
    half_images = image_total // 2
    far_gap = N_DP // 2 - half_images
    block_len, width = cotangent.shape[1], cotangent.shape[2]
    rows = image_total * block_len
    heads, size = out_weight.shape[1], out_weight.shape[2]
    share = width // N_SHARD
    me = lax.axis_index("shard")

    qkv_table = absolute_blocks(QKV_ORDER)
    out_table = absolute_blocks(OUT_ORDER)
    packed_share = lax.dynamic_slice_in_dim(packed, me * share, share, 1)
    image_counts = counts[0]
    offsets = jnp.cumsum(image_counts) - image_counts
    positions = jnp.arange(block_len, dtype=jnp.int32)
    offset_ids = jnp.arange(image_total, dtype=jnp.int32)
    chosen = dest_plan[0][None, :] == offset_ids[:, None]
    starts = jnp.sum(jnp.where(chosen, offsets[None, :], 0), axis=1)
    lengths = jnp.sum(jnp.where(chosen, image_counts[None, :], 0), axis=1)
    row_index = jnp.clip(starts[:, None] + positions[None, :], 0, packed.shape[0] - 1)
    keep_rows = (positions[None, :] < lengths[:, None])[..., None]
    outgoing = jnp.where(
        keep_rows, jnp.take(packed_share, row_index, axis=0), jnp.zeros((), BF)
    )
    outgoing = outgoing.reshape(rows, share)
    weight = qkv_weight.reshape(ROWS, heads * 3 * size)

    def pieces(chosen):
        return tuple(((i, k * block_len, (k + 1) * block_len),) for i, k in chosen)

    moved = dp_rotate(outgoing[rows // 2 :], half_images + far_gap)
    y_ahead, y_behind = y_step(weight, -1), y_step(weight, 1)
    out_start = copied(out_weight.reshape(ROWS, heads * size), (y_ahead, y_behind))
    out_ahead, out_behind = y_step(out_start, -1), y_step(out_start, 1)
    out_across = y_step(out_start, 2)
    z_weight = copied(weight, (moved, y_ahead, y_behind))
    z_ahead, z_behind = z_step(z_weight, -1), z_step(z_weight, 1)
    send, keep = combine(
        (
            pieces([(i, k) for i in (0, 1) for k in (2, 3)]),
            pieces([(i, k) for i in (0, 1) for k in (0, 1)]),
        ),
        outgoing,
        moved,
    )
    moved = dp_rotate(send, 2)
    send, keep = combine(
        (
            pieces([(i, k) for i in (0, 1) for k in (1, 3)]),
            pieces([(i, k) for i in (0, 1) for k in (0, 2)]),
        ),
        keep,
        moved,
        after=(out_ahead, out_behind, out_across),
    )
    moved = dp_rotate(send, 1)
    own_share = call(
        pick_kernel,
        shape((rows, share), BF),
        (source_plan[0],),
        keep,
        moved,
        after=(z_ahead, z_behind),
    )
    block_share = own_share.reshape(image_total, block_len, share)
    next_share = shard_shift(own_share, dl=1)

    first, up, near = gather_first(
        weight, z_ahead, z_behind, y_ahead, y_behind, ()
    )
    from_ahead, from_behind = y_step(up, -1), y_step(near, 1)
    other_first = swap(first)
    z_across = z_step(z_ahead, -1)

    (pair,) = combine(((((0, 0, rows),), ((1, 0, rows),)),), own_share, next_share)
    groups = [[x * NL + low for x in range(NX)] for low in range(NL)]
    tokens = lax.all_gather(pair, "shard", axis=0, tiled=True, axis_index_groups=groups)
    tokens = tokens.reshape(N_SHARD, rows, share)
    valid_rows = positions[None, :] < slot_counts[0][:, None]
    valid_keys = valid_rows.astype(F32).reshape(1, rows)
    valid_column = valid_rows.astype(F32).reshape(rows, 1)

    cot = call(
        reorder_kernel,
        shape((rows, width), BF),
        (out_table,),
        cotangent.reshape(rows, width),
        valid_column,
    )

    second, up, down = gather_second(
        from_ahead, from_behind, z_across, (other_first, cot, out_across)
    )
    third, fourth = y_step(up, -1), y_step(down, 1)
    other_second = swap(second)
    fifth = y_step(fourth[:ROWS], 1)
    out_mine, out_other, out_column, out_second = gather_out(
        out_start, out_ahead, out_behind, out_across, (first,), (third, fourth)
    )

    per = share // ROWS
    places = ((qkv_table // per) ^ (me % NL)) * per + qkv_table % per
    normed = call(
        norm_kernel,
        shape((rows, width), BF),
        (places, qkv_table),
        tokens,
        ln_gain.reshape(1, width),
        after=out_column,
    )
    sizes = [len(part) * ROWS for part in QKV_PARTS] * 2
    bounds = np.cumsum([0] + sizes)
    bounds = list(zip(bounds[:-1].tolist(), bounds[1:].tolist()))
    early, late = (0, 1, 5, 6), (2, 3, 4, 7, 8, 9)
    projected_shape = shape((rows, heads * 3 * size), F32)
    projected = call(
        project_kernel_over([bounds[i] for i in early], 0),
        projected_shape,
        (),
        normed,
        first,
        second,
        other_first,
        other_second,
        flops=2 * rows * width * heads * 2 * size,
    )
    other_third, other_fourth = swap(third), swap(fourth)
    other_fifth = swap(copied(fifth, (projected,)))
    parts = [first, second, third, fourth, fifth]
    parts += [other_first, other_second, other_third, other_fourth, other_fifth]
    projected = call(
        project_kernel_over([bounds[i] for i in late], 1),
        projected_shape,
        (),
        projected,
        normed,
        *[parts[i] for i in late],
        after=out_second,
        flops=2 * rows * width * heads * size,
    )
    attended = call(
        make_attend_kernel(block_len, size),
        shape((rows, heads * size), BF),
        (),
        projected,
        qk_gains,
        valid_keys,
    )

    out_sums, out_plus, *out_moved = scatter_out(cot, attended, out_other)

    out_parts = (*out_mine, *out_other)
    branch = call(
        branch_kernel,
        shape((N_SHARD, rows, share), BF),
        (out_table,),
        attended,
        *out_parts,
        after=(out_sums,),
        flops=2 * rows * width * heads * size,
    )
    summed = lax.psum_scatter(branch, "shard", scatter_dimension=0, tiled=False)
    summed = summed.reshape(image_total, block_len, share).astype(F32)
    block_out = jnp.where(valid_rows[..., None], block_share.astype(F32) + summed, 0.0).astype(BF)

    grad_attended = call(
        out_back_kernel,
        shape((rows, heads * size), BF),
        (),
        cot,
        *out_parts,
        flops=2 * rows * width * heads * size,
    )
    grad_projected, grad_gains = call(
        make_attend_back_kernel(block_len, size),
        (shape((rows, heads * 3 * size), BF), shape((2, size), F32)),
        (),
        projected,
        qk_gains,
        valid_keys,
        grad_attended,
        after=(out_plus,),
    )

    def gain_sums(midway):
        grad_gain = call(
            gain_kernel,
            shape((N_DP, ROWS), F32),
            (qkv_table,),
            grad_projected,
            normed,
            *parts,
            after=(midway,),
            flops=2 * rows * width * heads * 3 * size,
        )
        grad_gain = grad_gain / ln_gain.reshape(N_DP, ROWS)
        own_gains = jnp.concatenate([grad_gain, grad_gains], axis=0)
        return own_gains, sum_over(sum_over(own_gains, dp_exchange, (1,)), shard_exchange, (2, 4))

    final_q, totals, third_round = scatter_qkv(
        normed, grad_projected, (branch,), out_moved, gain_sums
    )
    final_o = scatter_out_last(out_sums, *out_moved, third_round)
    return (
        block_out,
        final_q.reshape(ROWS, heads, 3 * size),
        final_o.reshape(ROWS, heads, size),
        totals[:N_DP].reshape(width),
        totals[N_DP:],
    )


def solution(mesh):
    return jax.shard_map(
        per_device,
        mesh=mesh,
        in_specs=(
            P("dp", None),
            P("dp", None),
            P("dp", None),
            P("dp", None),
            P("dp", None),
            P("dp", None, None),
            P("dp", "shard", None),
            P("dp", "shard", None),
            P(),
            P(),
        ),
        out_specs=(
            P("dp", None, "shard"),
            P("dp", "shard", None),
            P("dp", "shard", None),
            P(),
            P(),
        ),
        check_vma=False,
    )
```

```python
import math

import jax
import jax.numpy as jnp
import numpy as np
from jax import lax
from jax.experimental import pallas as pl
from jax.experimental.pallas import tpu as pltpu
from jax.sharding import PartitionSpec as P

EPSILON = 1e-06
BF = jnp.bfloat16
F32 = jnp.float32

NZ, NY, NC = 4, 4, 2
NX, NL = 4, 2
N_DP = NZ * NY * NC
N_SHARD = NX * NL
ROWS = 128

QKV_PARTS = (
    ((0, 0), (0, 1), (0, 3), (1, 0), (3, 0)),
    ((1, 1), (1, 3), (2, 0), (3, 1), (3, 3), (0, 2)),
    ((1, 2), (2, 1)),
    ((3, 2), (2, 3)),
    ((2, 2),),
)
QKV_ORDER = [(c, y, z) for c in range(NC) for part in QKV_PARTS for y, z in part]
EARLY = 10 * ROWS
OUT_ORDER = [(c, y, z) for c in range(NC) for z in (0, 1, 3, 2) for y in (0, 1, 3, 2)]


def dp_shift(value, dz=0, dy=0, dc=0):
    pairs = []
    for z in range(NZ):
        for y in range(NY):
            for c in range(NC):
                target = ((z + dz) % NZ) * NY * NC + ((y + dy) % NY) * NC + (c + dc) % NC
                pairs.append((z * NY * NC + y * NC + c, target))
    return lax.ppermute(value, "dp", pairs)


def dp_rotate(value, steps):
    return lax.ppermute(value, "dp", [(s, (s + steps) % N_DP) for s in range(N_DP)])


def shard_shift(value, dx=0, dl=0):
    pairs = []
    for x in range(NX):
        for low in range(NL):
            pairs.append((x * NL + low, ((x + dx) % NX) * NL + (low + dl) % NL))
    return lax.ppermute(value, "shard", pairs)


def absolute_blocks(order):
    me = lax.axis_index("dp")
    z, y, c = me // (NY * NC), (me // NC) % NY, me % NC
    table = np.asarray(order, dtype=np.int32)
    return (
        ((z + table[:, 2]) % NZ) * (NY * NC) + ((y + table[:, 1]) % NY) * NC + (c + table[:, 0]) % NC
    ).astype(jnp.int32)


def y_step(value, steps):
    return dp_shift(value, dy=steps)


def z_step(value, steps):
    return dp_shift(value, dz=steps)


def swap(value):
    return dp_shift(value, dc=1)


def combine(plans, *arrays, after=(), dtype=BF):
    count = len(arrays)
    width = arrays[0].shape[1]

    def kernel(*refs):
        for plan, out in zip(plans, refs[count + len(after) :]):
            at = 0
            for terms in plan:
                rows = terms[0][2] - terms[0][1]
                parts = [refs[i][a:b, :] for i, a, b in terms]
                if len(parts) > 1:
                    parts = [part.astype(F32) for part in parts]
                total = parts[0]
                for part in parts[1:]:
                    total = total + part
                out[at : at + rows, :] = total.astype(dtype)
                at += rows

    sizes = [sum(terms[0][2] - terms[0][1] for terms in plan) for plan in plans]
    return call(kernel, tuple(shape((size, width), dtype) for size in sizes), (), *arrays, after=after)


def copied(value, after):
    (value,) = combine(((((0, 0, value.shape[0]),),),), value, after=after, dtype=value.dtype)
    return value


def gather_first(weight, z_ahead, z_behind, y_ahead, y_behind, after):
    one = ROWS
    return combine(
        (
            tuple(((i, 0, one),) for i in range(5)),
            (((1, 0, one),), ((2, 0, one),), ((3, 0, one),)),
            (((1, 0, one),), ((2, 0, one),)),
        ),
        weight,
        z_ahead,
        z_behind,
        y_ahead,
        y_behind,
        after=after,
    )


def gather_second(from_ahead, from_behind, z_across, after):
    one = ROWS
    return combine(
        (
            (((0, 0, 3 * one),), ((1, 0, 2 * one),), ((2, 0, one),)),
            (((2, 0, one),), ((0, 0, one),)),
            (((2, 0, one),), ((1, one, 2 * one),)),
        ),
        from_ahead,
        from_behind,
        z_across,
        after=after,
    )


def gather_out(column, z_behind, after_z):
    one = ROWS
    z_ahead = z_step(column, -1)
    first, up, down = combine(
        (
            (((0, 0, 4 * one),), ((1, 0, 4 * one),), ((2, 0, 4 * one),)),
            (((1, 0, 2 * one),),),
            (((2, 2 * one, 4 * one),),),
        ),
        column,
        z_ahead,
        z_behind,
        after=after_z,
    )
    (second,) = combine(
        ((((0, 0, 2 * one),), ((1, 0, 2 * one),)),), z_step(up, -1), z_step(down, 1)
    )
    return (first, second), (swap(first), swap(second)), (first,), (second,)


def core_sums(left, right, base, received, bounds, after=()):
    def kernel(left_ref, right_ref, received_ref, *refs):
        outs = refs[len(after) :]
        for (a, b), out in zip(bounds, outs):
            product = dot_tn(left_ref[:, base + a : base + b], right_ref[...])
            out[...] = (product + received_ref[a:b, :].astype(F32)).astype(BF)

    shapes = tuple(shape((b - a, right.shape[1]), BF) for a, b in bounds)
    return call(kernel, shapes, (), left, right, received, after=after)


def part_product(left, right, base, rows, after=()):
    def kernel(*refs):
        left_ref, right_ref, out = refs[0], refs[1], refs[-1]
        step = 2 * ROWS
        for a in range(0, rows, step):
            out[a : a + step, :] = dot_tn(
                left_ref[:, base + a : base + a + step], right_ref[...]
            ).astype(BF)

    return call(kernel, shape((rows, right.shape[1]), BF), (), left, right, after=after)


def scatter_qkv(normed, grad, after_first, after_sums, meanwhile):
    one = ROWS
    half = normed.shape[1] // 2
    late = half - EARLY
    product = part_product(normed, grad, half + EARLY, late, after_first)
    late_other = swap(product)
    product = part_product(normed, grad, half, EARLY, (product,))
    early_other = swap(product)
    own_gains, gains = meanwhile(product)
    rows = lambda *at: [(a * one, b * one) for a, b in at]
    s02, s12_21, s32_23, s22 = core_sums(
        normed, grad, EARLY, late_other, rows((0, 1), (1, 3), (3, 5), (5, 6)), (own_gains,)
    )
    hop = y_step(s22, 1)
    s00, s01_03, s10, s30, s11_13, s20, s31_33 = core_sums(
        normed,
        grad,
        0,
        early_other,
        rows((0, 1), (1, 3), (3, 4), (4, 5), (5, 7), (7, 8), (8, 10)),
    )
    (plus,) = combine(
        ((((0, 0, one), (1, 0, one)), ((0, one, 2 * one),)),), s12_21, hop, after=(gains, *after_sums)
    )
    gains = sum_over(copied(gains, (plus,)), shard_exchange, (1,))
    gains = sum_over(gains, dp_exchange, (8, 16))
    below, above = y_step(plus, 1), y_step(s32_23, -1)
    plus, minus, z_across = combine(
        (
            (((0, 0, one), (3, one, 2 * one)), ((0, one, 2 * one),)),
            (
                ((1, 0, one),),
                ((1, one, 2 * one), (4, one, 2 * one)),
                ((2, 0, one),),
            ),
            (((5, 0, one), (3, 0, one), (4, 0, one)),),
        ),
        s11_13,
        s31_33,
        s20,
        below,
        above,
        s02,
        after=(gains,),
    )
    z_hop = z_step(z_across, 1)
    gains = sum_over(copied(gains, (z_hop,)), dp_exchange, (2, 4))
    below, above = y_step(plus, 1), y_step(minus, -1)
    last_below = y_step(s10, 1)
    minus, z_ahead, z_behind = combine(
        (
            (((0, 0, one), (1, 2 * one, 3 * one)),),
            (((2, 0, one), (3, 0, one), (1, 0, one), (4, 0, one)),),
            (((2, one, 2 * one), (3, one, 2 * one), (1, one, 2 * one)),),
        ),
        s30,
        above,
        s01_03,
        below,
        z_hop,
        after=(gains,),
    )
    last_above = y_step(minus, -1)
    from_below, from_above = z_step(z_ahead, 1), z_step(z_behind, -1)
    total = sum(
        part.astype(F32) for part in (s00, last_below, last_above, from_below, from_above)
    )
    return total, gains, (z_hop,)


def scatter_out(cot, attended, after):
    one = ROWS
    half = cot.shape[1] // 2
    product = part_product(cot, attended, half, half, after)
    other = swap(product)
    own, ahead, behind, across_up, across_down = core_sums(
        cot,
        attended,
        0,
        other,
        [(a * one, b * one) for a, b in ((0, 4), (4, 8), (8, 12), (12, 14), (14, 16))],
    )
    up, down = z_step(across_up, 1), z_step(across_down, -1)
    plus, minus = combine(
        (
            (((0, 0, 2 * one), (2, 0, 2 * one)), ((0, 2 * one, 4 * one),)),
            (((1, 0, 2 * one),), ((1, 2 * one, 4 * one), (3, 0, 2 * one))),
        ),
        ahead,
        behind,
        up,
        down,
    )
    below, above = z_step(plus, 1), z_step(minus, -1)
    return own, plus, below, above


def scatter_out_last(own, below, above, after):
    one = ROWS
    parts = combine(
        tuple(
            (tuple((i, k * one, (k + 1) * one) for i in range(3)),) for k in range(4)
        ),
        own,
        below,
        above,
        after=after,
    )
    hops = (y_step(parts[1], 1), y_step(parts[2], -1), y_step(parts[3], 2))
    return sum(hop.astype(F32) for hop in (parts[0], *hops))


def dp_exchange(value, bit):
    return lax.ppermute(value, "dp", [(s, s ^ bit) for s in range(N_DP)])


def shard_exchange(value, bit):
    return lax.ppermute(value, "shard", [(s, s ^ bit) for s in range(N_SHARD)])


def sum_over(value, exchange, bits):
    for bit in bits:
        value = value + exchange(value, bit)
    return value


def norm_kernel(places, table, tokens, gain, after, out):
    width = tokens.shape[0] * tokens.shape[2]
    per = tokens.shape[2] // ROWS
    rows = tokens.shape[1]
    total = jnp.zeros((rows, ROWS), F32)
    for j in range(width // ROWS):
        total += tokens[j // per, :, (j % per) * ROWS : (j % per + 1) * ROWS].astype(F32)
    mean = jnp.sum(total, axis=-1, keepdims=True) / width
    square = jnp.zeros((rows, ROWS), F32)
    for j in range(width // ROWS):
        part = tokens[j // per, :, (j % per) * ROWS : (j % per + 1) * ROWS].astype(F32) - mean
        square += part * part
    scale = lax.rsqrt(jnp.sum(square, axis=-1, keepdims=True) / width + EPSILON)
    for j in range(width // ROWS):
        place = places[j]
        at = pl.multiple_of((place % per) * ROWS, ROWS)
        part = tokens[place // per, :, pl.ds(at, ROWS)].astype(F32) - mean
        full_at = pl.multiple_of(table[j] * ROWS, ROWS)
        out[:, j * ROWS : (j + 1) * ROWS] = (part * scale * gain[:, pl.ds(full_at, ROWS)]).astype(BF)


def pick_kernel(plan, kept, moved, *refs):
    rows = kept.shape[0] // 4
    out = refs[-1]
    for k in range(8):
        number = plan[k]
        at = pl.multiple_of((number // 2 % 2 * 2 + number // 4) * rows, rows)
        even = kept[pl.ds(at, rows), :].astype(F32)
        odd = moved[pl.ds(at, rows), :].astype(F32)
        out[k * rows : (k + 1) * rows, :] = jnp.where(number % 2 == 0, even, odd).astype(BF)


def reorder_kernel(table, values, keep, out):
    for j in range(values.shape[1] // ROWS):
        at = pl.multiple_of(table[j] * ROWS, ROWS)
        part = values[:, pl.ds(at, ROWS)].astype(F32)
        out[:, j * ROWS : (j + 1) * ROWS] = jnp.where(keep[...] > 0, part, 0.0).astype(BF)


def dot_nt(left, right):
    return lax.dot_general(left, right, (((1,), (1,)), ((), ())), preferred_element_type=F32)


def dot_tn(left, right):
    return lax.dot_general(left, right, (((0,), (0,)), ((), ())), preferred_element_type=F32)


def head_norm(values):
    centred = values - jnp.mean(values, axis=-1, keepdims=True)
    scale = lax.rsqrt(jnp.mean(centred * centred, axis=-1, keepdims=True) + EPSILON)
    return centred * scale, scale


def block_mask(valid_keys, block_len):
    rows = valid_keys.shape[1]
    row_block = lax.broadcasted_iota(jnp.int32, (rows, rows), 0) // block_len
    col_block = lax.broadcasted_iota(jnp.int32, (rows, rows), 1) // block_len
    return (row_block == col_block) & (valid_keys > 0)


def softmax(queries, keys, mask, size):
    scores = dot_nt(queries, keys) / math.sqrt(size)
    scores = jnp.where(mask, scores, -1e30)
    expo = jnp.exp(scores - jnp.max(scores, axis=-1, keepdims=True))
    return expo / jnp.sum(expo, axis=-1, keepdims=True)


def project_kernel_over(bounds, carry):
    def kernel(*refs):
        sums = refs[0] if carry else None
        normed, weights, out = refs[carry], refs[carry + 1 : carry + 1 + len(bounds)], refs[-1]
        step = 3 * ROWS
        for at in range(0, out.shape[1], step):
            total = sums[:, at : at + step] if carry else jnp.zeros((out.shape[0], step), F32)
            for (a, b), weight in zip(bounds, weights):
                total += jnp.dot(
                    normed[:, a:b], weight[:, at : at + step], preferred_element_type=F32
                )
            out[:, at : at + step] = total

    return kernel


def make_attend_kernel(block_len, size):
    def kernel(projected, gains, valid_keys, attended):
        mask = block_mask(valid_keys[...], block_len)
        for head in range(projected.shape[1] // (3 * size)):
            at = head * 3 * size
            q_hat, _ = head_norm(projected[:, at : at + size])
            k_hat, _ = head_norm(projected[:, at + size : at + 2 * size])
            queries = (q_hat * gains[0:1, :]).astype(BF)
            keys = (k_hat * gains[1:2, :]).astype(BF)
            values = projected[:, at + 2 * size : at + 3 * size].astype(BF)
            attend = softmax(queries, keys, mask, size).astype(BF)
            attended[:, head * size : (head + 1) * size] = jnp.dot(
                attend, values, preferred_element_type=F32
            ).astype(BF)

    return kernel


def make_attend_back_kernel(block_len, size):
    def norm_back(grad, hat, scale, gain):
        inner = grad * gain
        middle = jnp.mean(inner, axis=-1, keepdims=True)
        slope = jnp.mean(inner * hat, axis=-1, keepdims=True)
        return scale * (inner - middle - hat * slope)

    def kernel(projected, gains, valid_keys, grad_attended, grad_projected, grad_gains):
        mask = block_mask(valid_keys[...], block_len)
        gain_q, gain_k = gains[0:1, :], gains[1:2, :]
        sum_q = jnp.zeros((1, size), F32)
        sum_k = jnp.zeros((1, size), F32)
        for head in range(projected.shape[1] // (3 * size)):
            at = head * 3 * size
            q_hat, q_scale = head_norm(projected[:, at : at + size])
            k_hat, k_scale = head_norm(projected[:, at + size : at + 2 * size])
            queries = (q_hat * gain_q).astype(BF)
            keys = (k_hat * gain_k).astype(BF)
            values = projected[:, at + 2 * size : at + 3 * size].astype(BF)
            soft = softmax(queries, keys, mask, size)
            grad_out = grad_attended[:, head * size : (head + 1) * size]
            grad_values = dot_tn(soft.astype(BF), grad_out).astype(BF)
            grad_attend = dot_nt(grad_out, values).astype(BF).astype(F32)
            inner = jnp.sum(grad_attend * soft, axis=-1, keepdims=True)
            grad_scores = soft * (grad_attend - inner) / math.sqrt(size)
            grad_scores = jnp.where(mask, grad_scores, 0.0).astype(BF)
            grad_q = jnp.dot(grad_scores, keys, preferred_element_type=F32).astype(BF).astype(F32)
            grad_k = dot_tn(grad_scores, queries).astype(BF).astype(F32)
            sum_q += jnp.sum(grad_q * q_hat, axis=0, keepdims=True)
            sum_k += jnp.sum(grad_k * k_hat, axis=0, keepdims=True)
            grad_projected[:, at : at + size] = norm_back(grad_q, q_hat, q_scale, gain_q).astype(BF)
            grad_projected[:, at + size : at + 2 * size] = norm_back(
                grad_k, k_hat, k_scale, gain_k
            ).astype(BF)
            grad_projected[:, at + 2 * size : at + 3 * size] = grad_values
        grad_gains[0:1, :] = sum_q
        grad_gains[1:2, :] = sum_k

    return kernel


def branch_kernel(table, attended, *refs):
    weights, branch = refs[:-2], refs[-1]
    per = branch.shape[2] // ROWS
    j = 0
    for weight in weights:
        step = 2 * ROWS
        for a in range(0, weight.shape[0], step):
            product = dot_nt(attended[...], weight[a : a + step, :]).astype(BF)
            for k in range(2):
                block = table[j + k]
                at = pl.multiple_of((block % per) * ROWS, ROWS)
                branch[block // per, :, pl.ds(at, ROWS)] = product[:, k * ROWS : (k + 1) * ROWS]
            j += 2


def out_back_kernel(cot, *refs):
    weights, out = refs[:-1], refs[-1]
    total = jnp.zeros(out.shape, F32)
    at = 0
    for weight in weights:
        rows = weight.shape[0]
        total += jnp.dot(cot[:, at : at + rows], weight[...], preferred_element_type=F32)
        at += rows
    out[...] = total.astype(BF)


def gain_kernel(table, grad_projected, normed, *refs):
    weights, out = refs[:-2], refs[-1]
    j = 0
    for weight in weights:
        blocks = weight.shape[0] // ROWS
        grad = dot_nt(grad_projected[...], weight[...]).astype(BF).astype(F32)
        here = normed[:, j * ROWS : (j + blocks) * ROWS].astype(F32)
        sums = jnp.sum(grad * here, axis=0, keepdims=True)
        for k in range(blocks):
            out[pl.ds(table[j + k], 1), :] = sums[:, k * ROWS : (k + 1) * ROWS]
        j += blocks


def call(kernel, shapes, tables, *arrays, flops=0, after=()):
    smem = pl.BlockSpec(memory_space=pltpu.SMEM)
    vmem = pl.BlockSpec(memory_space=pltpu.VMEM)
    several = isinstance(shapes, tuple)
    moved = sum(a.size * a.dtype.itemsize for a in arrays)
    return pl.pallas_call(
        kernel,
        out_shape=shapes,
        in_specs=[smem] * len(tables)
        + [vmem] * len(arrays)
        + [pl.BlockSpec(memory_space=pl.ANY)] * len(after),
        out_specs=(vmem,) * len(shapes) if several else vmem,
        compiler_params=pltpu.CompilerParams(vmem_limit_bytes=28 * 1024 * 1024),
        cost_estimate=pl.CostEstimate(flops=flops, bytes_accessed=moved, transcendentals=0),
    )(*tables, *arrays, *after)


def shape(dims, dtype):
    return jax.ShapeDtypeStruct(dims, dtype)


def per_device(
    packed,
    counts,
    dest_plan,
    source_plan,
    slot_counts,
    cotangent,
    qkv_weight,
    out_weight,
    ln_gain,
    qk_gains,
):
    image_total = counts.shape[1]
    half_images = image_total // 2
    far_gap = N_DP // 2 - half_images
    block_len, width = cotangent.shape[1], cotangent.shape[2]
    rows = image_total * block_len
    heads, size = out_weight.shape[1], out_weight.shape[2]
    share = width // N_SHARD
    me = lax.axis_index("shard")

    qkv_table = absolute_blocks(QKV_ORDER)
    out_table = absolute_blocks(OUT_ORDER)
    packed_share = lax.dynamic_slice_in_dim(packed, me * share, share, 1)
    image_counts = counts[0]
    offsets = jnp.cumsum(image_counts) - image_counts
    positions = jnp.arange(block_len, dtype=jnp.int32)
    offset_ids = jnp.arange(image_total, dtype=jnp.int32)
    chosen = dest_plan[0][None, :] == offset_ids[:, None]
    starts = jnp.sum(jnp.where(chosen, offsets[None, :], 0), axis=1)
    lengths = jnp.sum(jnp.where(chosen, image_counts[None, :], 0), axis=1)
    row_index = jnp.clip(starts[:, None] + positions[None, :], 0, packed.shape[0] - 1)
    keep_rows = (positions[None, :] < lengths[:, None])[..., None]
    outgoing = jnp.where(
        keep_rows, jnp.take(packed_share, row_index, axis=0), jnp.zeros((), BF)
    )
    outgoing = outgoing.reshape(rows, share)
    weight = qkv_weight.reshape(ROWS, heads * 3 * size)

    def pieces(chosen):
        return tuple(((i, k * block_len, (k + 1) * block_len),) for i, k in chosen)

    moved = dp_rotate(outgoing[rows // 2 :], half_images + far_gap)
    y_ahead, y_behind = y_step(weight, -1), y_step(weight, 1)
    out_start = copied(out_weight.reshape(ROWS, heads * size), (y_ahead, y_behind))
    out_ahead, out_behind = y_step(out_start, -1), y_step(out_start, 1)
    out_across = y_step(out_start, 2)
    z_weight = copied(weight, (moved, y_ahead, y_behind))
    z_ahead, z_behind = z_step(z_weight, -1), z_step(z_weight, 1)
    send, keep = combine(
        (
            pieces([(i, k) for i in (0, 1) for k in (2, 3)]),
            pieces([(i, k) for i in (0, 1) for k in (0, 1)]),
        ),
        outgoing,
        moved,
    )
    moved = dp_rotate(send, 2)
    send, keep = combine(
        (
            pieces([(i, k) for i in (0, 1) for k in (1, 3)]),
            pieces([(i, k) for i in (0, 1) for k in (0, 2)]),
        ),
        keep,
        moved,
    )
    moved = dp_rotate(send, 1)
    own_share = call(
        pick_kernel,
        shape((rows, share), BF),
        (source_plan[0],),
        keep,
        moved,
        after=(z_ahead, z_behind, out_ahead, out_behind, out_across),
    )
    block_share = own_share.reshape(image_total, block_len, share)
    next_share = shard_shift(own_share, dl=1)

    first, up, near = gather_first(
        weight, z_ahead, z_behind, y_ahead, y_behind, ()
    )
    from_ahead, from_behind = y_step(up, -1), y_step(near, 1)
    other_first = swap(first)
    z_across = z_step(z_ahead, -1)

    (pair,) = combine(((((0, 0, rows),), ((1, 0, rows),)),), own_share, next_share)
    groups = [[x * NL + low for x in range(NX)] for low in range(NL)]
    tokens = lax.all_gather(pair, "shard", axis=0, tiled=True, axis_index_groups=groups)
    tokens = tokens.reshape(N_SHARD, rows, share)
    valid_rows = positions[None, :] < slot_counts[0][:, None]
    valid_keys = valid_rows.astype(F32).reshape(1, rows)
    valid_column = valid_rows.astype(F32).reshape(rows, 1)

    cot = call(
        reorder_kernel,
        shape((rows, width), BF),
        (out_table,),
        cotangent.reshape(rows, width),
        valid_column,
    )

    (column,) = combine(
        (tuple(((i, 0, ROWS),) for i in range(4)),),
        out_start,
        out_ahead,
        out_behind,
        out_across,
        after=(near,),
    )
    column_behind = z_step(column, 1)
    second, up, down = gather_second(
        from_ahead, from_behind, z_across, (other_first, cot, column_behind)
    )
    third, fourth = y_step(up, -1), y_step(down, 1)
    other_second = swap(second)
    (forward,) = combine(((((0, 0, ROWS),),),), fourth)
    fifth = y_step(forward, 1)
    out_mine, out_other, out_column, out_second = gather_out(column, column_behind, (forward, third))

    per = share // ROWS
    places = ((qkv_table // per) ^ (me % NL)) * per + qkv_table % per
    normed = call(
        norm_kernel,
        shape((rows, width), BF),
        (places, qkv_table),
        tokens,
        ln_gain.reshape(1, width),
        after=out_column,
    )
    sizes = [len(part) * ROWS for part in QKV_PARTS] * 2
    bounds = np.cumsum([0] + sizes)
    bounds = list(zip(bounds[:-1].tolist(), bounds[1:].tolist()))
    early, late = (0, 1, 5, 6), (2, 3, 4, 7, 8, 9)
    projected_shape = shape((rows, heads * 3 * size), F32)
    projected = call(
        project_kernel_over([bounds[i] for i in early], 0),
        projected_shape,
        (),
        normed,
        first,
        second,
        other_first,
        other_second,
        flops=2 * rows * width * heads * 2 * size,
    )
    other_third, other_fourth = swap(third), swap(fourth)
    other_fifth = swap(copied(fifth, (projected,)))
    parts = [first, second, third, fourth, fifth]
    parts += [other_first, other_second, other_third, other_fourth, other_fifth]
    projected = call(
        project_kernel_over([bounds[i] for i in late], 1),
        projected_shape,
        (),
        projected,
        normed,
        *[parts[i] for i in late],
        after=out_second,
        flops=2 * rows * width * heads * size,
    )
    attended = call(
        make_attend_kernel(block_len, size),
        shape((rows, heads * size), BF),
        (),
        projected,
        qk_gains,
        valid_keys,
    )

    out_sums, out_plus, *out_moved = scatter_out(cot, attended, out_other)

    out_parts = (*out_mine, *out_other)
    branch = call(
        branch_kernel,
        shape((N_SHARD, rows, share), BF),
        (out_table,),
        attended,
        *out_parts,
        after=(out_sums,),
        flops=2 * rows * width * heads * size,
    )
    summed = lax.psum_scatter(branch, "shard", scatter_dimension=0, tiled=False)
    summed = summed.reshape(image_total, block_len, share).astype(F32)
    block_out = jnp.where(valid_rows[..., None], block_share.astype(F32) + summed, 0.0).astype(BF)

    grad_attended = call(
        out_back_kernel,
        shape((rows, heads * size), BF),
        (),
        cot,
        *out_parts,
        flops=2 * rows * width * heads * size,
    )
    grad_projected, grad_gains = call(
        make_attend_back_kernel(block_len, size),
        (shape((rows, heads * 3 * size), BF), shape((2, size), F32)),
        (),
        projected,
        qk_gains,
        valid_keys,
        grad_attended,
    )

    def gain_sums(midway):
        grad_gain = call(
            gain_kernel,
            shape((N_DP, ROWS), F32),
            (qkv_table,),
            grad_projected,
            normed,
            *parts,
            after=(midway,),
            flops=2 * rows * width * heads * 3 * size,
        )
        grad_gain = grad_gain / ln_gain.reshape(N_DP, ROWS)
        own_gains = jnp.concatenate([grad_gain, grad_gains], axis=0)
        return own_gains, sum_over(sum_over(own_gains, dp_exchange, (1,)), shard_exchange, (2, 4))

    final_q, totals, third_round = scatter_qkv(
        normed, grad_projected, (branch, out_plus), out_moved, gain_sums
    )
    final_o = scatter_out_last(out_sums, *out_moved, third_round)
    return (
        block_out,
        final_q.reshape(ROWS, heads, 3 * size),
        final_o.reshape(ROWS, heads, size),
        totals[:N_DP].reshape(width),
        totals[N_DP:],
    )


def solution(mesh):
    return jax.shard_map(
        per_device,
        mesh=mesh,
        in_specs=(
            P("dp", None),
            P("dp", None),
            P("dp", None),
            P("dp", None),
            P("dp", None),
            P("dp", None, None),
            P("dp", "shard", None),
            P("dp", "shard", None),
            P(),
            P(),
        ),
        out_specs=(
            P("dp", None, "shard"),
            P("dp", "shard", None),
            P("dp", "shard", None),
            P(),
            P(),
        ),
        check_vma=False,
    )
```

```python
import math

import jax
import jax.numpy as jnp
import numpy as np
from jax import lax
from jax.experimental import pallas as pl
from jax.experimental.pallas import tpu as pltpu
from jax.sharding import PartitionSpec as P

EPSILON = 1e-06
BF = jnp.bfloat16
F32 = jnp.float32

NZ, NY, NC = 4, 4, 2
NX, NL = 4, 2
N_DP = NZ * NY * NC
N_SHARD = NX * NL
ROWS = 128

QKV_PARTS = (
    ((0, 0), (0, 1), (0, 3), (1, 0), (3, 0)),
    ((1, 1), (1, 3), (2, 0), (3, 1), (3, 3), (0, 2)),
    ((1, 2), (2, 1)),
    ((3, 2), (2, 3)),
    ((2, 2),),
)
QKV_ORDER = [(c, y, z) for c in range(NC) for part in QKV_PARTS for y, z in part]
EARLY = 10 * ROWS
OUT_ORDER = [(c, y, z) for c in range(NC) for z in (0, 1, 3, 2) for y in (0, 1, 3, 2)]


def dp_shift(value, dz=0, dy=0, dc=0):
    pairs = []
    for z in range(NZ):
        for y in range(NY):
            for c in range(NC):
                target = ((z + dz) % NZ) * NY * NC + ((y + dy) % NY) * NC + (c + dc) % NC
                pairs.append((z * NY * NC + y * NC + c, target))
    return lax.ppermute(value, "dp", pairs)


def dp_rotate(value, steps):
    return lax.ppermute(value, "dp", [(s, (s + steps) % N_DP) for s in range(N_DP)])


def shard_shift(value, dx=0, dl=0):
    pairs = []
    for x in range(NX):
        for low in range(NL):
            pairs.append((x * NL + low, ((x + dx) % NX) * NL + (low + dl) % NL))
    return lax.ppermute(value, "shard", pairs)


def absolute_blocks(order):
    me = lax.axis_index("dp")
    z, y, c = me // (NY * NC), (me // NC) % NY, me % NC
    table = np.asarray(order, dtype=np.int32)
    return (
        ((z + table[:, 2]) % NZ) * (NY * NC) + ((y + table[:, 1]) % NY) * NC + (c + table[:, 0]) % NC
    ).astype(jnp.int32)


def y_step(value, steps):
    return dp_shift(value, dy=steps)


def z_step(value, steps):
    return dp_shift(value, dz=steps)


def swap(value):
    return dp_shift(value, dc=1)


def combine(plans, *arrays, after=(), dtype=BF):
    count = len(arrays)
    width = arrays[0].shape[1]

    def kernel(*refs):
        for plan, out in zip(plans, refs[count + len(after) :]):
            at = 0
            for terms in plan:
                rows = terms[0][2] - terms[0][1]
                parts = [refs[i][a:b, :] for i, a, b in terms]
                if len(parts) > 1:
                    parts = [part.astype(F32) for part in parts]
                total = parts[0]
                for part in parts[1:]:
                    total = total + part
                out[at : at + rows, :] = total.astype(dtype)
                at += rows

    sizes = [sum(terms[0][2] - terms[0][1] for terms in plan) for plan in plans]
    return call(kernel, tuple(shape((size, width), dtype) for size in sizes), (), *arrays, after=after)


def copied(value, after):
    (value,) = combine(((((0, 0, value.shape[0]),),),), value, after=after, dtype=value.dtype)
    return value


def gather_first(weight, z_ahead, z_behind, y_ahead, y_behind, after):
    one = ROWS
    return combine(
        (
            tuple(((i, 0, one),) for i in range(5)),
            (((1, 0, one),), ((2, 0, one),), ((3, 0, one),)),
            (((1, 0, one),), ((2, 0, one),)),
        ),
        weight,
        z_ahead,
        z_behind,
        y_ahead,
        y_behind,
        after=after,
    )


def gather_second(from_ahead, from_behind, z_across, after):
    one = ROWS
    return combine(
        (
            (((0, 0, 3 * one),), ((1, 0, 2 * one),), ((2, 0, one),)),
            (((2, 0, one),), ((0, 0, one),)),
            (((2, 0, one),), ((1, one, 2 * one),)),
        ),
        from_ahead,
        from_behind,
        z_across,
        after=after,
    )


def gather_out(column, z_behind, after_z):
    one = ROWS
    z_ahead = z_step(column, -1)
    first, up, down = combine(
        (
            (((0, 0, 4 * one),), ((1, 0, 4 * one),), ((2, 0, 4 * one),)),
            (((1, 0, 2 * one),),),
            (((2, 2 * one, 4 * one),),),
        ),
        column,
        z_ahead,
        z_behind,
        after=after_z,
    )
    return first, z_step(up, -1), z_step(down, 1)


def core_sums(left, right, base, received, bounds, after=()):
    def kernel(left_ref, right_ref, received_ref, *refs):
        outs = refs[len(after) :]
        for (a, b), out in zip(bounds, outs):
            product = dot_tn(left_ref[:, base + a : base + b], right_ref[...])
            out[...] = (product + received_ref[a:b, :].astype(F32)).astype(BF)

    shapes = tuple(shape((b - a, right.shape[1]), BF) for a, b in bounds)
    return call(kernel, shapes, (), left, right, received, after=after)


def part_product(left, right, base, rows, after=()):
    def kernel(*refs):
        left_ref, right_ref, out = refs[0], refs[1], refs[-1]
        step = 2 * ROWS
        for a in range(0, rows, step):
            out[a : a + step, :] = dot_tn(
                left_ref[:, base + a : base + a + step], right_ref[...]
            ).astype(BF)

    return call(kernel, shape((rows, right.shape[1]), BF), (), left, right, after=after)


def scatter_qkv(normed, grad, product, after_first, after_sums, meanwhile):
    one = ROWS
    half = normed.shape[1] // 2
    late_other = swap(product)
    product = part_product(normed, grad, half, EARLY, (product,))
    early_other = swap(product)
    own_gains, gains = meanwhile(product)
    rows = lambda *at: [(a * one, b * one) for a, b in at]
    s02, s12_21, s32_23, s22 = core_sums(
        normed, grad, EARLY, late_other, rows((0, 1), (1, 3), (3, 5), (5, 6)), (own_gains, *after_first)
    )
    hop = y_step(s22, 1)
    s00, s01_03, s10, s30, s11_13, s20, s31_33 = core_sums(
        normed,
        grad,
        0,
        early_other,
        rows((0, 1), (1, 3), (3, 4), (4, 5), (5, 7), (7, 8), (8, 10)),
    )
    (plus,) = combine(
        ((((0, 0, one), (1, 0, one)), ((0, one, 2 * one),)),), s12_21, hop, after=(gains, *after_sums)
    )
    gains = sum_over(copied(gains, (plus,)), shard_exchange, (1,))
    gains = sum_over(gains, dp_exchange, (8, 16))
    below, above = y_step(plus, 1), y_step(s32_23, -1)
    plus, minus, z_across = combine(
        (
            (((0, 0, one), (3, one, 2 * one)), ((0, one, 2 * one),)),
            (
                ((1, 0, one),),
                ((1, one, 2 * one), (4, one, 2 * one)),
                ((2, 0, one),),
            ),
            (((5, 0, one), (3, 0, one), (4, 0, one)),),
        ),
        s11_13,
        s31_33,
        s20,
        below,
        above,
        s02,
        after=(gains,),
    )
    z_hop = z_step(z_across, 1)
    gains = sum_over(copied(gains, (z_hop,)), dp_exchange, (2, 4))
    below, above = y_step(plus, 1), y_step(minus, -1)
    last_below = y_step(s10, 1)
    minus, z_ahead, z_behind = combine(
        (
            (((0, 0, one), (1, 2 * one, 3 * one)),),
            (((2, 0, one), (3, 0, one), (1, 0, one), (4, 0, one)),),
            (((2, one, 2 * one), (3, one, 2 * one), (1, one, 2 * one)),),
        ),
        s30,
        above,
        s01_03,
        below,
        z_hop,
        after=(gains,),
    )
    last_above = y_step(minus, -1)
    from_below, from_above = z_step(z_ahead, 1), z_step(z_behind, -1)
    total = sum(
        part.astype(F32) for part in (s00, last_below, last_above, from_below, from_above)
    )
    return total, gains, (z_hop,)


def scatter_out(cot, attended, other, after):
    one = ROWS
    own, ahead, behind, across_up, across_down = core_sums(
        cot,
        attended,
        0,
        other,
        [(a * one, b * one) for a, b in ((0, 4), (4, 8), (8, 12), (12, 14), (14, 16))],
        after,
    )
    up, down = z_step(across_up, 1), z_step(across_down, -1)
    plus, minus = combine(
        (
            (((0, 0, 2 * one), (2, 0, 2 * one)), ((0, 2 * one, 4 * one),)),
            (((1, 0, 2 * one),), ((1, 2 * one, 4 * one), (3, 0, 2 * one))),
        ),
        ahead,
        behind,
        up,
        down,
    )
    below, above = z_step(plus, 1), z_step(minus, -1)
    return own, plus, below, above


def scatter_out_last(own, below, above, after):
    one = ROWS
    parts = combine(
        tuple(
            (tuple((i, k * one, (k + 1) * one) for i in range(3)),) for k in range(4)
        ),
        own,
        below,
        above,
        after=after,
    )
    hops = (y_step(parts[1], 1), y_step(parts[2], -1), y_step(parts[3], 2))
    return sum(hop.astype(F32) for hop in (parts[0], *hops))


def dp_exchange(value, bit):
    return lax.ppermute(value, "dp", [(s, s ^ bit) for s in range(N_DP)])


def shard_exchange(value, bit):
    return lax.ppermute(value, "shard", [(s, s ^ bit) for s in range(N_SHARD)])


def sum_over(value, exchange, bits):
    for bit in bits:
        value = value + exchange(value, bit)
    return value


def norm_kernel(places, table, tokens, gain, after, out):
    width = tokens.shape[0] * tokens.shape[2]
    per = tokens.shape[2] // ROWS
    rows = tokens.shape[1]
    total = jnp.zeros((rows, ROWS), F32)
    for j in range(width // ROWS):
        total += tokens[j // per, :, (j % per) * ROWS : (j % per + 1) * ROWS].astype(F32)
    mean = jnp.sum(total, axis=-1, keepdims=True) / width
    square = jnp.zeros((rows, ROWS), F32)
    for j in range(width // ROWS):
        part = tokens[j // per, :, (j % per) * ROWS : (j % per + 1) * ROWS].astype(F32) - mean
        square += part * part
    scale = lax.rsqrt(jnp.sum(square, axis=-1, keepdims=True) / width + EPSILON)
    for j in range(width // ROWS):
        place = places[j]
        at = pl.multiple_of((place % per) * ROWS, ROWS)
        part = tokens[place // per, :, pl.ds(at, ROWS)].astype(F32) - mean
        full_at = pl.multiple_of(table[j] * ROWS, ROWS)
        out[:, j * ROWS : (j + 1) * ROWS] = (part * scale * gain[:, pl.ds(full_at, ROWS)]).astype(BF)


def pick_kernel(plan, kept, moved, *refs):
    rows = kept.shape[0] // 4
    out = refs[-1]
    for k in range(8):
        number = plan[k]
        at = pl.multiple_of((number // 2 % 2 * 2 + number // 4) * rows, rows)
        even = kept[pl.ds(at, rows), :].astype(F32)
        odd = moved[pl.ds(at, rows), :].astype(F32)
        out[k * rows : (k + 1) * rows, :] = jnp.where(number % 2 == 0, even, odd).astype(BF)


def reorder_kernel(table, values, keep, out):
    for j in range(values.shape[1] // ROWS):
        at = pl.multiple_of(table[j] * ROWS, ROWS)
        part = values[:, pl.ds(at, ROWS)].astype(F32)
        out[:, j * ROWS : (j + 1) * ROWS] = jnp.where(keep[...] > 0, part, 0.0).astype(BF)


def dot_nt(left, right):
    return lax.dot_general(left, right, (((1,), (1,)), ((), ())), preferred_element_type=F32)


def dot_tn(left, right):
    return lax.dot_general(left, right, (((0,), (0,)), ((), ())), preferred_element_type=F32)


def head_norm(values):
    centred = values - jnp.mean(values, axis=-1, keepdims=True)
    scale = lax.rsqrt(jnp.mean(centred * centred, axis=-1, keepdims=True) + EPSILON)
    return centred * scale, scale


def block_mask(valid_keys, block_len):
    rows = valid_keys.shape[1]
    row_block = lax.broadcasted_iota(jnp.int32, (rows, rows), 0) // block_len
    col_block = lax.broadcasted_iota(jnp.int32, (rows, rows), 1) // block_len
    return (row_block == col_block) & (valid_keys > 0)


def softmax(queries, keys, mask, size):
    scores = dot_nt(queries, keys) / math.sqrt(size)
    scores = jnp.where(mask, scores, -1e30)
    expo = jnp.exp(scores - jnp.max(scores, axis=-1, keepdims=True))
    return expo / jnp.sum(expo, axis=-1, keepdims=True)


def project_kernel_over(bounds, carry):
    def kernel(*refs):
        sums = refs[0] if carry else None
        normed, weights, out = refs[carry], refs[carry + 1 : carry + 1 + len(bounds)], refs[-1]
        step = 3 * ROWS
        for at in range(0, out.shape[1], step):
            total = sums[:, at : at + step] if carry else jnp.zeros((out.shape[0], step), F32)
            for (a, b), weight in zip(bounds, weights):
                total += jnp.dot(
                    normed[:, a:b], weight[:, at : at + step], preferred_element_type=F32
                )
            out[:, at : at + step] = total

    return kernel


def make_attend_kernel(block_len, size):
    def kernel(projected, gains, valid_keys, attended):
        mask = block_mask(valid_keys[...], block_len)
        for head in range(projected.shape[1] // (3 * size)):
            at = head * 3 * size
            q_hat, _ = head_norm(projected[:, at : at + size])
            k_hat, _ = head_norm(projected[:, at + size : at + 2 * size])
            queries = (q_hat * gains[0:1, :]).astype(BF)
            keys = (k_hat * gains[1:2, :]).astype(BF)
            values = projected[:, at + 2 * size : at + 3 * size].astype(BF)
            attend = softmax(queries, keys, mask, size).astype(BF)
            attended[:, head * size : (head + 1) * size] = jnp.dot(
                attend, values, preferred_element_type=F32
            ).astype(BF)

    return kernel


def make_attend_back_kernel(block_len, size):
    def norm_back(grad, hat, scale, gain):
        inner = grad * gain
        middle = jnp.mean(inner, axis=-1, keepdims=True)
        slope = jnp.mean(inner * hat, axis=-1, keepdims=True)
        return scale * (inner - middle - hat * slope)

    def kernel(projected, gains, valid_keys, grad_attended, grad_projected, grad_gains):
        mask = block_mask(valid_keys[...], block_len)
        gain_q, gain_k = gains[0:1, :], gains[1:2, :]
        sum_q = jnp.zeros((1, size), F32)
        sum_k = jnp.zeros((1, size), F32)
        for head in range(projected.shape[1] // (3 * size)):
            at = head * 3 * size
            q_hat, q_scale = head_norm(projected[:, at : at + size])
            k_hat, k_scale = head_norm(projected[:, at + size : at + 2 * size])
            queries = (q_hat * gain_q).astype(BF)
            keys = (k_hat * gain_k).astype(BF)
            values = projected[:, at + 2 * size : at + 3 * size].astype(BF)
            soft = softmax(queries, keys, mask, size)
            grad_out = grad_attended[:, head * size : (head + 1) * size]
            grad_values = dot_tn(soft.astype(BF), grad_out).astype(BF)
            grad_attend = dot_nt(grad_out, values).astype(BF).astype(F32)
            inner = jnp.sum(grad_attend * soft, axis=-1, keepdims=True)
            grad_scores = soft * (grad_attend - inner) / math.sqrt(size)
            grad_scores = jnp.where(mask, grad_scores, 0.0).astype(BF)
            grad_q = jnp.dot(grad_scores, keys, preferred_element_type=F32).astype(BF).astype(F32)
            grad_k = dot_tn(grad_scores, queries).astype(BF).astype(F32)
            sum_q += jnp.sum(grad_q * q_hat, axis=0, keepdims=True)
            sum_k += jnp.sum(grad_k * k_hat, axis=0, keepdims=True)
            grad_projected[:, at : at + size] = norm_back(grad_q, q_hat, q_scale, gain_q).astype(BF)
            grad_projected[:, at + size : at + 2 * size] = norm_back(
                grad_k, k_hat, k_scale, gain_k
            ).astype(BF)
            grad_projected[:, at + 2 * size : at + 3 * size] = grad_values
        grad_gains[0:1, :] = sum_q
        grad_gains[1:2, :] = sum_k

    return kernel


def branch_kernel(table, attended, *refs):
    weights, branch = refs[:-2], refs[-1]
    per = branch.shape[2] // ROWS
    j = 0
    for weight in weights:
        step = 2 * ROWS
        for a in range(0, weight.shape[0], step):
            product = dot_nt(attended[...], weight[a : a + step, :]).astype(BF)
            for k in range(2):
                block = table[j + k]
                at = pl.multiple_of((block % per) * ROWS, ROWS)
                branch[block // per, :, pl.ds(at, ROWS)] = product[:, k * ROWS : (k + 1) * ROWS]
            j += 2


def out_back_kernel(cot, *refs):
    weights, out = refs[:-1], refs[-1]
    total = jnp.zeros(out.shape, F32)
    at = 0
    for weight in weights:
        rows = weight.shape[0]
        total += jnp.dot(cot[:, at : at + rows], weight[...], preferred_element_type=F32)
        at += rows
    out[...] = total.astype(BF)


def gain_kernel(table, grad_projected, normed, *refs):
    weights, out = refs[:-2], refs[-1]
    j = 0
    for weight in weights:
        blocks = weight.shape[0] // ROWS
        grad = dot_nt(grad_projected[...], weight[...]).astype(BF).astype(F32)
        here = normed[:, j * ROWS : (j + blocks) * ROWS].astype(F32)
        sums = jnp.sum(grad * here, axis=0, keepdims=True)
        for k in range(blocks):
            out[pl.ds(table[j + k], 1), :] = sums[:, k * ROWS : (k + 1) * ROWS]
        j += blocks


def call(kernel, shapes, tables, *arrays, flops=0, after=()):
    smem = pl.BlockSpec(memory_space=pltpu.SMEM)
    vmem = pl.BlockSpec(memory_space=pltpu.VMEM)
    several = isinstance(shapes, tuple)
    moved = sum(a.size * a.dtype.itemsize for a in arrays)
    return pl.pallas_call(
        kernel,
        out_shape=shapes,
        in_specs=[smem] * len(tables)
        + [vmem] * len(arrays)
        + [pl.BlockSpec(memory_space=pl.ANY)] * len(after),
        out_specs=(vmem,) * len(shapes) if several else vmem,
        compiler_params=pltpu.CompilerParams(vmem_limit_bytes=28 * 1024 * 1024),
        cost_estimate=pl.CostEstimate(flops=flops, bytes_accessed=moved, transcendentals=0),
    )(*tables, *arrays, *after)


def shape(dims, dtype):
    return jax.ShapeDtypeStruct(dims, dtype)


def per_device(
    packed,
    counts,
    dest_plan,
    source_plan,
    slot_counts,
    cotangent,
    qkv_weight,
    out_weight,
    ln_gain,
    qk_gains,
):
    image_total = counts.shape[1]
    half_images = image_total // 2
    far_gap = N_DP // 2 - half_images
    block_len, width = cotangent.shape[1], cotangent.shape[2]
    rows = image_total * block_len
    heads, size = out_weight.shape[1], out_weight.shape[2]
    share = width // N_SHARD
    me = lax.axis_index("shard")

    qkv_table = absolute_blocks(QKV_ORDER)
    out_table = absolute_blocks(OUT_ORDER)
    packed_share = lax.dynamic_slice_in_dim(packed, me * share, share, 1)
    image_counts = counts[0]
    offsets = jnp.cumsum(image_counts) - image_counts
    positions = jnp.arange(block_len, dtype=jnp.int32)
    offset_ids = jnp.arange(image_total, dtype=jnp.int32)
    chosen = dest_plan[0][None, :] == offset_ids[:, None]
    starts = jnp.sum(jnp.where(chosen, offsets[None, :], 0), axis=1)
    lengths = jnp.sum(jnp.where(chosen, image_counts[None, :], 0), axis=1)
    row_index = jnp.clip(starts[:, None] + positions[None, :], 0, packed.shape[0] - 1)
    keep_rows = (positions[None, :] < lengths[:, None])[..., None]
    outgoing = jnp.where(
        keep_rows, jnp.take(packed_share, row_index, axis=0), jnp.zeros((), BF)
    )
    outgoing = outgoing.reshape(rows, share)
    weight = qkv_weight.reshape(ROWS, heads * 3 * size)

    def pieces(chosen):
        return tuple(((i, k * block_len, (k + 1) * block_len),) for i, k in chosen)

    moved = dp_rotate(outgoing[rows // 2 :], half_images + far_gap)
    y_ahead, y_behind = y_step(weight, -1), y_step(weight, 1)
    out_start = copied(out_weight.reshape(ROWS, heads * size), (y_ahead, y_behind))
    out_ahead, out_behind = y_step(out_start, -1), y_step(out_start, 1)
    out_across = y_step(out_start, 2)
    z_weight = copied(weight, (moved, y_ahead, y_behind))
    z_ahead, z_behind = z_step(z_weight, -1), z_step(z_weight, 1)
    send, keep = combine(
        (
            pieces([(i, k) for i in (0, 1) for k in (2, 3)]),
            pieces([(i, k) for i in (0, 1) for k in (0, 1)]),
        ),
        outgoing,
        moved,
    )
    moved = dp_rotate(send, 2)
    send, keep = combine(
        (
            pieces([(i, k) for i in (0, 1) for k in (1, 3)]),
            pieces([(i, k) for i in (0, 1) for k in (0, 2)]),
        ),
        keep,
        moved,
    )
    moved = dp_rotate(send, 1)
    own_share = call(
        pick_kernel,
        shape((rows, share), BF),
        (source_plan[0],),
        keep,
        moved,
        after=(z_ahead, z_behind),
    )
    block_share = own_share.reshape(image_total, block_len, share)
    next_share = shard_shift(own_share, dl=1)

    first, up, near = gather_first(
        weight, z_ahead, z_behind, y_ahead, y_behind, (out_ahead, out_behind, out_across)
    )
    from_ahead, from_behind = y_step(up, -1), y_step(near, 1)
    other_first = swap(first)
    z_across = z_step(z_ahead, -1)

    (pair,) = combine(((((0, 0, rows),), ((1, 0, rows),)),), own_share, next_share)
    groups = [[x * NL + low for x in range(NX)] for low in range(NL)]
    tokens = lax.all_gather(pair, "shard", axis=0, tiled=True, axis_index_groups=groups)
    tokens = tokens.reshape(N_SHARD, rows, share)
    valid_rows = positions[None, :] < slot_counts[0][:, None]
    valid_keys = valid_rows.astype(F32).reshape(1, rows)
    valid_column = valid_rows.astype(F32).reshape(rows, 1)

    cot = call(
        reorder_kernel,
        shape((rows, width), BF),
        (out_table,),
        cotangent.reshape(rows, width),
        valid_column,
    )

    (column,) = combine(
        (tuple(((i, 0, ROWS),) for i in range(4)),),
        out_start,
        out_ahead,
        out_behind,
        out_across,
        after=(near,),
    )
    column_behind = z_step(column, 1)
    second, up, down = gather_second(
        from_ahead, from_behind, z_across, (other_first, cot, column_behind)
    )
    third, fourth = y_step(up, -1), y_step(down, 1)
    other_second = swap(second)
    (forward,) = combine(((((0, 0, ROWS),),),), fourth)
    fifth = y_step(forward, 1)
    out_first, out_up, out_down = gather_out(
        column, column_behind, (forward, third, other_second)
    )
    other_out_first = swap(out_first)

    per = share // ROWS
    places = ((qkv_table // per) ^ (me % NL)) * per + qkv_table % per
    normed = call(
        norm_kernel,
        shape((rows, width), BF),
        (places, qkv_table),
        tokens,
        ln_gain.reshape(1, width),
        after=(out_first,),
    )
    sizes = [len(part) * ROWS for part in QKV_PARTS]
    sizes += sizes[:2] + [sizes[2] + sizes[3], sizes[4]]
    bounds = np.cumsum([0] + sizes)
    bounds = list(zip(bounds[:-1].tolist(), bounds[1:].tolist()))
    early, late = (0, 1, 5, 6), (2, 3, 4, 7, 8)
    projected_shape = shape((rows, heads * 3 * size), F32)
    projected = call(
        project_kernel_over([bounds[i] for i in early], 0),
        projected_shape,
        (),
        normed,
        first,
        second,
        other_first,
        other_second,
        flops=2 * rows * width * heads * 2 * size,
    )
    (out_second,) = combine(
        ((((0, 0, 2 * ROWS),), ((1, 0, 2 * ROWS),)),), out_up, out_down, after=(projected,)
    )
    out_mine, out_other = (out_first, out_second), (other_out_first, swap(out_second))
    (pair,) = combine(
        ((((0, 0, 2 * ROWS),), ((1, 0, 2 * ROWS),)),), third, fourth, after=(out_first,)
    )
    other_pair = swap(pair)
    other_fifth = swap(copied(fifth, (projected,)))
    parts = [first, second, third, fourth, fifth]
    parts += [other_first, other_second, other_pair, other_fifth]
    projected = call(
        project_kernel_over([bounds[i] for i in late], 1),
        projected_shape,
        (),
        projected,
        normed,
        *[parts[i] for i in late],
        after=(out_second,),
        flops=2 * rows * width * heads * size,
    )
    attended = call(
        make_attend_kernel(block_len, size),
        shape((rows, heads * size), BF),
        (),
        projected,
        qk_gains,
        valid_keys,
    )

    half = width // 2
    out_parts = (*out_mine, *out_other)
    out_theirs = swap(part_product(cot, attended, half, half, out_other))
    grad_attended = call(
        out_back_kernel,
        shape((rows, heads * size), BF),
        (),
        cot,
        *out_parts,
        flops=2 * rows * width * heads * size,
    )
    grad_projected, grad_gains = call(
        make_attend_back_kernel(block_len, size),
        (shape((rows, heads * 3 * size), BF), shape((2, size), F32)),
        (),
        projected,
        qk_gains,
        valid_keys,
        grad_attended,
    )
    out_sums, out_plus, *out_moved = scatter_out(cot, attended, out_theirs, (grad_projected,))
    late_product = part_product(normed, grad_projected, half + EARLY, half - EARLY, (out_sums,))
    branch = call(
        branch_kernel,
        shape((N_SHARD, rows, share), BF),
        (out_table,),
        attended,
        *out_parts,
        after=(out_plus,),
        flops=2 * rows * width * heads * size,
    )
    summed = lax.psum_scatter(branch, "shard", scatter_dimension=0, tiled=False)
    summed = summed.reshape(image_total, block_len, share).astype(F32)
    block_out = jnp.where(valid_rows[..., None], block_share.astype(F32) + summed, 0.0).astype(BF)

    def gain_sums(midway):
        grad_gain = call(
            gain_kernel,
            shape((N_DP, ROWS), F32),
            (qkv_table,),
            grad_projected,
            normed,
            *parts,
            after=(midway,),
            flops=2 * rows * width * heads * 3 * size,
        )
        grad_gain = grad_gain / ln_gain.reshape(N_DP, ROWS)
        own_gains = jnp.concatenate([grad_gain, grad_gains], axis=0)
        return own_gains, sum_over(sum_over(own_gains, dp_exchange, (1,)), shard_exchange, (2, 4))

    final_q, totals, third_round = scatter_qkv(
        normed, grad_projected, late_product, (out_plus,), out_moved, gain_sums
    )
    final_o = scatter_out_last(out_sums, *out_moved, third_round)
    return (
        block_out,
        final_q.reshape(ROWS, heads, 3 * size),
        final_o.reshape(ROWS, heads, size),
        totals[:N_DP].reshape(width),
        totals[N_DP:],
    )


def solution(mesh):
    return jax.shard_map(
        per_device,
        mesh=mesh,
        in_specs=(
            P("dp", None),
            P("dp", None),
            P("dp", None),
            P("dp", None),
            P("dp", None),
            P("dp", None, None),
            P("dp", "shard", None),
            P("dp", "shard", None),
            P(),
            P(),
        ),
        out_specs=(
            P("dp", None, "shard"),
            P("dp", "shard", None),
            P("dp", "shard", None),
            P(),
            P(),
        ),
        check_vma=False,
    )
```

```python
import math

import jax
import jax.numpy as jnp
import numpy as np
from jax import lax
from jax.experimental import pallas as pl
from jax.experimental.pallas import tpu as pltpu
from jax.sharding import PartitionSpec as P

EPSILON = 1e-06
BF = jnp.bfloat16
F32 = jnp.float32

NZ, NY, NC = 4, 4, 2
NX, NL = 4, 2
N_DP = NZ * NY * NC
N_SHARD = NX * NL
ROWS = 128

QKV_PARTS = (
    ((0, 0), (0, 1), (0, 3), (1, 0), (3, 0)),
    ((1, 1), (1, 3), (2, 0), (3, 1), (3, 3), (0, 2)),
    ((1, 2), (2, 1)),
    ((3, 2), (2, 3)),
    ((2, 2),),
)
QKV_ORDER = [(c, y, z) for c in range(NC) for part in QKV_PARTS for y, z in part]
EARLY = 10 * ROWS
OUT_ORDER = [(c, y, z) for c in range(NC) for z in (0, 1, 3, 2) for y in (0, 1, 3, 2)]


def dp_shift(value, dz=0, dy=0, dc=0):
    pairs = []
    for z in range(NZ):
        for y in range(NY):
            for c in range(NC):
                target = ((z + dz) % NZ) * NY * NC + ((y + dy) % NY) * NC + (c + dc) % NC
                pairs.append((z * NY * NC + y * NC + c, target))
    return lax.ppermute(value, "dp", pairs)


def dp_rotate(value, steps):
    return lax.ppermute(value, "dp", [(s, (s + steps) % N_DP) for s in range(N_DP)])


def shard_shift(value, dx=0, dl=0):
    pairs = []
    for x in range(NX):
        for low in range(NL):
            pairs.append((x * NL + low, ((x + dx) % NX) * NL + (low + dl) % NL))
    return lax.ppermute(value, "shard", pairs)


def absolute_blocks(order):
    me = lax.axis_index("dp")
    z, y, c = me // (NY * NC), (me // NC) % NY, me % NC
    table = np.asarray(order, dtype=np.int32)
    return (
        ((z + table[:, 2]) % NZ) * (NY * NC) + ((y + table[:, 1]) % NY) * NC + (c + table[:, 0]) % NC
    ).astype(jnp.int32)


def y_step(value, steps):
    return dp_shift(value, dy=steps)


def z_step(value, steps):
    return dp_shift(value, dz=steps)


def swap(value):
    return dp_shift(value, dc=1)


def combine(plans, *arrays, after=(), dtype=BF):
    count = len(arrays)
    width = arrays[0].shape[1]

    def kernel(*refs):
        for plan, out in zip(plans, refs[count + len(after) :]):
            at = 0
            for terms in plan:
                rows = terms[0][2] - terms[0][1]
                parts = [refs[i][a:b, :] for i, a, b in terms]
                if len(parts) > 1:
                    parts = [part.astype(F32) for part in parts]
                total = parts[0]
                for part in parts[1:]:
                    total = total + part
                out[at : at + rows, :] = total.astype(dtype)
                at += rows

    sizes = [sum(terms[0][2] - terms[0][1] for terms in plan) for plan in plans]
    return call(kernel, tuple(shape((size, width), dtype) for size in sizes), (), *arrays, after=after)


def copied(value, after):
    (value,) = combine(((((0, 0, value.shape[0]),),),), value, after=after, dtype=value.dtype)
    return value


def gather_first(weight, z_ahead, z_behind, y_ahead, y_behind, after):
    one = ROWS
    return combine(
        (
            tuple(((i, 0, one),) for i in range(5)),
            (((1, 0, one),), ((2, 0, one),), ((3, 0, one),)),
            (((1, 0, one),), ((2, 0, one),)),
        ),
        weight,
        z_ahead,
        z_behind,
        y_ahead,
        y_behind,
        after=after,
    )


def gather_second(from_ahead, from_behind, z_across, after):
    one = ROWS
    return combine(
        (
            (((0, 0, 3 * one),), ((1, 0, 2 * one),), ((2, 0, one),)),
            (((2, 0, one),), ((0, 0, one),)),
            (((2, 0, one),), ((1, one, 2 * one),)),
        ),
        from_ahead,
        from_behind,
        z_across,
        after=after,
    )


def gather_out(column, z_behind, after_z):
    one = ROWS
    z_ahead = z_step(column, -1)
    first, up, down = combine(
        (
            (((0, 0, 4 * one),), ((1, 0, 4 * one),), ((2, 0, 4 * one),)),
            (((1, 0, 2 * one),),),
            (((2, 2 * one, 4 * one),),),
        ),
        column,
        z_ahead,
        z_behind,
        after=after_z,
    )
    return first, z_step(up, -1), z_step(down, 1)


def core_sums(left, right, base, received, bounds, after=()):
    def kernel(left_ref, right_ref, received_ref, *refs):
        outs = refs[len(after) :]
        for (a, b), out in zip(bounds, outs):
            product = dot_tn(left_ref[:, base + a : base + b], right_ref[...])
            out[...] = (product + received_ref[a:b, :].astype(F32)).astype(BF)

    shapes = tuple(shape((b - a, right.shape[1]), BF) for a, b in bounds)
    return call(kernel, shapes, (), left, right, received, after=after)


def part_product(left, right, base, rows, after=()):
    def kernel(*refs):
        left_ref, right_ref, out = refs[0], refs[1], refs[-1]
        step = 2 * ROWS
        for a in range(0, rows, step):
            out[a : a + step, :] = dot_tn(
                left_ref[:, base + a : base + a + step], right_ref[...]
            ).astype(BF)

    return call(kernel, shape((rows, right.shape[1]), BF), (), left, right, after=after)


def scatter_qkv(normed, grad, after_first, after_sums, meanwhile):
    one = ROWS
    half = normed.shape[1] // 2
    late = half - EARLY
    product = part_product(normed, grad, half + EARLY, late, after_first)
    late_other = swap(product)
    product = part_product(normed, grad, half, EARLY, (product,))
    early_other = swap(product)
    own_gains, gains = meanwhile(product)
    rows = lambda *at: [(a * one, b * one) for a, b in at]
    s02, s12_21, s32_23, s22 = core_sums(
        normed, grad, EARLY, late_other, rows((0, 1), (1, 3), (3, 5), (5, 6)), (own_gains,)
    )
    hop = y_step(s22, 1)
    s00, s01_03, s10, s30, s11_13, s20, s31_33 = core_sums(
        normed,
        grad,
        0,
        early_other,
        rows((0, 1), (1, 3), (3, 4), (4, 5), (5, 7), (7, 8), (8, 10)),
    )
    (plus,) = combine(
        ((((0, 0, one), (1, 0, one)), ((0, one, 2 * one),)),), s12_21, hop, after=(gains, *after_sums)
    )
    gains = sum_over(copied(gains, (plus,)), shard_exchange, (1,))
    gains = sum_over(gains, dp_exchange, (8, 16))
    below, above = y_step(plus, 1), y_step(s32_23, -1)
    plus, minus, z_across = combine(
        (
            (((0, 0, one), (3, one, 2 * one)), ((0, one, 2 * one),)),
            (
                ((1, 0, one),),
                ((1, one, 2 * one), (4, one, 2 * one)),
                ((2, 0, one),),
            ),
            (((5, 0, one), (3, 0, one), (4, 0, one)),),
        ),
        s11_13,
        s31_33,
        s20,
        below,
        above,
        s02,
        after=(gains,),
    )
    z_hop = z_step(z_across, 1)
    gains = sum_over(copied(gains, (z_hop,)), dp_exchange, (2, 4))
    below, above = y_step(plus, 1), y_step(minus, -1)
    last_below = y_step(s10, 1)
    minus, z_ahead, z_behind = combine(
        (
            (((0, 0, one), (1, 2 * one, 3 * one)),),
            (((2, 0, one), (3, 0, one), (1, 0, one), (4, 0, one)),),
            (((2, one, 2 * one), (3, one, 2 * one), (1, one, 2 * one)),),
        ),
        s30,
        above,
        s01_03,
        below,
        z_hop,
        after=(gains,),
    )
    last_above = y_step(minus, -1)
    from_below, from_above = z_step(z_ahead, 1), z_step(z_behind, -1)
    total = sum(
        part.astype(F32) for part in (s00, last_below, last_above, from_below, from_above)
    )
    return total, gains, (z_hop,)


def scatter_out(cot, attended, after):
    one = ROWS
    half = cot.shape[1] // 2
    product = part_product(cot, attended, half, half, after)
    other = swap(product)
    own, ahead, behind, across_up, across_down = core_sums(
        cot,
        attended,
        0,
        other,
        [(a * one, b * one) for a, b in ((0, 4), (4, 8), (8, 12), (12, 14), (14, 16))],
    )
    up, down = z_step(across_up, 1), z_step(across_down, -1)
    plus, minus = combine(
        (
            (((0, 0, 2 * one), (2, 0, 2 * one)), ((0, 2 * one, 4 * one),)),
            (((1, 0, 2 * one),), ((1, 2 * one, 4 * one), (3, 0, 2 * one))),
        ),
        ahead,
        behind,
        up,
        down,
    )
    below, above = z_step(plus, 1), z_step(minus, -1)
    return own, plus, below, above


def scatter_out_last(own, below, above, after):
    one = ROWS
    parts = combine(
        tuple(
            (tuple((i, k * one, (k + 1) * one) for i in range(3)),) for k in range(4)
        ),
        own,
        below,
        above,
        after=after,
    )
    hops = (y_step(parts[1], 1), y_step(parts[2], -1), y_step(parts[3], 2))
    return sum(hop.astype(F32) for hop in (parts[0], *hops))


def dp_exchange(value, bit):
    return lax.ppermute(value, "dp", [(s, s ^ bit) for s in range(N_DP)])


def shard_exchange(value, bit):
    return lax.ppermute(value, "shard", [(s, s ^ bit) for s in range(N_SHARD)])


def sum_over(value, exchange, bits):
    for bit in bits:
        value = value + exchange(value, bit)
    return value


def norm_kernel(places, table, tokens, gain, after, out):
    width = tokens.shape[0] * tokens.shape[2]
    per = tokens.shape[2] // ROWS
    rows = tokens.shape[1]
    total = jnp.zeros((rows, ROWS), F32)
    for j in range(width // ROWS):
        total += tokens[j // per, :, (j % per) * ROWS : (j % per + 1) * ROWS].astype(F32)
    mean = jnp.sum(total, axis=-1, keepdims=True) / width
    square = jnp.zeros((rows, ROWS), F32)
    for j in range(width // ROWS):
        part = tokens[j // per, :, (j % per) * ROWS : (j % per + 1) * ROWS].astype(F32) - mean
        square += part * part
    scale = lax.rsqrt(jnp.sum(square, axis=-1, keepdims=True) / width + EPSILON)
    for j in range(width // ROWS):
        place = places[j]
        at = pl.multiple_of((place % per) * ROWS, ROWS)
        part = tokens[place // per, :, pl.ds(at, ROWS)].astype(F32) - mean
        full_at = pl.multiple_of(table[j] * ROWS, ROWS)
        out[:, j * ROWS : (j + 1) * ROWS] = (part * scale * gain[:, pl.ds(full_at, ROWS)]).astype(BF)


def pick_kernel(plan, kept, moved, *refs):
    rows = kept.shape[0] // 4
    out = refs[-1]
    for k in range(8):
        number = plan[k]
        at = pl.multiple_of((number // 2 % 2 * 2 + number // 4) * rows, rows)
        even = kept[pl.ds(at, rows), :].astype(F32)
        odd = moved[pl.ds(at, rows), :].astype(F32)
        out[k * rows : (k + 1) * rows, :] = jnp.where(number % 2 == 0, even, odd).astype(BF)


def reorder_kernel(table, values, keep, out):
    for j in range(values.shape[1] // ROWS):
        at = pl.multiple_of(table[j] * ROWS, ROWS)
        part = values[:, pl.ds(at, ROWS)].astype(F32)
        out[:, j * ROWS : (j + 1) * ROWS] = jnp.where(keep[...] > 0, part, 0.0).astype(BF)


def dot_nt(left, right):
    return lax.dot_general(left, right, (((1,), (1,)), ((), ())), preferred_element_type=F32)


def dot_tn(left, right):
    return lax.dot_general(left, right, (((0,), (0,)), ((), ())), preferred_element_type=F32)


def head_norm(values):
    centred = values - jnp.mean(values, axis=-1, keepdims=True)
    scale = lax.rsqrt(jnp.mean(centred * centred, axis=-1, keepdims=True) + EPSILON)
    return centred * scale, scale


def block_mask(valid_keys, block_len):
    rows = valid_keys.shape[1]
    row_block = lax.broadcasted_iota(jnp.int32, (rows, rows), 0) // block_len
    col_block = lax.broadcasted_iota(jnp.int32, (rows, rows), 1) // block_len
    return (row_block == col_block) & (valid_keys > 0)


def softmax(queries, keys, mask, size):
    scores = dot_nt(queries, keys) / math.sqrt(size)
    scores = jnp.where(mask, scores, -1e30)
    expo = jnp.exp(scores - jnp.max(scores, axis=-1, keepdims=True))
    return expo / jnp.sum(expo, axis=-1, keepdims=True)


def project_kernel_over(bounds, carry):
    def kernel(*refs):
        sums = refs[0] if carry else None
        normed, weights, out = refs[carry], refs[carry + 1 : carry + 1 + len(bounds)], refs[-1]
        step = 3 * ROWS
        for at in range(0, out.shape[1], step):
            total = sums[:, at : at + step] if carry else jnp.zeros((out.shape[0], step), F32)
            for (a, b), weight in zip(bounds, weights):
                total += jnp.dot(
                    normed[:, a:b], weight[:, at : at + step], preferred_element_type=F32
                )
            out[:, at : at + step] = total

    return kernel


def make_attend_kernel(block_len, size):
    def kernel(projected, gains, valid_keys, attended):
        mask = block_mask(valid_keys[...], block_len)
        for head in range(projected.shape[1] // (3 * size)):
            at = head * 3 * size
            q_hat, _ = head_norm(projected[:, at : at + size])
            k_hat, _ = head_norm(projected[:, at + size : at + 2 * size])
            queries = (q_hat * gains[0:1, :]).astype(BF)
            keys = (k_hat * gains[1:2, :]).astype(BF)
            values = projected[:, at + 2 * size : at + 3 * size].astype(BF)
            attend = softmax(queries, keys, mask, size).astype(BF)
            attended[:, head * size : (head + 1) * size] = jnp.dot(
                attend, values, preferred_element_type=F32
            ).astype(BF)

    return kernel


def make_attend_back_kernel(block_len, size):
    def norm_back(grad, hat, scale, gain):
        inner = grad * gain
        middle = jnp.mean(inner, axis=-1, keepdims=True)
        slope = jnp.mean(inner * hat, axis=-1, keepdims=True)
        return scale * (inner - middle - hat * slope)

    def kernel(projected, gains, valid_keys, grad_attended, grad_projected, grad_gains):
        mask = block_mask(valid_keys[...], block_len)
        gain_q, gain_k = gains[0:1, :], gains[1:2, :]
        sum_q = jnp.zeros((1, size), F32)
        sum_k = jnp.zeros((1, size), F32)
        for head in range(projected.shape[1] // (3 * size)):
            at = head * 3 * size
            q_hat, q_scale = head_norm(projected[:, at : at + size])
            k_hat, k_scale = head_norm(projected[:, at + size : at + 2 * size])
            queries = (q_hat * gain_q).astype(BF)
            keys = (k_hat * gain_k).astype(BF)
            values = projected[:, at + 2 * size : at + 3 * size].astype(BF)
            soft = softmax(queries, keys, mask, size)
            grad_out = grad_attended[:, head * size : (head + 1) * size]
            grad_values = dot_tn(soft.astype(BF), grad_out).astype(BF)
            grad_attend = dot_nt(grad_out, values).astype(BF).astype(F32)
            inner = jnp.sum(grad_attend * soft, axis=-1, keepdims=True)
            grad_scores = soft * (grad_attend - inner) / math.sqrt(size)
            grad_scores = jnp.where(mask, grad_scores, 0.0).astype(BF)
            grad_q = jnp.dot(grad_scores, keys, preferred_element_type=F32).astype(BF).astype(F32)
            grad_k = dot_tn(grad_scores, queries).astype(BF).astype(F32)
            sum_q += jnp.sum(grad_q * q_hat, axis=0, keepdims=True)
            sum_k += jnp.sum(grad_k * k_hat, axis=0, keepdims=True)
            grad_projected[:, at : at + size] = norm_back(grad_q, q_hat, q_scale, gain_q).astype(BF)
            grad_projected[:, at + size : at + 2 * size] = norm_back(
                grad_k, k_hat, k_scale, gain_k
            ).astype(BF)
            grad_projected[:, at + 2 * size : at + 3 * size] = grad_values
        grad_gains[0:1, :] = sum_q
        grad_gains[1:2, :] = sum_k

    return kernel


def branch_kernel(table, attended, *refs):
    weights, branch = refs[:-2], refs[-1]
    per = branch.shape[2] // ROWS
    j = 0
    for weight in weights:
        step = 2 * ROWS
        for a in range(0, weight.shape[0], step):
            product = dot_nt(attended[...], weight[a : a + step, :]).astype(BF)
            for k in range(2):
                block = table[j + k]
                at = pl.multiple_of((block % per) * ROWS, ROWS)
                branch[block // per, :, pl.ds(at, ROWS)] = product[:, k * ROWS : (k + 1) * ROWS]
            j += 2


def out_back_kernel(cot, *refs):
    weights, out = refs[:-1], refs[-1]
    total = jnp.zeros(out.shape, F32)
    at = 0
    for weight in weights:
        rows = weight.shape[0]
        total += jnp.dot(cot[:, at : at + rows], weight[...], preferred_element_type=F32)
        at += rows
    out[...] = total.astype(BF)


def gain_kernel(table, grad_projected, normed, *refs):
    weights, out = refs[:-2], refs[-1]
    j = 0
    for weight in weights:
        blocks = weight.shape[0] // ROWS
        grad = dot_nt(grad_projected[...], weight[...]).astype(BF).astype(F32)
        here = normed[:, j * ROWS : (j + blocks) * ROWS].astype(F32)
        sums = jnp.sum(grad * here, axis=0, keepdims=True)
        for k in range(blocks):
            out[pl.ds(table[j + k], 1), :] = sums[:, k * ROWS : (k + 1) * ROWS]
        j += blocks


def call(kernel, shapes, tables, *arrays, flops=0, after=()):
    smem = pl.BlockSpec(memory_space=pltpu.SMEM)
    vmem = pl.BlockSpec(memory_space=pltpu.VMEM)
    several = isinstance(shapes, tuple)
    moved = sum(a.size * a.dtype.itemsize for a in arrays)
    return pl.pallas_call(
        kernel,
        out_shape=shapes,
        in_specs=[smem] * len(tables)
        + [vmem] * len(arrays)
        + [pl.BlockSpec(memory_space=pl.ANY)] * len(after),
        out_specs=(vmem,) * len(shapes) if several else vmem,
        compiler_params=pltpu.CompilerParams(vmem_limit_bytes=28 * 1024 * 1024),
        cost_estimate=pl.CostEstimate(flops=flops, bytes_accessed=moved, transcendentals=0),
    )(*tables, *arrays, *after)


def shape(dims, dtype):
    return jax.ShapeDtypeStruct(dims, dtype)


def per_device(
    packed,
    counts,
    dest_plan,
    source_plan,
    slot_counts,
    cotangent,
    qkv_weight,
    out_weight,
    ln_gain,
    qk_gains,
):
    image_total = counts.shape[1]
    half_images = image_total // 2
    far_gap = N_DP // 2 - half_images
    block_len, width = cotangent.shape[1], cotangent.shape[2]
    rows = image_total * block_len
    heads, size = out_weight.shape[1], out_weight.shape[2]
    share = width // N_SHARD
    me = lax.axis_index("shard")

    qkv_table = absolute_blocks(QKV_ORDER)
    out_table = absolute_blocks(OUT_ORDER)
    packed_share = lax.dynamic_slice_in_dim(packed, me * share, share, 1)
    image_counts = counts[0]
    offsets = jnp.cumsum(image_counts) - image_counts
    positions = jnp.arange(block_len, dtype=jnp.int32)
    offset_ids = jnp.arange(image_total, dtype=jnp.int32)
    chosen = dest_plan[0][None, :] == offset_ids[:, None]
    starts = jnp.sum(jnp.where(chosen, offsets[None, :], 0), axis=1)
    lengths = jnp.sum(jnp.where(chosen, image_counts[None, :], 0), axis=1)
    row_index = jnp.clip(starts[:, None] + positions[None, :], 0, packed.shape[0] - 1)
    keep_rows = (positions[None, :] < lengths[:, None])[..., None]
    outgoing = jnp.where(
        keep_rows, jnp.take(packed_share, row_index, axis=0), jnp.zeros((), BF)
    )
    outgoing = outgoing.reshape(rows, share)
    weight = qkv_weight.reshape(ROWS, heads * 3 * size)

    def pieces(chosen):
        return tuple(((i, k * block_len, (k + 1) * block_len),) for i, k in chosen)

    moved = dp_rotate(outgoing[rows // 2 :], half_images + far_gap)
    y_ahead, y_behind = y_step(weight, -1), y_step(weight, 1)
    out_start = copied(out_weight.reshape(ROWS, heads * size), (y_ahead, y_behind))
    out_ahead, out_behind = y_step(out_start, -1), y_step(out_start, 1)
    out_across = y_step(out_start, 2)
    z_weight = copied(weight, (moved, y_ahead, y_behind))
    z_ahead, z_behind = z_step(z_weight, -1), z_step(z_weight, 1)
    send, keep = combine(
        (
            pieces([(i, k) for i in (0, 1) for k in (2, 3)]),
            pieces([(i, k) for i in (0, 1) for k in (0, 1)]),
        ),
        outgoing,
        moved,
    )
    moved = dp_rotate(send, 2)
    send, keep = combine(
        (
            pieces([(i, k) for i in (0, 1) for k in (1, 3)]),
            pieces([(i, k) for i in (0, 1) for k in (0, 2)]),
        ),
        keep,
        moved,
    )
    moved = dp_rotate(send, 1)
    own_share = call(
        pick_kernel,
        shape((rows, share), BF),
        (source_plan[0],),
        keep,
        moved,
        after=(z_ahead, z_behind, out_ahead, out_behind, out_across),
    )
    block_share = own_share.reshape(image_total, block_len, share)
    next_share = shard_shift(own_share, dl=1)

    first, up, near = gather_first(
        weight, z_ahead, z_behind, y_ahead, y_behind, ()
    )
    from_ahead, from_behind = y_step(up, -1), y_step(near, 1)
    other_first = swap(first)
    z_across = z_step(z_ahead, -1)

    (pair,) = combine(((((0, 0, rows),), ((1, 0, rows),)),), own_share, next_share)
    groups = [[x * NL + low for x in range(NX)] for low in range(NL)]
    tokens = lax.all_gather(pair, "shard", axis=0, tiled=True, axis_index_groups=groups)
    tokens = tokens.reshape(N_SHARD, rows, share)
    valid_rows = positions[None, :] < slot_counts[0][:, None]
    valid_keys = valid_rows.astype(F32).reshape(1, rows)
    valid_column = valid_rows.astype(F32).reshape(rows, 1)

    cot = call(
        reorder_kernel,
        shape((rows, width), BF),
        (out_table,),
        cotangent.reshape(rows, width),
        valid_column,
    )

    (column,) = combine(
        (tuple(((i, 0, ROWS),) for i in range(4)),),
        out_start,
        out_ahead,
        out_behind,
        out_across,
        after=(near,),
    )
    column_behind = z_step(column, 1)
    second, up, down = gather_second(
        from_ahead, from_behind, z_across, (other_first, cot, column_behind)
    )
    third, fourth = y_step(up, -1), y_step(down, 1)
    other_second = swap(second)
    (forward,) = combine(((((0, 0, ROWS),),),), fourth)
    fifth = y_step(forward, 1)
    out_first, out_up, out_down = gather_out(
        column, column_behind, (forward, third, other_second)
    )
    other_out_first = swap(out_first)

    per = share // ROWS
    places = ((qkv_table // per) ^ (me % NL)) * per + qkv_table % per
    normed = call(
        norm_kernel,
        shape((rows, width), BF),
        (places, qkv_table),
        tokens,
        ln_gain.reshape(1, width),
        after=(out_first,),
    )
    sizes = [len(part) * ROWS for part in QKV_PARTS]
    sizes += sizes[:2] + [sizes[2] + sizes[3], sizes[4]]
    bounds = np.cumsum([0] + sizes)
    bounds = list(zip(bounds[:-1].tolist(), bounds[1:].tolist()))
    early, late = (0, 1, 5, 6), (2, 3, 4, 7, 8)
    projected_shape = shape((rows, heads * 3 * size), F32)
    projected = call(
        project_kernel_over([bounds[i] for i in early], 0),
        projected_shape,
        (),
        normed,
        first,
        second,
        other_first,
        other_second,
        flops=2 * rows * width * heads * 2 * size,
    )
    (out_second,) = combine(
        ((((0, 0, 2 * ROWS),), ((1, 0, 2 * ROWS),)),), out_up, out_down, after=(projected,)
    )
    out_mine, out_other = (out_first, out_second), (other_out_first, swap(out_second))
    (pair,) = combine(
        ((((0, 0, 2 * ROWS),), ((1, 0, 2 * ROWS),)),), third, fourth, after=(out_first,)
    )
    other_pair = swap(pair)
    other_fifth = swap(copied(fifth, (projected,)))
    parts = [first, second, third, fourth, fifth]
    parts += [other_first, other_second, other_pair, other_fifth]
    projected = call(
        project_kernel_over([bounds[i] for i in late], 1),
        projected_shape,
        (),
        projected,
        normed,
        *[parts[i] for i in late],
        after=(out_second,),
        flops=2 * rows * width * heads * size,
    )
    attended = call(
        make_attend_kernel(block_len, size),
        shape((rows, heads * size), BF),
        (),
        projected,
        qk_gains,
        valid_keys,
    )

    out_sums, out_plus, *out_moved = scatter_out(cot, attended, out_other)

    out_parts = (*out_mine, *out_other)
    branch = call(
        branch_kernel,
        shape((N_SHARD, rows, share), BF),
        (out_table,),
        attended,
        *out_parts,
        after=(out_sums,),
        flops=2 * rows * width * heads * size,
    )
    summed = lax.psum_scatter(branch, "shard", scatter_dimension=0, tiled=False)
    summed = summed.reshape(image_total, block_len, share).astype(F32)
    block_out = jnp.where(valid_rows[..., None], block_share.astype(F32) + summed, 0.0).astype(BF)

    grad_attended = call(
        out_back_kernel,
        shape((rows, heads * size), BF),
        (),
        cot,
        *out_parts,
        flops=2 * rows * width * heads * size,
    )
    grad_projected, grad_gains = call(
        make_attend_back_kernel(block_len, size),
        (shape((rows, heads * 3 * size), BF), shape((2, size), F32)),
        (),
        projected,
        qk_gains,
        valid_keys,
        grad_attended,
    )

    def gain_sums(midway):
        grad_gain = call(
            gain_kernel,
            shape((N_DP, ROWS), F32),
            (qkv_table,),
            grad_projected,
            normed,
            *parts,
            after=(midway,),
            flops=2 * rows * width * heads * 3 * size,
        )
        grad_gain = grad_gain / ln_gain.reshape(N_DP, ROWS)
        own_gains = jnp.concatenate([grad_gain, grad_gains], axis=0)
        return own_gains, sum_over(sum_over(own_gains, dp_exchange, (1,)), shard_exchange, (2, 4))

    final_q, totals, third_round = scatter_qkv(
        normed, grad_projected, (branch, out_plus), out_moved, gain_sums
    )
    final_o = scatter_out_last(out_sums, *out_moved, third_round)
    return (
        block_out,
        final_q.reshape(ROWS, heads, 3 * size),
        final_o.reshape(ROWS, heads, size),
        totals[:N_DP].reshape(width),
        totals[N_DP:],
    )


def solution(mesh):
    return jax.shard_map(
        per_device,
        mesh=mesh,
        in_specs=(
            P("dp", None),
            P("dp", None),
            P("dp", None),
            P("dp", None),
            P("dp", None),
            P("dp", None, None),
            P("dp", "shard", None),
            P("dp", "shard", None),
            P(),
            P(),
        ),
        out_specs=(
            P("dp", None, "shard"),
            P("dp", "shard", None),
            P("dp", "shard", None),
            P(),
            P(),
        ),
        check_vma=False,
    )
```
